32 devices in a mesh: batch: 8 (over y, x, core), rows: 4 (over z).
Axes of the slice: x: 2, y: 2, z: 4, core: 2. Of those that a mesh axis runs over, the one named last changes fastest.
Arguments:
- patches: bfloat16 [16, 32, 32, 384], P('batch', 'rows'), may hold values from -6 to 6
- cotangent: bfloat16 [16, 32, 32, 384], P('batch', 'rows'), may hold values from -6 to 6
- heights: int32 [16], P('batch'), may hold values from 8 to 32, as said below
- widths: int32 [16], P('batch'), may hold values from 8 to 32, as said below
- qkv_weight: float32 [384, 1152], P(None, 'rows'), may hold values from -0.4375 to 0.4375
- qkv_moment: float32 [384, 1152], P(None, 'rows'), may hold values from -512 to 512
- proj_weight: float32 [384, 384], P(None, 'rows'), may hold values from -0.625 to 0.625
- proj_moment: float32 [384, 384], P(None, 'rows'), may hold values from -512 to 512
- expand_weight: float32 [384, 1536], P(None, 'rows'), may hold values from -0.3125 to 0.3125
- expand_moment: float32 [384, 1536], P(None, 'rows'), may hold values from -512 to 512
- shrink_weight: float32 [1536, 384], P('rows'), may hold values from -0.15625 to 0.15625
- shrink_moment: float32 [1536, 384], P('rows'), may hold values from -512 to 512
- norm_gains: float32 [2, 384], replicated, may hold values from 0.5 to 1.5
- gains_moment: float32 [2, 384], P(None, 'rows'), may hold values from -512 to 512
- all_biases: float32 [4224], replicated, may hold values from -1 to 1
- biases_moment: float32 [4224], P('rows'), may hold values from -512 to 512
- frequencies: float32 [2, 192], replicated, may hold values from -0.5 to 0.5
- freq_moment: float32 [2, 192], P(None, 'rows'), may hold values from -4096 to 4096
Outputs:
- block_out: bfloat16 [16, 32, 32, 384], P('batch', 'rows')
- patch_grad: float32 [16, 32, 32, 384], P('batch', 'rows')
- qkv_moment_new: float32 [384, 1152], P(None, 'rows')
- qkv_weight_new: float32 [384, 1152], P(None, 'rows')
- proj_moment_new: float32 [384, 384], P(None, 'rows')
- proj_weight_new: float32 [384, 384], P(None, 'rows')
- expand_moment_new: float32 [384, 1536], P(None, 'rows')
- expand_weight_new: float32 [384, 1536], P(None, 'rows')
- shrink_moment_new: float32 [1536, 384], P('rows')
- shrink_weight_new: float32 [1536, 384], P('rows')
- gains_moment_new: float32 [2, 384], P(None, 'rows')
- norm_gains_new: float32 [2, 384], P(None, 'rows')
- biases_moment_new: float32 [4224], P('rows')
- all_biases_new: float32 [4224], P('rows')
- freq_moment_new: float32 [2, 192], P(None, 'rows')
- frequencies_new: float32 [2, 192], P(None, 'rows')
The draws below stay inside these ranges and needn't reach their ends.
Inputs may be any that keep to these rules, and one draw needn't show every extreme that they name: `heights`: in each block of 2 images that one device index of batch holds, one image, drawn from the seed, has 32 rows and 32 columns. `widths`: in each block of 2 images that one device index of batch holds, one image, drawn from the seed, has 32 rows and 32 columns.
All inputs are finite; a program needn't handle non-finite values.
Results may differ from the reference program's by a relative error of at most 0.01.
The reference program's roundings to bfloat16 on the way count: a program that leaves them out, or rounds other values in their place, can miss the bound.
Values may be sent and summed in bfloat16 or wider, within the bound.
No kernel may reach another device: no remote copies, remote signals or barrier semaphores. Data moves between devices by JAX's collectives and lax.ppermute only.
A program may use at most 448 MiB of HBM per device.

```python
import math
import jax
import jax.numpy as jnp
from jax import lax

D = 384
H = 6
HD = 64
FF = 1536
GW = 32
IMG_DEV = 2
GH = 32
IMAGES = 16
PAIRS = 192
BIAS = 4224


def full_image(key):
    return jax.random.randint(jax.random.fold_in(key, 7), (IMAGES // IMG_DEV,), 0, IMG_DEV)


def draw_heights(key, part):
    chosen = full_image(key)
    key = jax.random.fold_in(key, 1)
    drawn_sizes = jax.random.randint(key, (IMAGES,), GH // 4, GH + 1)
    position = jnp.arange(IMAGES) % IMG_DEV
    owner_pick = jnp.repeat(chosen, IMG_DEV)
    return jnp.where(position == owner_pick, GH, drawn_sizes).astype(jnp.int32)


def draw_widths(key, part):
    chosen = full_image(key)
    key = jax.random.fold_in(key, 2)
    drawn_sizes = jax.random.randint(key, (IMAGES,), GW // 4, GW + 1)
    position = jnp.arange(IMAGES) % IMG_DEV
    owner_pick = jnp.repeat(chosen, IMG_DEV)
    return jnp.where(position == owner_pick, GW, drawn_sizes).astype(jnp.int32)


def steps_of(stream_key, extent, shards, least, largest):
    level = 1.0
    for axis_at, parts in shards:
        steps = jax.random.uniform(jax.random.fold_in(jax.random.fold_in(stream_key, 6), axis_at), (parts,), jnp.float32, least / len(shards), largest / len(shards))
        level = level * jnp.repeat(jnp.exp(steps), extent[axis_at] // parts).reshape((-1,) + (1,) * (len(extent) - 1 - axis_at))
    return level


def normal_values(own_key, dims, width, limit, cuts=(), held_as=jnp.bfloat16):
    level = steps_of(own_key, dims, cuts, -0.22, 0.18) if cuts else 1.0
    entries = jax.random.normal(own_key, dims, jnp.float32) * width * level
    return jnp.minimum(jnp.maximum(entries, -limit), limit).astype(held_as)


def setup_inputs(seed: int = 0) -> dict:
    seeds = jax.random.split(jax.random.key(seed), 19)
    patches = normal_values(seeds[0], (IMAGES, GH, GW, D), 1.0, 6.0, ((0, 8), (1, 4)))
    cotangent = normal_values(seeds[1], (IMAGES, GH, GW, D), 1.0, 6.0, ((0, 8), (1, 4)))
    heights = draw_heights(jax.random.fold_in(seeds[18], 71), 0)
    widths = draw_widths(jax.random.fold_in(seeds[18], 71), 0)
    qkv_weight = normal_values(seeds[4], (D, 3 * D), (D // 2) ** -0.5, 0.4375, ((1, 4),), jnp.float32)
    qkv_moment = normal_values(seeds[5], (D, 3 * D), ((IMAGES * GH * GW // 2) ** 0.5), 512.0, ((1, 4),), jnp.float32)
    proj_weight = normal_values(seeds[6], (D, D), (D // 4) ** -0.5, 0.625, ((1, 4),), jnp.float32)
    proj_moment = normal_values(seeds[7], (D, D), ((IMAGES * GH * GW // 2) ** 0.5), 512.0, ((1, 4),), jnp.float32)
    expand_weight = normal_values(seeds[8], (D, FF), D ** -0.5, 0.3125, ((1, 4),), jnp.float32)
    expand_moment = normal_values(seeds[9], (D, FF), ((IMAGES * GH * GW // 2) ** 0.5), 512.0, ((1, 4),), jnp.float32)
    shrink_weight = normal_values(seeds[10], (FF, D), FF ** -0.5, 0.15625, ((0, 4),), jnp.float32)
    shrink_moment = normal_values(seeds[11], (FF, D), ((IMAGES * GH * GW // 2) ** 0.5), 512.0, ((0, 4),), jnp.float32)
    norm_gains = jnp.clip(1.0 + 0.1 * jax.random.normal(seeds[12], (2, D), jnp.float32), 0.5, 1.5)
    gains_moment = normal_values(seeds[13], (2, D), ((IMAGES * GH * GW // 2) ** 0.5), 512.0, ((1, 4),), jnp.float32)
    all_biases = normal_values(seeds[14], (BIAS,), 0.2, 1.0, (), jnp.float32)
    biases_moment = normal_values(seeds[15], (BIAS,), ((IMAGES * GH * GW // 2) ** 0.5), 512.0, ((0, 4),), jnp.float32)
    frequencies = jnp.clip(jax.random.uniform(seeds[16], (2, PAIRS), jnp.float32, -0.5, 0.5), -0.5, 0.5)
    freq_moment = normal_values(seeds[17], (2, PAIRS), (8 * (IMAGES * GH * GW // 2) ** 0.5), 4096.0, ((1, 4),), jnp.float32)
    return {"patches": patches, "cotangent": cotangent, "heights": heights, "widths": widths, "qkv_weight": qkv_weight, "qkv_moment": qkv_moment, "proj_weight": proj_weight, "proj_moment": proj_moment, "expand_weight": expand_weight, "expand_moment": expand_moment, "shrink_weight": shrink_weight, "shrink_moment": shrink_moment, "norm_gains": norm_gains, "gains_moment": gains_moment, "all_biases": all_biases, "biases_moment": biases_moment, "frequencies": frequencies, "freq_moment": freq_moment}


highest = lax.Precision.HIGHEST
coeff_one = 3.4445
coeff_two = -4.775
coeff_three = 2.0315

@jax.custom_vjp
def low(v):
    return lax.optimization_barrier(v.astype(jnp.bfloat16)).astype(jnp.float32)

@jax.custom_vjp
def low_back(v):
    return v

def low_keep(v):
    return (low(v), None)

def low_pass(kept, grad):
    return (grad,)

def back_keep(v):
    return (v, None)

def back_low(kept, grad):
    return (low(grad),)
low.defvjp(low_keep, low_pass)
low_back.defvjp(back_keep, back_low)

def layer_norm(values, gain_row, shift_row):
    centered = values - lax.optimization_barrier(jnp.mean(values, axis=-1, keepdims=True))
    variance = lax.optimization_barrier(jnp.mean(centered * centered, axis=-1, keepdims=True))
    return centered * lax.rsqrt(variance + 1e-06) * gain_row + shift_row

def rotate_half(values, cosine, sine_part):
    half_dim = values.shape[-1] // 2
    first_half = values[..., :half_dim]
    second_half = values[..., half_dim:]
    return jnp.concatenate([first_half * cosine - second_half * sine_part, second_half * cosine + first_half * sine_part], axis=-1)

def image_layer(image_rows, height, image_width, rounded, norm_gains, all_biases, frequencies):
    qkv_w, proj_w, expand_w, shrink_w = rounded
    grid_h = image_rows.shape[0]
    grid_w = image_rows.shape[1]
    length = grid_h * grid_w
    row_pos = jnp.repeat(jnp.arange(grid_h, dtype=jnp.int32), grid_w)
    col_pos = jnp.tile(jnp.arange(grid_w, dtype=jnp.int32), grid_h)
    valid_mask = (row_pos < height) & (col_pos < image_width)
    flat_rows = image_rows.reshape(length, D)
    normed = low(layer_norm(flat_rows, norm_gains[0], all_biases[0:D]))
    mixed_proj = low_back(jnp.dot(normed, qkv_w, precision=highest, preferred_element_type=jnp.float32) + all_biases[2 * D:5 * D])
    queries = mixed_proj[:, :D].reshape(length, H, HD)
    keys_raw = mixed_proj[:, D:2 * D].reshape(length, H, HD)
    values_low = low(mixed_proj[:, 2 * D:]).reshape(length, H, HD)
    angles = row_pos.astype(jnp.float32)[:, None] * frequencies[0][None, :] + col_pos.astype(jnp.float32)[:, None] * frequencies[1][None, :]
    angles = angles.reshape(length, H, HD // 2)
    cosine = jnp.cos(angles)
    sine_part = jnp.sin(angles)
    query_rot = low(rotate_half(queries, cosine, sine_part))
    key_rot = low(rotate_half(keys_raw, cosine, sine_part))
    scores = jnp.einsum('qhd,khd->hqk', query_rot, key_rot, precision=highest) * HD ** (-0.5)
    scores = low_back(jnp.where(valid_mask[None, None, :], scores, -1000000000.0))
    attn_probs = jax.nn.softmax(scores, axis=-1)
    attended = jnp.einsum('hqk,khd->qhd', low(attn_probs), values_low, precision=highest).reshape(length, D)
    attended = low(low_back(attended))
    branch = low_back(jnp.dot(attended, proj_w, precision=highest, preferred_element_type=jnp.float32) + all_biases[5 * D:6 * D])
    residual = flat_rows + branch
    normed_two = low(layer_norm(residual, norm_gains[1], all_biases[D:2 * D]))
    pre_act = low_back(jnp.dot(normed_two, expand_w, precision=highest, preferred_element_type=jnp.float32) + all_biases[6 * D:6 * D + FF])
    hidden = low(jax.nn.gelu(pre_act, approximate=False))
    result = residual + jnp.dot(hidden, shrink_w, precision=highest, preferred_element_type=jnp.float32) + all_biases[6 * D + FF:]
    return (result * valid_mask[:, None].astype(jnp.float32)).reshape(grid_h, grid_w, D)

def orthogonalize(matrix):
    is_tall = matrix.shape[0] > matrix.shape[1]
    current = matrix.T if is_tall else matrix
    current = current / (jnp.sqrt(jnp.sum(current * current)) + 1e-07)
    for sweep_index in range(5):
        gram_one = jnp.dot(current, current.T, precision=highest)
        polynomial = coeff_two * gram_one + coeff_three * jnp.dot(gram_one, gram_one, precision=highest)
        current = coeff_one * current + jnp.dot(polynomial, current, precision=highest)
    return current.T if is_tall else current

def matrix_step(weight, moment, gradient):
    moment_new = 0.5 * moment + gradient
    stretch = 0.05 * math.sqrt(max(weight.shape))
    return (moment_new, weight - stretch * orthogonalize(moment_new))

def vector_step(values, moment, gradient):
    moment_new = 0.5 * moment + gradient
    return (moment_new, values - 0.2 * moment_new * lax.rsqrt(jnp.mean(moment_new * moment_new) + 1e-06))

def reference(patches, cotangent, heights, widths, qkv_weight, qkv_moment, proj_weight, proj_moment, expand_weight, expand_moment, shrink_weight, shrink_moment, norm_gains, gains_moment, all_biases, biases_moment, frequencies, freq_moment):
    floats = patches.astype(jnp.float32)
    masters = (qkv_weight, proj_weight, expand_weight, shrink_weight)

    def forward(floats, masters, norm_gains, all_biases, frequencies):
        rounded = tuple((low(master) for master in masters))

        def scan_step(carry_value, item_data):
            image_rows, height, image_width = item_data
            return (carry_value, image_layer(image_rows, height, image_width, rounded, norm_gains, all_biases, frequencies))
        unused, outputs = lax.scan(jax.checkpoint(scan_step), jnp.zeros((), jnp.float32), (floats, heights, widths))
        return outputs
    outputs, pullback = jax.vjp(forward, floats, masters, norm_gains, all_biases, frequencies)
    patch_grad, weight_grads, gains_grad, biases_grad, freq_grad = pullback(cotangent.astype(jnp.float32))
    qkv_moment_new, qkv_weight_new = matrix_step(qkv_weight, qkv_moment, weight_grads[0])
    proj_moment_new, proj_weight_new = matrix_step(proj_weight, proj_moment, weight_grads[1])
    expand_moment_new, expand_weight_new = matrix_step(expand_weight, expand_moment, weight_grads[2])
    shrink_moment_new, shrink_weight_new = matrix_step(shrink_weight, shrink_moment, weight_grads[3])
    gains_moment_new, norm_gains_new = vector_step(norm_gains, gains_moment, gains_grad)
    biases_moment_new, all_biases_new = vector_step(all_biases, biases_moment, biases_grad)
    freq_moment_new, frequencies_new = vector_step(frequencies, freq_moment, freq_grad)
    return (outputs.astype(jnp.bfloat16), patch_grad, qkv_moment_new, qkv_weight_new, proj_moment_new, proj_weight_new, expand_moment_new, expand_weight_new, shrink_moment_new, shrink_weight_new, gains_moment_new, norm_gains_new, biases_moment_new, all_biases_new, freq_moment_new, frequencies_new)
```

```python
import functools
import math

import jax
import jax.numpy as jnp
from jax import lax
from jax.experimental import pallas as pl
from jax.experimental.pallas import tpu as pltpu
from jax.sharding import PartitionSpec as P

D = 384
H = 6
HD = 64
FF = 1536
HALF = HD // 2
OWN_HEADS = H // 2
OWN = OWN_HEADS * HD
AUG = HD + 16

coeff_one = 3.4445
coeff_two = -4.775
coeff_three = 2.0315

bf16 = jnp.bfloat16
f32 = jnp.float32
AXES = ("batch", "rows")


def dot_nn(a, b):
    return lax.dot_general(a, b, (((1,), (0,)), ((), ())), preferred_element_type=f32)


def dot_nt(a, b):
    return lax.dot_general(a, b, (((1,), (1,)), ((), ())), preferred_element_type=f32)


def dot_tn(a, b):
    return lax.dot_general(a, b, (((0,), (0,)), ((), ())), preferred_element_type=f32)


def kernel_call(body, out_shape, scratch=(), smem=0, n_in=0, limit=52):
    specs = [pl.BlockSpec(memory_space=pltpu.SMEM)] * smem
    specs += [pl.BlockSpec(memory_space=pltpu.VMEM)] * n_in
    return pl.pallas_call(
        body,
        out_shape=out_shape,
        in_specs=specs,
        out_specs=jax.tree.map(lambda _: pl.BlockSpec(memory_space=pltpu.VMEM), out_shape),
        scratch_shapes=list(scratch),
        compiler_params=pltpu.CompilerParams(vmem_limit_bytes=limit * 2**20),
    )


def sds(shape, dtype):
    return jax.ShapeDtypeStruct(shape, dtype)


def norm_rows(x):
    centered = x - jnp.mean(x, axis=-1, keepdims=True)
    rstd = lax.rsqrt(jnp.mean(centered * centered, axis=-1, keepdims=True) + 1e-06)
    return centered * rstd, rstd


def half_blocks(core, shard):
    if isinstance(shard, int):
        base = jnp.where(core == 0, (0, 4, 8, 10)[shard], (0, 2, 4, 8)[shard])
        count = jnp.where(core == 0, (4, 4, 2, 2)[shard], (2, 2, 4, 4)[shard])
        return base, count
    raise TypeError(shard)


def front_kernel(
    pos, own_a, own_b, oth_a, oth_b, w0, w1, w2, w3, bias, gain, shift, cos, sin, rows, cols,
    normed, w_own, qrot, krot, q_aug, k_aug, k_nat, v_nat, logs, o_own, o_oth,
    w_all, v_t, o_all,
):
    core, band, chip = pos[0], pos[1], pos[2]
    tokens = normed.shape[0]
    half = tokens // 2
    block = 256
    for e, ref in enumerate((w0, w1, w2, w3)):
        quarter = lax.bitwise_xor(chip, e)
        for shard in range(4):
            base, count = half_blocks(core, shard)
            at = jnp.where(quarter < count, base + quarter, 12)
            w_all[pl.ds(pl.multiple_of(at * 48, 16), 48), :] = ref[lax.bitwise_xor(band, shard)]
    w_own[...] = w_all[0 : 3 * OWN, :]
    for b, src in enumerate((own_a, own_b, oth_a, oth_b)):
        xhat, _ = norm_rows(src[0:block, :].astype(f32))
        normed[b * block : (b + 1) * block, :] = (xhat * gain[...] + shift[...]).astype(bf16)
    high = own_a[block : block + 1, 0:1].astype(f32)
    wide = own_a[block + 1 : block + 2, 0:1].astype(f32)
    inside = jnp.logical_and(rows[...] < high, cols[...] < wide)
    key_bias = jnp.where(inside, 0.0, -1e9).astype(f32)
    ones_row = (lax.broadcasted_iota(jnp.int32, (AUG - HD, block), 0) == 0).astype(f32)
    for b in range(tokens // block):
        here = slice(b * block, (b + 1) * block)
        mixed = dot_nt(w_own[...], normed[here, :]) + bias[...]
        for h in range(OWN_HEADS):
            c = cos[h * HALF : (h + 1) * HALF, here]
            s = sin[h * HALF : (h + 1) * HALF, here]
            qu = mixed[h * HD : h * HD + HALF, :]
            qw = mixed[h * HD + HALF : (h + 1) * HD, :]
            ku = mixed[OWN + h * HD : OWN + h * HD + HALF, :]
            kw = mixed[OWN + h * HD + HALF : OWN + (h + 1) * HD, :]
            qr = jnp.concatenate([qu * c - qw * s, qw * c + qu * s], axis=0)
            kr = jnp.concatenate([ku * c - kw * s, kw * c + ku * s], axis=0)
            qrot[h * HD : (h + 1) * HD, here] = qr
            krot[h * HD : (h + 1) * HD, here] = kr
            q_low = qr.astype(bf16).astype(f32) * 0.125
            q_aug[h, :, here] = jnp.concatenate([q_low, ones_row], axis=0).astype(bf16)
            k_full = jnp.concatenate([kr, ones_row * key_bias[:, here]], axis=0)
            k_aug[h, :, here] = k_full.astype(bf16)
            k_nat[h, here, :] = k_full.T.astype(bf16)
            vv = mixed[2 * OWN + h * HD : 2 * OWN + (h + 1) * HD, :]
            v_t[h, :, here] = vv.astype(bf16)
            v_nat[h, here, :] = vv.T.astype(bf16)

    blocks = tokens // block

    def attend(item, carry):
        h = item // blocks
        at = pl.multiple_of(lax.rem(item, blocks) * block, block)
        here = pl.ds(at, block)
        scores = dot_nn(k_nat[h], q_aug[h, :, here])
        peak = jnp.max(scores, axis=0, keepdims=True)
        e = jnp.exp(scores - peak)
        total = jnp.sum(e, axis=0, keepdims=True)
        out = dot_nn(v_t[h], (e * (1.0 / total)).astype(bf16))
        logs[h, :, here] = peak + jnp.log(total)
        o_all[h, :, here] = out.astype(bf16)
        return carry

    lax.fori_loop(0, OWN_HEADS * blocks, attend, 0)
    for h in range(OWN_HEADS):
        o_own[h * HD : (h + 1) * HD, :] = o_all[h, :, 0:half]
        o_oth[h * HD : (h + 1) * HD, :] = o_all[h, :, half:tokens]


def front(pos, slabs, weights, bias, gain, shift, cos, sin, rows, cols):
    tokens = rows.shape[1]
    half = tokens // 2
    nh = OWN_HEADS
    outs = (
        sds((tokens, D), bf16),
        sds((3 * OWN, D), bf16),
        sds((OWN, tokens), f32),
        sds((OWN, tokens), f32),
        sds((nh, AUG, tokens), bf16),
        sds((nh, AUG, tokens), bf16),
        sds((nh, tokens, AUG), bf16),
        sds((nh, tokens, HD), bf16),
        sds((nh, 1, tokens), f32),
        sds((OWN, half), bf16),
        sds((OWN, half), bf16),
    )
    scratch = [
        pltpu.VMEM((3 * OWN + 48, D), bf16),
        pltpu.VMEM((nh, HD, tokens), bf16),
        pltpu.VMEM((nh, HD, tokens), bf16),
    ]
    return kernel_call(front_kernel, outs, scratch, 1, 15)(
        pos, *slabs, *weights, bias, gain, shift, cos, sin, rows, cols
    )


def middle_kernel(
    pos, own_a, own_b, cot_a, cot_b, row_col, att_mine, att_oth,
    m0, m1, m2, m3, t0, t1, t2, t3, gain, shift, proj_bias, expand_bias, shrink_bias,
    block_out, d_residual, d_mine, d_send, keep, send, vec,
    p_all, e_one, s_one, att, resid, xhat_s, rstd_s, n2, g16, pre, dh, hidden, dpre, acc, dn2, dat, valid,
):
    core, band, chip = pos[0], pos[1], pos[2]
    half = block_out.shape[0]
    slab = half // 2
    att_t = jnp.concatenate(
        [
            jnp.where(core == 0, att_mine[...].astype(f32), att_oth[...].astype(f32)),
            jnp.where(core == 0, att_oth[...].astype(f32), att_mine[...].astype(f32)),
        ],
        axis=0,
    )
    att[...] = att_t.T.astype(bf16)
    pieces = []
    for e, (mine, other) in enumerate(((m0, t0), (m1, t1), (m2, t2), (m3, t3))):
        chip_e = lax.bitwise_xor(chip, e)
        pieces.append((mine, chip_e * 2 + core))
        pieces.append((other, chip_e * 2 + 1 - core))
    for ref, piece in pieces:
        for d in range(4):
            shard = lax.bitwise_xor(band, d)
            at = jnp.where(piece < 6, shard * 6 + piece, 24)
            p_all[pl.ds(pl.multiple_of(at * 16, 16), 16), :] = ref[d, 0:16, :]
    high = own_a[slab : slab + 1, 0:1].astype(f32)
    wide = own_a[slab + 1 : slab + 2, 0:1].astype(f32)
    inside = jnp.logical_and(row_col[:, 0:1] < high, row_col[:, 1:2] < wide)
    valid[...] = inside.astype(f32)
    g16[0:slab, :] = (cot_a[...].astype(f32) * valid[0:slab, :]).astype(bf16)
    g16[slab:half, :] = (cot_b[...].astype(f32) * valid[slab:half, :]).astype(bf16)
    rows = 128
    proj = p_all[0:D, :]
    for b in range(half // rows):
        here = slice(b * rows, (b + 1) * rows)
        src = own_a if b * rows < slab else own_b
        at = (b * rows) % slab
        res = src[at : at + rows, :].astype(f32) + dot_nt(att[here, :], proj) + proj_bias[...]
        resid[here, :] = res
        xhat, rstd = norm_rows(res)
        xhat_s[here, :] = xhat
        rstd_s[here, :] = rstd
        n2[here, :] = (xhat * gain[...] + shift[...]).astype(bf16)
    acc[...] = jnp.zeros_like(acc)
    dn2[...] = jnp.zeros_like(dn2)
    vec[...] = jnp.zeros_like(vec)

    def chunk(j, carry):
        d = lax.bitwise_xor(band, j)
        for ref, piece in pieces:
            at = pl.ds(pl.multiple_of(piece * 48, 16), 48)
            e_one[at, :] = ref[d, 16:64, :]
            s_one[at, :] = ref[d, 64:112, :]
        pre[...] = dot_nt(n2[...], e_one[...]) + expand_bias[j]
        dh[...] = dot_nt(g16[...], s_one[...])
        for b in range(half // 64):
            here = slice(b * 64, (b + 1) * 64)
            x = pre[here, :]
            cdf = 0.5 * (1.0 + lax.erf(x * math.sqrt(0.5)))
            hidden[here, :] = (x * cdf).astype(bf16)
            slope = cdf + x * (jnp.exp(-0.5 * x * x) * (1.0 / math.sqrt(2.0 * math.pi)))
            dpre[here, :] = (dh[here, :] * slope).astype(bf16)
        acc[...] += dot_nn(hidden[...], s_one[...])
        dn2[...] += dot_nn(dpre[...], e_one[...])
        vec[pl.ds(8 + j, 1), :] = jnp.sum(dpre[...].astype(f32), axis=0, keepdims=True)
        grad_s = dot_tn(hidden[...], g16[...])
        grad_e = dot_tn(dpre[...], n2[...])
        first = core == 0
        kept = jnp.where(first, grad_s, grad_e)
        sent = jnp.where(first, grad_e, grad_s).astype(bf16)
        for q in range(4):
            keep[q, j, 0:96, :] = kept[q * 96 : (q + 1) * 96, :]
            send[q, j, 0:96, :] = sent[q * 96 : (q + 1) * 96, :]
        return carry

    lax.fori_loop(0, 4, chunk, 0)
    block_out[...] = ((resid[...] + acc[...] + shrink_bias[...]) * valid[...]).astype(bf16)
    g = g16[...].astype(f32)
    vec[12:13, :] = jnp.sum(g, axis=0, keepdims=True)
    dn = dn2[...]
    xhat = xhat_s[...]
    vec[3:4, :] = jnp.sum(dn, axis=0, keepdims=True)
    vec[1:2, :] = jnp.sum(dn * xhat, axis=0, keepdims=True)
    dx = dn * gain[...]
    back_x = rstd_s[...] * (
        dx - jnp.mean(dx, axis=-1, keepdims=True) - xhat * jnp.mean(dx * xhat, axis=-1, keepdims=True)
    )
    d_res = g + back_x
    d_residual[...] = d_res
    branch = d_res.astype(bf16)
    vec[7:8, :] = jnp.sum(branch.astype(f32), axis=0, keepdims=True)
    grad_p = dot_tn(branch, att[...])
    rest = jnp.zeros((8, D), f32)
    for z in range(4):
        for q in range(4):
            at = z * 96 + q * 24
            padded = jnp.concatenate([grad_p[at : at + 24, :], rest], axis=0).astype(bf16)
            send[q, z, 96:128, :] = padded
            keep[q, z, 96:128, :] = padded.astype(f32)
    d_att = dot_nn(branch, proj)
    dat[...] = d_att.T.astype(bf16)
    d_mine[...] = dat[pl.ds(pl.multiple_of(core * OWN, 16), OWN), :]
    d_send[...] = dat[pl.ds(pl.multiple_of((1 - core) * OWN, 16), OWN), :]


def middle(pos, own, cot, row_col, att, mine, other, gain, shift, pb, eb, sb):
    half = row_col.shape[0]
    outs = (
        sds((half, D), bf16),
        sds((half, D), f32),
        sds((OWN, half), bf16),
        sds((OWN, half), bf16),
        sds((4, 4, 128, D), f32),
        sds((4, 4, 128, D), bf16),
        sds((16, D), f32),
    )
    v = pltpu.VMEM
    scratch = [
        v((D + 16, D), bf16), v((D, D), bf16), v((D, D), bf16), v((half, D), bf16), v((half, D), f32),
        v((half, D), f32), v((half, 1), f32), v((half, D), bf16), v((half, D), bf16), v((half, D), f32),
        v((half, D), f32), v((half, D), bf16), v((half, D), bf16), v((half, D), f32), v((half, D), f32),
        v((D, half), bf16), v((half, 1), f32),
    ]
    return kernel_call(middle_kernel, outs, scratch, 1, 20)(
        pos, *own, *cot, row_col, *att, *mine, *other, gain, shift, pb, eb, sb
    )


def merge_kernel(pos, keep, recv, mine, s1, s2, s3):
    chip = pos[2]

    def add(z, carry):
        mine[z] = keep[chip, z] + recv[chip, z].astype(f32)
        for e, ref in ((1, s1), (2, s2), (3, s3)):
            at = lax.bitwise_xor(chip, e)
            ref[z] = (keep[at, z] + recv[at, z].astype(f32)).astype(bf16)
        return carry

    lax.fori_loop(0, 4, add, 0)


def merge(pos, keep, recv):
    shape = keep.shape[1:]
    outs = (sds(shape, f32),) + (sds(shape, bf16),) * 3
    return kernel_call(merge_kernel, outs, (), 1, 2)(pos, keep, recv)


def bands_kernel(pos, mine, r1, r2, r3, own, s1, s2, s3):
    band = pos[1]
    for d, ref in ((0, own), (1, s1), (2, s2), (3, s3)):
        z = lax.bitwise_xor(band, d)
        part = (mine[z] + r1[z].astype(f32)) + (r2[z].astype(f32) + r3[z].astype(f32))
        ref[...] = part.astype(ref.dtype)


def bands(pos, mine, received):
    shape = mine.shape[1:]
    outs = (sds(shape, f32),) + (sds(shape, bf16),) * 3
    return kernel_call(bands_kernel, outs, (), 1, 4)(pos, mine, *received)


def piece_kernel(own, r1, r2, r3, mom, out):
    total = (own[...] + r1[...].astype(f32)) + (r2[...].astype(f32) + r3[...].astype(f32))
    out[...] = (total + 0.5 * mom[...]).astype(bf16)


def piece_sum(own, received, mom):
    return kernel_call(piece_kernel, sds(own.shape, bf16), (), 0, 5)(own, *received, mom)


def sum_low_kernel(own, r1, r2, r3, out):
    out[...] = ((own[...].astype(f32) + r1[...].astype(f32)) + (r2[...].astype(f32) + r3[...].astype(f32))).astype(bf16)


def sum_low(own, received):
    return kernel_call(sum_low_kernel, sds(own.shape, bf16), (), 0, 4)(own, *received)


def back_step(k_nat, v_nat, k_t, q_t, g, logs):
    p = jnp.exp(dot_nn(k_nat, q_t) - logs)
    dp = dot_nn(v_nat, g)
    inner = jnp.sum(p * dp, axis=0, keepdims=True)
    ds = (p * (dp - inner)).astype(bf16)
    dv = dot_nt(p.astype(bf16), g)
    dk = dot_nt(ds, q_t[0:HD, :])
    dq = dot_nn(k_t, ds) * 0.125
    return dq, dk, dv


def back_heads_kernel(heads, q_aug, k_aug, k_nat, v_nat, logs, d_mine, d_recv, dq, dk, dv, d_out):
    tokens = q_aug.shape[2]
    half = tokens // 2
    block = 256
    blocks = tokens // block
    count = heads[1] - heads[0]
    for i in range(count):
        h = heads[0] + i
        d_out[i, :, 0:half] = d_mine[h * HD : (h + 1) * HD, :]
        d_out[i, :, half:tokens] = d_recv[h * HD : (h + 1) * HD, :]
    dk[...] = jnp.zeros_like(dk)
    dv[...] = jnp.zeros_like(dv)

    def step(item, carry):
        i = item // blocks
        h = heads[0] + i
        at = pl.multiple_of(lax.rem(item, blocks) * block, block)
        here = pl.ds(at, block)
        dq_one, dk_one, dv_one = back_step(
            k_nat[h], v_nat[h], k_aug[h, 0:HD, :], q_aug[h, :, here], d_out[i, :, here], logs[h, :, here]
        )
        dv[i] += dv_one
        dk[i] += dk_one
        dq[i, :, here] = dq_one
        return carry

    lax.fori_loop(0, count * blocks, step, 0)


def back_heads(heads, q_aug, k_aug, k_nat, v_nat, logs, d_mine, d_recv):
    tokens = q_aug.shape[2]
    n = heads[1] - heads[0]
    outs = (sds((n, HD, tokens), f32), sds((n, tokens, HD), f32), sds((n, tokens, HD), f32))
    return kernel_call(functools.partial(back_heads_kernel, heads), outs, [pltpu.VMEM((n, HD, tokens), bf16)], 0, 7)(
        q_aug, k_aug, k_nat, v_nat, logs, d_mine, d_recv
    )


def back_kernel(
    pos, normed, w_own, qrot, krot, dq_a, dk_a, dv_a, dq_b, dk_b, dv_b, cos, sin, rows, cols, own_a, own_b, oth_a, oth_b,
    mom, vec_in,
    mine, s1, s2, s3, dn_own, dn_oth,
    dm, dm_full, freq, d_w, vec,
):
    core, band, chip, group = pos[0], pos[1], pos[2], pos[3]
    tokens = normed.shape[0]
    half = tokens // 2
    slab = half // 2
    dm_full[...] = jnp.zeros_like(dm_full)
    freq[...] = jnp.zeros_like(freq)
    for h in range(OWN_HEADS):
        c = cos[h * HALF : (h + 1) * HALF, :]
        s = sin[h * HALF : (h + 1) * HALF, :]
        na = dq_a.shape[0]
        dq, dk, dv, i = (dq_a, dk_a, dv_a, h) if h < na else (dq_b, dk_b, dv_b, h - na)
        angle = None
        for which, source, rotated in ((0, dq[i], qrot), (1, dk[i].T, krot)):
            du = source[0:HALF, :]
            dw = source[HALF:HD, :]
            u = rotated[h * HD : h * HD + HALF, :]
            w = rotated[h * HD + HALF : (h + 1) * HD, :]
            turn = dw * u - du * w
            angle = turn if angle is None else angle + turn
            at = which * OWN + h * HD
            dm[at : at + HD, :] = jnp.concatenate([du * c + dw * s, dw * c - du * s], axis=0).astype(bf16)
        at = pl.multiple_of(core * 96 + h * HALF, 32)
        freq[pl.ds(at, HALF), :] = jnp.sum(angle * rows[...], axis=1, keepdims=True)
        at = pl.multiple_of(192 + core * 96 + h * HALF, 32)
        freq[pl.ds(at, HALF), :] = jnp.sum(angle * cols[...], axis=1, keepdims=True)
        at = 2 * OWN + h * HD
        dm[at : at + HD, :] = dv[i].T.astype(bf16)
    for t in range(3):
        at = pl.multiple_of(t * D + core * OWN, 16)
        dm_full[pl.ds(at, OWN), :] = dm[t * OWN : (t + 1) * OWN, :]
    d_w[...] = dot_nn(dm[...], normed[...])
    for j in range(3):
        whole = band * 3 + j
        here = jnp.logical_and(lax.rem(whole, 4) // 2 == core, group == 0)
        at = pl.multiple_of(((whole // 4) * 2 + lax.rem(whole, 2)) * 96, 32)

        @pl.when(here)
        def _():
            d_w[pl.ds(at, 96), :] += 0.5 * mom[j * 96 : (j + 1) * 96, :]

    vec[...] = vec_in[...]
    sums = dot_nt(jnp.ones((8, tokens), bf16), dm_full[...])
    for t in range(3):
        vec[4 + t : 5 + t, :] += sums[0:1, t * D : (t + 1) * D]
    vec[13:14, :] += jnp.broadcast_to(freq[...], (D, 128)).T[0:1, :]
    for b, src in enumerate((own_a, own_b, oth_a, oth_b)):
        part = dot_tn(dm[:, b * slab : (b + 1) * slab], w_own[...])
        xhat, _ = norm_rows(src[0:slab, :].astype(f32))
        vec[0:1, :] += jnp.sum(part * xhat, axis=0, keepdims=True)
        vec[2:3, :] += jnp.sum(part, axis=0, keepdims=True)
        to, at = (dn_own, b) if b < 2 else (dn_oth, b - 2)
        to[at * slab : (at + 1) * slab, :] = part
    low = vec[...].astype(bf16)
    rows_q = mine.shape[0] - 16
    for e, ref in ((0, mine), (1, s1), (2, s2), (3, s3)):
        at = pl.multiple_of(lax.bitwise_xor(chip, e) * rows_q, 16)
        ref[0:rows_q, :] = d_w[pl.ds(at, rows_q), :].astype(ref.dtype)
        ref[rows_q : rows_q + 16, :] = low.astype(ref.dtype)


def back(pos, normed, w_own, qrot, krot, first, second, cos, sin, rows, cols, slabs, mom, vec_in):
    tokens = normed.shape[0]
    half = tokens // 2
    shape = (3 * OWN // 4 + 16, D)
    outs = (sds(shape, f32),) + (sds(shape, bf16),) * 3 + (sds((half, D), f32),) * 2
    v = pltpu.VMEM
    scratch = [
        v((3 * OWN, tokens), bf16),
        v((3 * D, tokens), bf16),
        v((D, 1), f32),
        v((3 * OWN, D), f32),
        v((16, D), f32),
    ]
    return kernel_call(back_kernel, outs, scratch, 1, 20)(
        pos, normed, w_own, qrot, krot, *first, *second, cos, sin, rows, cols, *slabs, mom, vec_in
    )


def tail_kernel(own_a, own_b, d_residual, dn_one, dn_two, gain, out_a, out_b):
    slab = out_a.shape[0]
    for b, (src, out) in enumerate(((own_a, out_a), (own_b, out_b))):
        here = slice(b * slab, (b + 1) * slab)
        xhat, rstd = norm_rows(src[0:slab, :].astype(f32))
        dx = (dn_one[here, :] + dn_two[here, :]) * gain[...]
        back_x = rstd * (
            dx - jnp.mean(dx, axis=-1, keepdims=True) - xhat * jnp.mean(dx * xhat, axis=-1, keepdims=True)
        )
        out[...] = d_residual[here, :] + back_x


def tail(own, d_residual, dn_one, dn_two, gain):
    slab = d_residual.shape[0] // 2
    outs = (sds((slab, D), f32),) * 2
    return kernel_call(tail_kernel, outs, (), 0, 6)(*own, d_residual, dn_one, dn_two, gain)


def split_low(x):
    high = x.astype(bf16)
    return high, (x - high.astype(f32)).astype(bf16)


def dot_three(a, b):
    return dot_nn(a[0], b[0]) + (dot_nn(a[0], b[1]) + dot_nn(a[1], b[0]))


def sweeps(gram):
    row = lax.broadcasted_iota(jnp.int32, (D, D), 0)
    col = lax.broadcasted_iota(jnp.int32, (D, D), 1)
    eye = (row == col).astype(f32)
    trace = jnp.sum(jnp.sum(gram * eye, axis=1, keepdims=True), axis=0, keepdims=True)
    scale = 1.0 / (jnp.sqrt(trace) + 1e-07)
    a = gram * (scale * scale)
    total = None
    for sweep in range(5):
        a2 = split_low(a)
        poly = coeff_one * eye + coeff_two * a + coeff_three * dot_three(a2, a2)
        p2 = split_low(poly)
        total = poly if total is None else dot_three(p2, split_low(total))
        if sweep < 4:
            a = dot_three(split_low(dot_three(p2, a2)), p2)
    return total * scale


def muon_big_kernel(pos, a0, a1, a2, a3, out, band_rows, big):
    chip = pos[2]
    for e, ref in enumerate((a0, a1, a2, a3)):
        for d in range(4):
            at = (e * 4 + d) * 96
            big[at : at + 96, :] = ref[d, 0:96, :]
        at = pl.multiple_of(lax.bitwise_xor(chip, e) * 96, 32)
        band_rows[pl.ds(at, 96), :] = ref[0, 0:96, :]
    out[...] = sweeps(dot_tn(big[...], big[...]))


def muon_big(pos, parts):
    outs = (sds((D, D), f32), sds((D, D), bf16))
    return kernel_call(muon_big_kernel, outs, [pltpu.VMEM((FF, D), bf16)], 1, 4)(pos, *parts)


def muon_small_kernel(pos, a0, a1, a2, a3, q0, q1, q2, q3, o0, o1, o2, o3, out, gram, rows):
    core = pos[0]
    n = q0.shape[0] - 16

    @pl.when(core == 0)
    def _():
        for e, ref in enumerate((q0, q1, q2, q3, o0, o1, o2, o3)):
            rows[e * n : (e + 1) * n, :] = ref[0:n, :]
        gram[...] = dot_tn(rows[...], rows[...])

    @pl.when(core != 0)
    def _():
        for e, ref in enumerate((a0, a1, a2, a3)):
            for d in range(4):
                at = (e * 4 + d) * 32
                rows[at : at + 32, :] = ref[d, 96:128, :]
        gram[...] = dot_tn(rows[0:512, :], rows[0:512, :])

    out[...] = sweeps(gram[...])


def muon_small(pos, parts, own_q, oth_q):
    scratch = [pltpu.VMEM((D, D), f32), pltpu.VMEM((3 * D, D), bf16)]
    return kernel_call(muon_small_kernel, sds((D, D), f32), scratch, 1, 12)(pos, *parts, *own_q, *oth_q)


def final_kernel(
    pos, one, one_oth, two, two_oth, band_mine, band_oth, a0, a1, a2, a3, q0, q1, q2, q3, o0, o1, o2, o3,
    qkv_w, proj_w, expand_w, shrink_w,
    qkv_m, qkv_new, proj_m, proj_new, expand_m, expand_new, shrink_m, shrink_new,
    proj_rows, q_mine, q_oth, q_rows,
):
    core, band, chip = pos[0], pos[1], pos[2]
    first = core == 0
    n = q0.shape[0] - 16

    def choose(when_first, a, b):
        return split_low(jnp.where(first == when_first, a[...], b[...]))

    for e, ref in enumerate((a0, a1, a2, a3)):
        at = pl.multiple_of(lax.bitwise_xor(chip, e) * 24, 8)
        proj_rows[pl.ds(at, 24), :] = ref[0, 96:128, :].astype(f32)[0:24, :]
    for e in range(4):
        at = pl.multiple_of(lax.bitwise_xor(chip, e) * n, 16)
        q_mine[pl.ds(at, n), :] = (q0, q1, q2, q3)[e][0:n, :]
        q_oth[pl.ds(at, n), :] = (o0, o1, o2, o3)[e][0:n, :]
    for j in range(3):
        whole = band * 3 + j
        at = pl.multiple_of(((whole // 4) * 2 + lax.rem(whole, 2)) * 96, 32)
        mine = lax.rem(whole, 4) // 2 == core

        @pl.when(mine)
        def _():
            q_rows[j * 96 : (j + 1) * 96, :] = q_mine[pl.ds(at, 96), :]

        @pl.when(jnp.logical_not(mine))
        def _():
            q_rows[j * 96 : (j + 1) * 96, :] = q_oth[pl.ds(at, 96), :]

    m_shrink = jnp.where(first, band_mine[...].astype(f32), band_oth[...].astype(f32))
    m_expand = jnp.where(first, band_oth[...].astype(f32), band_mine[...].astype(f32))
    t_shrink, t_expand = choose(True, one, one_oth), choose(False, one, one_oth)
    t_qkv, t_proj = choose(True, two, two_oth), choose(False, two, two_oth)
    for w, t, m, mom, new, size in (
        (qkv_w, t_qkv, q_rows[...].astype(f32), qkv_m, qkv_new, 3 * D),
        (proj_w, t_proj, proj_rows[...], proj_m, proj_new, D),
        (expand_w, t_expand, m_expand, expand_m, expand_new, FF),
    ):
        low = m.astype(bf16)
        mom[...] = m.T
        new[...] = w[...] - 0.05 * math.sqrt(size) * (dot_nt(t[0], low) + dot_nt(t[1], low))
    low = m_shrink.astype(bf16)
    shrink_m[...] = m_shrink
    shrink_new[...] = shrink_w[...] - 0.05 * math.sqrt(FF) * (dot_nn(low, t_shrink[0]) + dot_nn(low, t_shrink[1]))


def final(pos, one, one_oth, two, two_oth, band_mine, band_oth, parts, own_q, oth_q, *weights):
    outs = []
    for w in weights:
        outs += [sds(w.shape, f32)] * 2
    v = pltpu.VMEM
    scratch = [v((96, D), f32), v((3 * OWN, D), bf16), v((3 * OWN, D), bf16), v((288, D), bf16)]
    return kernel_call(final_kernel, tuple(outs), scratch, 1, 22)(
        pos, one, one_oth, two, two_oth, band_mine, band_oth, *parts, *own_q, *oth_q, *weights
    )


def flip(x, bit):
    n = lax.axis_size("batch")
    return lax.ppermute(x, "batch", [(i, i ^ bit) for i in range(n)])


def swap_bands(x, d):
    return lax.ppermute(x, "rows", [(i, i ^ d) for i in range(4)])


def moves(which):
    pairs = []
    for k in range(lax.axis_size("batch") // 2):
        for c in range(2):
            for i in range(4):
                band = (i - 2 * c - which) % 4
                pairs.append(((2 * k + i // 2) * 4 + band, (2 * k + c) * 4 + i))
    return pairs


def to_image(slabs, band):
    even = band % 2 == 0
    return [
        lax.ppermute(jnp.where(even, slabs[which], slabs[1 - which]), AXES, moves(which)) for which in range(2)
    ]


def from_image(parts, band):
    got = [lax.ppermute(parts[which], AXES, [(b, a) for a, b in moves(which)]) for which in range(2)]
    even = band % 2 == 0
    return jnp.stack([jnp.where(even, got[0], got[1]), jnp.where(even, got[1], got[0])])


def pick(x, at, axis=0):
    return lax.dynamic_index_in_dim(x, at, axis, keepdims=False)


def other_chips(x):
    bit = 8
    while bit < lax.axis_size("batch"):
        x = x + flip(x.astype(f32), bit).astype(x.dtype)
        bit *= 2
    return x


def over_chips(x):
    return [flip(x, 2 * e) for e in range(1, 4)]


def over_bands(x):
    return [swap_bands(x, d) for d in range(1, 4)]


def local(
    patches,
    cotangent,
    heights,
    widths,
    qkv_weight,
    qkv_moment,
    proj_weight,
    proj_moment,
    expand_weight,
    expand_moment,
    shrink_weight,
    shrink_moment,
    norm_gains,
    gains_moment,
    all_biases,
    biases_moment,
    frequencies,
    freq_moment,
):
    images, band_rows, grid_w, _ = patches.shape
    slab = band_rows * grid_w
    batch = lax.axis_index("batch")
    band = lax.axis_index("rows")
    core = batch % 2
    chip = (batch // 2) % 4
    first = core == 0
    group = batch // 2
    pos = jnp.stack([core, band, chip, group]).astype(jnp.int32)

    sizes = jnp.stack([heights, widths], axis=1).astype(bf16)
    size_rows = jnp.concatenate([sizes, jnp.zeros((images, 14), bf16)], axis=1)
    with_size = jnp.concatenate(
        [patches.reshape(images, slab, D), jnp.broadcast_to(size_rows[:, :, None], (images, 16, D))], axis=1
    )
    own = to_image(with_size, band)
    oth = [flip(x, 1) for x in own]
    start = pick(pick(jnp.array([[0, 2, 4, 0], [4, 0, 0, 2]], jnp.int32), core), band)
    count = pick(pick(jnp.array([[4, 4, 2, 2], [2, 2, 4, 4]], jnp.int32), core), band)
    qkv_at = 48 * (start + jnp.minimum(chip, count - 1))
    piece = 2 * chip + core
    proj_at = 16 * jnp.where(piece < 6, piece, 0)
    shard16 = jnp.concatenate(
        [
            lax.dynamic_slice_in_dim(qkv_weight.T.astype(bf16), qkv_at, 48, 0),
            lax.dynamic_slice_in_dim(proj_weight.T.astype(bf16), proj_at, 16, 0),
            lax.dynamic_slice_in_dim(expand_weight.T.astype(bf16), piece * 48, 48, 0),
            lax.dynamic_slice_in_dim(shrink_weight.astype(bf16), piece * 48, 48, 0),
        ]
    )
    shards = jnp.stack([shard16] + over_bands(shard16))
    qkv_own = shards[:, 0:48]
    w_qkv = [qkv_own] + over_chips(qkv_own)
    rest_own = shards[:, 48:160]
    w_rest = [rest_own] + over_chips(rest_own)
    w_rest_oth = [flip(x, 1) for x in w_rest]
    cot = to_image(cotangent.reshape(images, slab, D), band)

    slots = jnp.stack([2 * core, 2 * core + 1, 2 - 2 * core, 3 - 2 * core])
    slot_band = (band - slots) % 4
    rows_one = slot_band[:, None] * band_rows + jnp.arange(band_rows)[None, :]
    rows_tok = jnp.repeat(rows_one.reshape(-1), grid_w).astype(f32)
    cols_tok = jnp.tile(jnp.arange(grid_w), 4 * band_rows).astype(f32)
    row_col = jnp.stack([rows_tok, cols_tok], axis=1)[: 2 * slab]
    freq_own = lax.dynamic_slice_in_dim(frequencies, core * 96, 96, 1)
    angle = freq_own[0][:, None] * rows_tok[None, :] + freq_own[1][:, None] * cols_tok[None, :]
    cos, sin = jnp.cos(angle), jnp.sin(angle)
    rows_tok, cols_tok = rows_tok[None, :], cols_tok[None, :]

    gain_one, gain_two = norm_gains[0][None, :], norm_gains[1][None, :]
    shift_one, shift_two = all_biases[0:D][None, :], all_biases[D : 2 * D][None, :]
    qkv_bias = all_biases[2 * D : 5 * D].reshape(3, 2, OWN)
    bias_own = pick(qkv_bias, core, 1).reshape(3 * OWN, 1)
    proj_bias = all_biases[5 * D : 6 * D][None, :]
    expand_bias = all_biases[6 * D : 6 * D + FF].reshape(4, 1, D)
    shrink_bias = all_biases[6 * D + FF :][None, :]

    mom_s = pick(shrink_moment.reshape(4, 96, D), chip)
    mom_e = pick(expand_moment.T.reshape(4, 96, D), chip)
    mom_p = pick(proj_moment.T.reshape(4, 24, D), chip)
    mom_big = jnp.concatenate([jnp.where(first, mom_s, mom_e), mom_p, jnp.zeros((8, D), f32)])
    n_bias = all_biases.shape[0]

    def placed(shape, part, axis):
        return lax.dynamic_update_slice_in_dim(
            jnp.zeros(shape, f32), part, band * (shape[axis] // 4), axis
        ).reshape(-1)

    vec_mom = jnp.concatenate(
        [
            placed((2, D), gains_moment, 1),
            placed((n_bias,), biases_moment, 0),
            placed((2, H * HALF), freq_moment, 1),
            jnp.zeros((2 * D,), f32),
        ]
    ).reshape(16, D)
    vec_mom = jnp.where(batch == 0, 0.5 * vec_mom, 0.0)
    qkv_mom = qkv_moment.T

    normed, w_own, qrot, krot, q_aug, k_aug, k_nat, v_nat, logs, o_own, o_oth = front(
        pos, own + oth, w_qkv, bias_own, gain_one, shift_one, cos, sin, rows_tok, cols_tok
    )
    o_recv = flip(o_oth, 1)
    block_own, d_residual, d_mine, d_send, keep, send, vec_mid = middle(
        pos, own, cot, row_col, (o_own, o_recv), w_rest, w_rest_oth, gain_two, shift_two, proj_bias, expand_bias, shrink_bias
    )
    d_recv = flip(d_send, 1)
    heads_args = (q_aug, k_aug, k_nat, v_nat, logs, d_mine, d_recv)
    head_a = back_heads((0, 1), *heads_args)
    mine_big, *to_chips = merge(pos, keep, flip(send, 1))
    k_aug, to_chips = lax.optimization_barrier((k_aug, to_chips))
    from_chips = [flip(x, 2 * e) for e, x in zip((1, 2, 3), to_chips)]
    head_b = back_heads((1, 3), q_aug, k_aug, *heads_args[2:])
    mine_q, s1, s2, s3, dn_own, dn_oth = back(
        pos, normed, w_own, qrot, krot, head_a, head_b, cos, sin, rows_tok, cols_tok, own + oth, qkv_mom, vec_mid + vec_mom
    )
    dn_recv = flip(dn_oth, 1)
    q_chips = [flip(x, 2 * e) for e, x in zip((1, 2, 3), (s1, s2, s3))]

    mine_big = other_chips(mine_big)
    own_big, *to_bands = bands(pos, mine_big, from_chips)
    from_bands = [swap_bands(x, d) for d, x in zip((1, 2, 3), to_bands)]
    patch_own = tail(own, d_residual, dn_own, dn_recv, gain_one)

    q_low = other_chips(sum_low(mine_q, q_chips))
    q_piece = sum_low(q_low, over_bands(q_low))
    own_q = [q_piece] + over_chips(q_piece)
    oth_q = [flip(x, 1) for x in own_q]

    big_piece = piece_sum(own_big, from_bands, mom_big)
    big_bands = jnp.stack([big_piece] + over_bands(big_piece))
    big_all = [big_bands] + over_chips(big_bands)

    one, band_mine = muon_big(pos, big_all)
    one_oth, band_oth = flip(one, 1), flip(band_mine, 1)
    two = muon_small(pos, big_all, own_q, oth_q)
    two_oth = flip(two, 1)
    new = final(
        pos, one, one_oth, two, two_oth, band_mine, band_oth, big_all, own_q, oth_q,
        qkv_weight, proj_weight, expand_weight, shrink_weight,
    )

    block_out = from_image([block_own[:slab], block_own[slab:]], band).reshape(images, band_rows, grid_w, D)
    patch_grad = from_image(patch_own, band).reshape(images, band_rows, grid_w, D)

    vec = (own_q[0][-16:].astype(f32) + oth_q[0][-16:].astype(f32)).reshape(-1)

    def vector_step(values, new, axis):
        stepped = values - 0.2 * new * lax.rsqrt(jnp.mean(new * new) + 1e-06)
        size_one = new.shape[axis] // 4
        return (
            lax.dynamic_slice_in_dim(new, band * size_one, size_one, axis),
            lax.dynamic_slice_in_dim(stepped, band * size_one, size_one, axis),
        )

    vectors = (
        vector_step(norm_gains, vec[: 2 * D].reshape(2, D), 1)
        + vector_step(all_biases, vec[2 * D : 2 * D + n_bias], 0)
        + vector_step(frequencies, vec[2 * D + n_bias : 2 * D + n_bias + H * HD].reshape(2, H * HALF), 1)
    )
    return (block_out, patch_grad) + tuple(new) + vectors


def solution(mesh):
    image = P("batch", "rows", None, None)
    cols, rows = P(None, "rows"), P("rows", None)
    return jax.shard_map(
        local,
        mesh=mesh,
        in_specs=(
            image, image, P("batch"), P("batch"), cols, cols, cols, cols, cols, cols, rows, rows,
            P(), cols, P(), P("rows"), P(), cols,
        ),
        out_specs=(
            image, image, cols, cols, cols, cols, cols, cols, rows, rows, cols, cols, P("rows"), P("rows"), cols, cols,
        ),
        check_vma=False,
    )
```

```python
import functools
import math

import jax
import jax.numpy as jnp
from jax import lax
from jax.experimental import pallas as pl
from jax.experimental.pallas import tpu as pltpu
from jax.sharding import PartitionSpec as P

D = 384
H = 6
HD = 64
FF = 1536
HALF = HD // 2
OWN_HEADS = H // 2
OWN = OWN_HEADS * HD
AUG = HD + 16

coeff_one = 3.4445
coeff_two = -4.775
coeff_three = 2.0315

bf16 = jnp.bfloat16
f32 = jnp.float32
AXES = ("batch", "rows")


def dot_nn(a, b):
    return lax.dot_general(a, b, (((1,), (0,)), ((), ())), preferred_element_type=f32)


def dot_nt(a, b):
    return lax.dot_general(a, b, (((1,), (1,)), ((), ())), preferred_element_type=f32)


def dot_tn(a, b):
    return lax.dot_general(a, b, (((0,), (0,)), ((), ())), preferred_element_type=f32)


def vmem_bytes(x):
    *lead, rows, lanes = (1,) * max(0, 2 - len(x.shape)) + tuple(x.shape)
    size = jnp.dtype(x.dtype).itemsize
    tile = 8 * 4 // size
    return math.prod(lead) * (-(-rows // tile) * tile) * (-(-lanes // 128) * 128) * size


def kernel_call(body, out_shape, scratch=(), smem=0, n_in=0, extra=4):
    specs = [pl.BlockSpec(memory_space=pltpu.SMEM)] * smem
    specs += [pl.BlockSpec(memory_space=pltpu.VMEM)] * n_in

    def call(*args):
        held = list(args[smem:]) + jax.tree.leaves(out_shape) + [s for s in scratch]
        limit = sum(vmem_bytes(x) for x in held) + extra * 2**20
        return pl.pallas_call(
            body,
            out_shape=out_shape,
            in_specs=specs,
            out_specs=jax.tree.map(lambda _: pl.BlockSpec(memory_space=pltpu.VMEM), out_shape),
            scratch_shapes=list(scratch),
            compiler_params=pltpu.CompilerParams(vmem_limit_bytes=int(limit)),
        )(*args)

    return call


def sds(shape, dtype):
    return jax.ShapeDtypeStruct(shape, dtype)


def norm_rows(x):
    centered = x - jnp.mean(x, axis=-1, keepdims=True)
    rstd = lax.rsqrt(jnp.mean(centered * centered, axis=-1, keepdims=True) + 1e-06)
    return centered * rstd, rstd


def weights_kernel(pos, qkv_t, proj_t, expand, shrink, out, q_s, p_s, e_s, s_s, sem_q, sem_p, sem_e, sem_s):
    core, band, chip = pos[0], pos[1], pos[2]
    start = jnp.where(core == 0, jnp.where(band < 3, 2 * band, 0), jnp.where(band == 0, 4, jnp.where(band == 3, 2, 0)))
    count = jnp.where((core == 0) == (band < 2), 4, 2)
    at_q = pl.multiple_of((start + jnp.minimum(chip, count - 1)) * 48, 8)
    at_p = pl.multiple_of(jnp.minimum(chip, 2) * 32, 8)
    at = pl.multiple_of(core * 192 + chip * 48, 8)
    copies = (
        pltpu.make_async_copy(expand, e_s, sem_e),
        pltpu.make_async_copy(qkv_t.at[pl.ds(at_q, 48), :], q_s, sem_q),
        pltpu.make_async_copy(proj_t.at[pl.ds(at_p, 32), :], p_s, sem_p),
        pltpu.make_async_copy(shrink.at[pl.ds(at, 48), :], s_s, sem_s),
    )
    for copy in copies:
        copy.start()
    for copy in copies[1:]:
        copy.wait()
    out[0:48, :] = q_s[...].astype(bf16)
    out[48:80, :] = p_s[...].astype(bf16)
    out[128:176, :] = s_s[...].astype(bf16)
    copies[0].wait()
    e_s[...] = e_s[...].T
    out[80:128, :] = e_s[pl.ds(at, 48), :].astype(bf16)


def own_weights(pos, qkv_t, proj_t, expand, shrink):
    v = pltpu.VMEM
    dma = pltpu.SemaphoreType.DMA
    scratch = [v((48, D), f32), v((32, D), f32), v((D, D), f32), v((48, D), f32), dma, dma, dma, dma]
    hbm = pl.BlockSpec(memory_space=pltpu.HBM)
    return pl.pallas_call(
        weights_kernel,
        out_shape=sds((176, D), bf16),
        in_specs=[pl.BlockSpec(memory_space=pltpu.SMEM)] + [hbm] * 4,
        out_specs=pl.BlockSpec(memory_space=pltpu.VMEM),
        scratch_shapes=scratch,
        compiler_params=pltpu.CompilerParams(vmem_limit_bytes=16 * 2**20),
    )(pos, qkv_t, proj_t, expand, shrink)


def slabs_kernel(pos, heights, widths, patches, cot, p_a, p_b, c_a, c_b):
    band = pos[1]
    slab = patches.shape[1]
    row = lax.broadcasted_iota(jnp.int32, (16, D), 0)
    for which, (p, c) in enumerate(((p_a, c_a), (p_b, c_b))):
        image = lax.rem(band + which, 2)
        p[0:slab, :] = patches[image]
        size = jnp.where(row == 0, heights[image], widths[image])
        p[slab : slab + 16, :] = size.astype(f32).astype(bf16)
        c[...] = cot[image]


def slabs(pos, heights, widths, patches, cot):
    slab = patches.shape[1]
    outs = (sds((slab + 16, D), bf16),) * 2 + (sds((slab, D), bf16),) * 2
    return kernel_call(slabs_kernel, outs, (), 3, 2)(pos, heights, widths, patches, cot)


def setup_kernel(
    pos, freq, biases, expand_mom, shrink_mom, cos, sin, rows, cols, bias_own, mom_big, column, turned, band_rows, grid_w
):
    core, band, chip = pos[0], pos[1], pos[2]
    tokens = rows.shape[1]
    slab = band_rows * grid_w
    token = lax.broadcasted_iota(jnp.int32, (1, tokens), 1)
    slot = token // slab
    d = jnp.where(slot < 2, 2 * core + slot, 2 - 2 * core + slot - 2)
    row = lax.bitwise_and(band + 4 - d, 3) * band_rows + lax.rem(token, slab) // grid_w
    rows[...] = row.astype(f32)
    cols[...] = lax.rem(token, grid_w).astype(f32)
    angle = freq[:, 0:1] * rows[...] + freq[:, 1:2] * cols[...]
    cos[...] = jnp.cos(angle)
    sin[...] = jnp.sin(angle)
    for t in range(3):
        column[...] = jnp.broadcast_to(biases[2 + t : 3 + t, :], (128, D)).T
        at = pl.multiple_of(core * OWN, 8)
        bias_own[t * OWN : (t + 1) * OWN, :] = column[pl.ds(at, OWN), 0:1]
    at = pl.multiple_of(core * 192 + chip * 48, 8)
    mom_big[0:48, :] = shrink_mom[pl.ds(at, 48), :]
    turned[...] = expand_mom[...].T
    mom_big[48:96, :] = turned[pl.ds(at, 48), :]


def setup(pos, freq, biases, expand_mom, shrink_mom, tokens, band_rows, grid_w):
    v = pltpu.VMEM
    outs = (
        sds((96, tokens), f32),
        sds((96, tokens), f32),
        sds((1, tokens), f32),
        sds((1, tokens), f32),
        sds((3 * OWN, 1), f32),
        sds((96, D), f32),
    )
    body = functools.partial(setup_kernel, band_rows=band_rows, grid_w=grid_w)
    return kernel_call(body, outs, [v((D, 128), f32), v((D, D), f32)], 1, 4)(pos, freq, biases, expand_mom, shrink_mom)


def pack_kernel(own, r1, r2, r3, qkv, first, second):
    for d, ref in enumerate((own, r1, r2, r3)):
        qkv[d] = ref[0:48, :]
        first[d] = ref[48:128, :]
        second[d] = ref[128:176, :]


def pack(own, received):
    outs = (sds((4, 48, D), bf16), sds((4, 80, D), bf16), sds((4, 48, D), bf16))
    return kernel_call(pack_kernel, outs, (), 0, 4)(own, *received)


def front_kernel(
    pos, own_a, own_b, oth_a, oth_b, w0, w1, w2, w3, bias, gains, biases, cos, sin, rows, cols,
    normed, w_own, qrot, krot, q_aug, k_aug, k_nat, v_nat, logs, o_own, o_oth,
    w_all, v_t, o_all,
):
    core, band, chip = pos[0], pos[1], pos[2]
    tokens = normed.shape[0]
    block = tokens // 4
    for e, ref in enumerate((w0, w1, w2, w3)):
        quarter = lax.bitwise_xor(chip, e)
        for shard in range(4):
            base = jnp.where(core == 0, (0, 4, 8, 10)[shard], (0, 2, 4, 8)[shard])
            count = jnp.where(core == 0, (4, 4, 2, 2)[shard], (2, 2, 4, 4)[shard])
            at = jnp.where(quarter < count, base + quarter, 12)
            w_all[pl.ds(pl.multiple_of(at * 48, 16), 48), :] = ref[lax.bitwise_xor(band, shard)]
    w_own[...] = w_all[0 : 3 * OWN, :]
    for b, src in enumerate((own_a, own_b, oth_a, oth_b)):
        xhat, _ = norm_rows(src[0:block, :].astype(f32))
        normed[b * block : (b + 1) * block, :] = (xhat * gains[0:1, :] + biases[0:1, :]).astype(bf16)
    high = own_a[block : block + 1, 0:1].astype(f32)
    wide = own_a[block + 1 : block + 2, 0:1].astype(f32)
    inside = jnp.logical_and(rows[...] < high, cols[...] < wide)
    key_bias = jnp.where(inside, 0.0, -1e9).astype(f32)
    ones_row = (lax.broadcasted_iota(jnp.int32, (AUG - HD, block), 0) == 0).astype(f32)
    for b in range(4):
        here = slice(b * block, (b + 1) * block)
        mixed = dot_nt(w_own[...], normed[here, :]) + bias[...]
        for h in range(OWN_HEADS):
            c = cos[h * HALF : (h + 1) * HALF, here]
            s = sin[h * HALF : (h + 1) * HALF, here]
            qu = mixed[h * HD : h * HD + HALF, :]
            qw = mixed[h * HD + HALF : (h + 1) * HD, :]
            ku = mixed[OWN + h * HD : OWN + h * HD + HALF, :]
            kw = mixed[OWN + h * HD + HALF : OWN + (h + 1) * HD, :]
            qr = jnp.concatenate([qu * c - qw * s, qw * c + qu * s], axis=0)
            kr = jnp.concatenate([ku * c - kw * s, kw * c + ku * s], axis=0)
            qrot[h * HD : (h + 1) * HD, here] = qr
            krot[h * HD : (h + 1) * HD, here] = kr
            q_low = qr.astype(bf16).astype(f32) * 0.125
            q_aug[h, :, here] = jnp.concatenate([q_low, ones_row], axis=0).astype(bf16)
            k_full = jnp.concatenate([kr, ones_row * key_bias[:, here]], axis=0)
            k_aug[h, :, here] = k_full.astype(bf16)
            k_nat[h, here, :] = k_full.T.astype(bf16)
            vv = mixed[2 * OWN + h * HD : 2 * OWN + (h + 1) * HD, :]
            v_t[h, :, here] = vv.astype(bf16)
            v_nat[h, here, :] = vv.T.astype(bf16)

    half = tokens // 2

    def attend(item, carry):
        here = pl.ds(pl.multiple_of(item * half, half), half)
        scores = [dot_nn(k_nat[h], q_aug[h, :, here]) for h in range(OWN_HEADS)]
        for h in range(OWN_HEADS):
            peak = jnp.max(scores[h], axis=0, keepdims=True)
            e = jnp.exp(scores[h] - peak)
            total = jnp.sum(e, axis=0, keepdims=True)
            out = dot_nn(v_t[h], (e * (1.0 / total)).astype(bf16))
            logs[h, :, here] = peak + jnp.log(total)
            o_all[h * HD : (h + 1) * HD, here] = out.astype(bf16)
        return carry

    lax.fori_loop(0, 2, attend, 0)
    o_own[...] = o_all[:, 0:half]
    o_oth[...] = o_all[:, half:tokens]


def front(pos, slab_refs, weights, bias, gains, biases, cos, sin, rows, cols):
    tokens = rows.shape[1]
    nh = OWN_HEADS
    outs = (
        sds((tokens, D), bf16),
        sds((3 * OWN, D), bf16),
        sds((OWN, tokens), f32),
        sds((OWN, tokens), f32),
        sds((nh, AUG, tokens), bf16),
        sds((nh, AUG, tokens), bf16),
        sds((nh, tokens, AUG), bf16),
        sds((nh, tokens, HD), bf16),
        sds((nh, 1, tokens), f32),
        sds((OWN, tokens // 2), bf16),
        sds((OWN, tokens // 2), bf16),
    )
    scratch = [
        pltpu.VMEM((3 * OWN + 48, D), bf16),
        pltpu.VMEM((nh, HD, tokens), bf16),
        pltpu.VMEM((OWN, tokens), bf16),
    ]
    return kernel_call(front_kernel, outs, scratch, 1, 15, extra=24)(
        pos, *slab_refs, *weights, bias, gains, biases, cos, sin, rows, cols
    )


def valid_column(pos, sized, first_slot, band_rows, grid_w):
    core, band = pos[0], pos[1]
    slab = band_rows * grid_w
    d = 2 * core + first_slot if first_slot < 2 else 2 - 2 * core + first_slot - 2
    token = lax.broadcasted_iota(jnp.int32, (slab, 1), 0)
    row = lax.bitwise_and(band + 4 - d, 3) * band_rows + token // grid_w
    col = lax.rem(token, grid_w)
    high = sized[slab : slab + 1, 0:1].astype(f32)
    wide = sized[slab + 1 : slab + 2, 0:1].astype(f32)
    return jnp.logical_and(row.astype(f32) < high, col.astype(f32) < wide).astype(f32)


def expand_kernel(
    pos, own_a, own_b, oth_a, oth_b, mine_a, mine_b, far_a, far_b, w0, w1, w2, w3, gains, biases,
    resid_own, att_own, proj_out, e_all, n2, hidden, slope,
    p_all,
):
    core, band, chip = pos[0], pos[1], pos[2]
    half = resid_own.shape[0]
    slab = half // 2
    first = core == 0
    for e, ref in enumerate((w0, w1, w2, w3)):
        quarter = lax.bitwise_xor(chip, e)
        for shard in range(4):
            d = lax.bitwise_xor(band, shard)
            at = jnp.where(quarter < 3, shard * 96 + quarter * 32, D)
            p_all[pl.ds(pl.multiple_of(at, 16), 32), :] = ref[d, 0:32, :]
            at = pl.multiple_of(shard * 192 + quarter * 48, 16)
            e_all[pl.ds(at, 48), :] = ref[d, 32:80, :]
    proj = p_all[0:D, :]
    proj_out[...] = proj
    bias = jnp.concatenate(
        [jnp.where(first, biases[6 + s : 7 + s, 0:192], biases[6 + s : 7 + s, 192:384]) for s in range(4)], axis=1
    )
    for b, src in enumerate((own_a, own_b, oth_a, oth_b)):
        here = slice(b * slab, (b + 1) * slab)
        there = slice((b % 2) * slab, (b % 2 + 1) * slab)
        m, o = (mine_a, far_b) if b < 2 else (mine_b, far_a)
        m, o = m[:, there].astype(f32), o[:, there].astype(f32)
        att = jnp.concatenate([jnp.where(first, m, o), jnp.where(first, o, m)], axis=0).T.astype(bf16)
        res = src[0:slab, :].astype(f32) + dot_nt(att, proj) + biases[5:6, :]
        if b < 2:
            resid_own[here, :] = res
            att_own[here, :] = att
        xhat, _ = norm_rows(res)
        n2[here, :] = (xhat * gains[1:2, :] + biases[1:2, :]).astype(bf16)

    def part(b, carry):
        here = pl.ds(pl.multiple_of(b * slab, slab), slab)
        pre = dot_nt(n2[here, :], e_all[...]) + bias
        cdf = 0.5 * (1.0 + lax.erf(pre * math.sqrt(0.5)))
        hidden[here, :] = (pre * cdf).astype(bf16)
        slope[here, :] = cdf + pre * (jnp.exp(-0.5 * pre * pre) * (1.0 / math.sqrt(2.0 * math.pi)))
        return carry

    lax.fori_loop(0, 4, part, 0)


def expand_layer(pos, slab_refs, att, weights, gains, biases, half):
    v = pltpu.VMEM
    outs = (
        sds((half, D), f32),
        sds((half, D), bf16),
        sds((D, D), bf16),
        sds((FF // 2, D), bf16),
        sds((2 * half, D), bf16),
        sds((2 * half, FF // 2), bf16),
        sds((2 * half, FF // 2), f32),
    )
    return kernel_call(expand_kernel, outs, [v((D + 32, D), bf16)], 1, 14, extra=12)(
        pos, *slab_refs, *att, *weights, gains, biases
    )


def slope_kernel(
    pos, own_a, cot_a, cot_b, cot_c, cot_d, w0, w1, w2, w3, e_all, slope, g16, s_all, dpre, dn_own, dn_send,
    band_rows, grid_w,
):
    core, band, chip = pos[0], pos[1], pos[2]
    slab = band_rows * grid_w
    for e, ref in enumerate((w0, w1, w2, w3)):
        quarter = lax.bitwise_xor(chip, e)
        for shard in range(4):
            at = pl.multiple_of(shard * 192 + quarter * 48, 16)
            s_all[pl.ds(at, 48), :] = ref[lax.bitwise_xor(band, shard)]
    for b, cot in enumerate((cot_a, cot_b, cot_c, cot_d)):
        here = slice(b * slab, (b + 1) * slab)
        g16[here, :] = (cot[...].astype(f32) * valid_column(pos, own_a, b, band_rows, grid_w)).astype(bf16)
    for b in range(4):
        here = slice(b * slab, (b + 1) * slab)
        dpre[here, :] = (dot_nt(g16[here, :], s_all[...]) * slope[here, :]).astype(bf16)
    half = 2 * slab
    dn_send[...] = dot_nn(dpre[half : 2 * half, :], e_all[...]).astype(bf16)
    dn_own[...] = dot_nn(dpre[0:half, :], e_all[...])


def slope_layer(pos, own_a, cots, weights, e_all, slope, band_rows, grid_w):
    half = 2 * band_rows * grid_w
    outs = (
        sds((2 * half, D), bf16),
        sds((FF // 2, D), bf16),
        sds((2 * half, FF // 2), bf16),
        sds((half, D), f32),
        sds((half, D), bf16),
    )
    body = functools.partial(slope_kernel, band_rows=band_rows, grid_w=grid_w)
    return kernel_call(body, outs, (), 1, 11, extra=10)(pos, own_a, *cots, *weights, e_all, slope)


def shrink_kernel(pos, hidden, dpre, g16, n2, s_all, acc_own, acc_send, mine, s1, s2, s3, vec, grads):
    core, chip = pos[0], pos[2]
    half = acc_own.shape[0]
    first = core == 0
    grads[0] = dot_tn(hidden[...], g16[...])
    grads[1] = dot_tn(dpre[...], n2[...])
    for e, ref in ((0, mine), (1, s1), (2, s2), (3, s3)):
        for z in range(4):
            at = pl.ds(pl.multiple_of(z * 192 + lax.bitwise_xor(chip, e) * 48, 16), 48)
            ref[z, 0:48, :] = grads[0, at, :].astype(ref.dtype)
            ref[z, 48:96, :] = grads[1, at, :].astype(ref.dtype)
    for to, at in ((acc_own, 0), (acc_send, half)):
        to[...] = dot_nn(hidden[at : at + half, :], s_all[...]).astype(to.dtype)
    vec[...] = jnp.zeros_like(vec)
    sums = dot_nn(jnp.ones((8, 2 * half), bf16), dpre[...])
    none = jnp.zeros((1, 192), f32)
    for s in range(4):
        x = sums[0:1, s * 192 : (s + 1) * 192]
        vec[8 + s : 9 + s, :] = jnp.where(
            first, jnp.concatenate([x, none], axis=1), jnp.concatenate([none, x], axis=1)
        )
    vec[12:13, :] = jnp.sum(g16[0:half, :].astype(f32), axis=0, keepdims=True)


def shrink_layer(pos, hidden, dpre, g16, n2, s_all):
    half = g16.shape[0] // 2
    outs = (
        sds((half, D), f32),
        sds((half, D), bf16),
        sds((4, 96, D), f32),
        sds((4, 96, D), bf16),
        sds((4, 96, D), bf16),
        sds((4, 96, D), bf16),
        sds((16, D), f32),
    )
    return kernel_call(shrink_kernel, outs, [pltpu.VMEM((2, FF // 2, D), f32)], 1, 5, extra=10)(pos, hidden, dpre, g16, n2, s_all)


def branch_kernel(
    pos, own_a, cot_a, cot_b, resid, att, proj, dn_one, dn_two, gains, vec_in,
    d_residual, d_mine, d_send, p_keep, p_send, vec,
    g_s, dat, grad_p, band_rows, grid_w,
):
    core = pos[0]
    slab = band_rows * grid_w
    for b, cot in enumerate((cot_a, cot_b)):
        here = slice(b * slab, (b + 1) * slab)
        g_s[here, :] = cot[...].astype(f32) * valid_column(pos, own_a, b, band_rows, grid_w)
    vec[...] = vec_in[...]
    xhat, rstd = norm_rows(resid[...])
    dn = dn_one[...] + dn_two[...].astype(f32)
    vec[3:4, :] = jnp.sum(dn, axis=0, keepdims=True)
    vec[1:2, :] = jnp.sum(dn * xhat, axis=0, keepdims=True)
    dx = dn * gains[1:2, :]
    back_x = rstd * (
        dx - jnp.mean(dx, axis=-1, keepdims=True) - xhat * jnp.mean(dx * xhat, axis=-1, keepdims=True)
    )
    d_res = g_s[...] + back_x
    d_residual[...] = d_res
    low = d_res.astype(bf16)
    dat[...] = dot_nn(low, proj[...]).T.astype(bf16)
    d_mine[...] = dat[pl.ds(pl.multiple_of(core * OWN, 16), OWN), :]
    d_send[...] = dat[pl.ds(pl.multiple_of((1 - core) * OWN, 16), OWN), :]
    vec[7:8, :] = jnp.sum(low.astype(f32), axis=0, keepdims=True)
    grad_p[...] = dot_tn(low, att[...])
    p_keep[...] = grad_p[pl.ds(pl.multiple_of(core * OWN, 8), OWN), :]
    p_send[...] = grad_p[pl.ds(pl.multiple_of((1 - core) * OWN, 8), OWN), :].astype(bf16)


def branch(pos, own_a, cots, resid, att, proj, dn_one, dn_two, gains, vec, band_rows, grid_w):
    half = resid.shape[0]
    v = pltpu.VMEM
    outs = (
        sds((half, D), f32),
        sds((OWN, half), bf16),
        sds((OWN, half), bf16),
        sds((OWN, D), f32),
        sds((OWN, D), bf16),
        sds((16, D), f32),
    )
    body = functools.partial(branch_kernel, band_rows=band_rows, grid_w=grid_w)
    return kernel_call(body, outs, [v((half, D), f32), v((D, half), bf16), v((D, D), f32)], 1, 10)(
        pos, own_a, *cots, resid, att, proj, dn_one, dn_two, gains, vec
    )


def scores_kernel(which, q_aug, k_aug, k_nat, v_nat, logs, d_out, *refs):
    before, (dq, dk, dv) = refs[:-3], refs[-3:]
    half = d_out.shape[1]
    here = slice(which * half, (which + 1) * half)
    for h in range(OWN_HEADS):
        q_t = q_aug[h, :, here]
        g = d_out[h * HD : (h + 1) * HD, :]
        p = jnp.exp(dot_nn(k_nat[h], q_t) - logs[h, :, here])
        dp = dot_nn(v_nat[h], g)
        inner = jnp.sum(p * dp, axis=0, keepdims=True)
        ds = (p * (dp - inner)).astype(bf16)
        dv_one = dot_nt(g, p.astype(bf16))
        dk_one = dot_nt(q_t[0:HD, :], ds)
        dq[h] = dot_nn(k_aug[h, 0:HD, :], ds) * 0.125
        dk[h] = dk_one + before[0][h] if before else dk_one
        dv[h] = dv_one + before[1][h] if before else dv_one


def scores_back(which, q_aug, k_aug, k_nat, v_nat, logs, d_out, before=()):
    tokens = q_aug.shape[2]
    outs = (sds((OWN_HEADS, HD, tokens // 2), f32),) + (sds((OWN_HEADS, HD, tokens), f32),) * 2
    return kernel_call(functools.partial(scores_kernel, which), outs, (), 0, 6 + len(before), extra=28)(
        q_aug, k_aug, k_nat, v_nat, logs, d_out, *before
    )


def back_kernel(
    pos, normed, w_own, qrot, krot, dq_a, dq_b, dk, dv, cos, sin, rows, cols, own_a, own_b, oth_a, oth_b,
    qkv_mom, proj_mom, p_keep, p_recv, vec_in, vec_mom,
    out, dn_own, dn_oth,
    dm, dm_full, freq, d_w, d_p, vec,
):
    core, band, group = pos[0], pos[1], pos[3]
    tokens = normed.shape[0]
    half = tokens // 2
    slab = half // 2
    dm_full[...] = jnp.zeros_like(dm_full)
    freq[...] = jnp.zeros_like(freq)
    for h in range(OWN_HEADS):
        c = cos[h * HALF : (h + 1) * HALF, :]
        s = sin[h * HALF : (h + 1) * HALF, :]
        angle = None
        d_query = jnp.concatenate([dq_a[h], dq_b[h]], axis=1)
        for which, source, rotated in ((0, d_query, qrot), (1, dk[h], krot)):
            du = source[0:HALF, :]
            dw = source[HALF:HD, :]
            u = rotated[h * HD : h * HD + HALF, :]
            w = rotated[h * HD + HALF : (h + 1) * HD, :]
            turn = dw * u - du * w
            angle = turn if angle is None else angle + turn
            at = which * OWN + h * HD
            dm[at : at + HD, :] = jnp.concatenate([du * c + dw * s, dw * c - du * s], axis=0).astype(bf16)
        at = pl.multiple_of(core * 96 + h * HALF, 32)
        freq[pl.ds(at, HALF), :] = jnp.sum(angle * rows[...], axis=1, keepdims=True)
        at = pl.multiple_of(192 + core * 96 + h * HALF, 32)
        freq[pl.ds(at, HALF), :] = jnp.sum(angle * cols[...], axis=1, keepdims=True)
        at = 2 * OWN + h * HD
        dm[at : at + HD, :] = dv[h].astype(bf16)
    for t in range(3):
        at = pl.multiple_of(t * D + core * OWN, 16)
        dm_full[pl.ds(at, OWN), :] = dm[t * OWN : (t + 1) * OWN, :]
    d_w[...] = dot_nn(dm[...], normed[...])
    for j in range(3):
        whole = band * 3 + j
        here = jnp.logical_and(lax.rem(whole, 4) // 2 == core, group == 0)
        at = pl.multiple_of(((whole // 4) * 2 + lax.rem(whole, 2)) * 96, 32)

        @pl.when(here)
        def _():
            d_w[pl.ds(at, 96), :] += 0.5 * qkv_mom[j * 96 : (j + 1) * 96, :]

    d_p[...] = p_keep[...] + p_recv[...].astype(f32)

    @pl.when(jnp.logical_and(band // 2 == core, group == 0))
    def _():
        d_p[pl.ds(pl.multiple_of(lax.rem(band, 2) * 96, 32), 96), :] += 0.5 * proj_mom[...]

    vec[...] = vec_in[...] + vec_mom[...]
    sums = dot_nt(jnp.ones((8, tokens), bf16), dm_full[...])
    for t in range(3):
        vec[4 + t : 5 + t, :] += sums[0:1, t * D : (t + 1) * D]
    vec[13:14, :] += jnp.broadcast_to(freq[...], (D, 128)).T[0:1, :]
    for b, src in enumerate((own_a, own_b, oth_a, oth_b)):
        part = dot_tn(dm[:, b * slab : (b + 1) * slab], w_own[...])
        xhat, _ = norm_rows(src[0:slab, :].astype(f32))
        vec[0:1, :] += jnp.sum(part * xhat, axis=0, keepdims=True)
        vec[2:3, :] += jnp.sum(part, axis=0, keepdims=True)
        to, at = (dn_own, b) if b < 2 else (dn_oth, b - 2)
        to[at * slab : (at + 1) * slab, :] = part.astype(to.dtype)
    low = vec[...].astype(bf16)
    for quarter in range(4):
        out[quarter, 0:144, :] = d_w[quarter * 144 : (quarter + 1) * 144, :].astype(bf16)
        out[quarter, 144:192, :] = d_p[quarter * 48 : (quarter + 1) * 48, :].astype(bf16)
        out[quarter, 192:208, :] = low


def back(pos, normed, w_own, qrot, krot, grads, cos, sin, rows, cols, slab_refs, moms, projs, vecs):
    tokens = normed.shape[0]
    half = tokens // 2
    outs = (sds((4, 208, D), bf16), sds((half, D), f32), sds((half, D), bf16))
    v = pltpu.VMEM
    scratch = [
        v((3 * OWN, tokens), bf16),
        v((3 * D, tokens), bf16),
        v((D, 1), f32),
        v((3 * OWN, D), f32),
        v((OWN, D), f32),
        v((16, D), f32),
    ]
    return kernel_call(back_kernel, outs, scratch, 1, 22, extra=10)(
        pos, normed, w_own, qrot, krot, *grads, cos, sin, rows, cols, *slab_refs, *moms, *projs, *vecs
    )


def tail_kernel(
    pos, own_a, own_b, d_residual, dn_one, dn_two, resid, acc_one, acc_two, gains, biases, out_a, out_b, band_rows, grid_w
):
    slab = band_rows * grid_w
    for b, (src, out) in enumerate(((own_a, out_a), (own_b, out_b))):
        here = slice(b * slab, (b + 1) * slab)
        total = resid[here, :] + (acc_one[here, :] + acc_two[here, :].astype(f32)) + biases[10:11, :]
        out[0:slab, :] = (total * valid_column(pos, own_a, b, band_rows, grid_w)).astype(bf16)
        xhat, rstd = norm_rows(src[0:slab, :].astype(f32))
        dx = (dn_one[here, :] + dn_two[here, :].astype(f32)) * gains[0:1, :]
        back_x = rstd * (
            dx - jnp.mean(dx, axis=-1, keepdims=True) - xhat * jnp.mean(dx * xhat, axis=-1, keepdims=True)
        )
        out[slab : 2 * slab, :] = (d_residual[here, :] + back_x).astype(bf16)


def tail(pos, own, d_residual, dn_one, dn_two, resid, acc_one, acc_two, gains, biases, band_rows, grid_w):
    outs = (sds((2 * band_rows * grid_w, D), bf16),) * 2
    body = functools.partial(tail_kernel, band_rows=band_rows, grid_w=grid_w)
    return kernel_call(body, outs, (), 1, 10)(
        pos, *own, d_residual, dn_one, dn_two, resid, acc_one, acc_two, gains, biases
    )


def place_kernel(pos, a, b, block_out, patch_grad):
    band = pos[1]
    slab = block_out.shape[1]
    for which, ref in ((0, a), (1, b)):
        image = lax.rem(band + which, 2)
        block_out[image] = ref[0:slab, :]
        patch_grad[image] = ref[slab : 2 * slab, :].astype(f32)


def place(pos, got):
    slab = got[0].shape[0] // 2
    outs = (sds((2, slab, D), bf16), sds((2, slab, D), f32))
    return kernel_call(place_kernel, outs, (), 1, 2)(pos, *got)


def bands_kernel(pos, mine, r1, r2, r3, own, s1, s2, s3):
    band = pos[1]
    for d, ref in ((0, own), (1, s1), (2, s2), (3, s3)):
        z = lax.bitwise_xor(band, d)
        part = (mine[z] + r1[z].astype(f32)) + (r2[z].astype(f32) + r3[z].astype(f32))
        ref[...] = part.astype(ref.dtype)


def bands(pos, mine, received):
    shape = mine.shape[1:]
    outs = (sds(shape, f32),) + (sds(shape, bf16),) * 3
    return kernel_call(bands_kernel, outs, (), 1, 4)(pos, mine, *received)


def piece_kernel(own, r1, r2, r3, mom, out):
    total = (own[...] + r1[...].astype(f32)) + (r2[...].astype(f32) + r3[...].astype(f32)) + 0.5 * mom[...]
    out[...] = total.astype(bf16)


def piece_sum(own, received, mom):
    return kernel_call(piece_kernel, sds(own.shape, bf16), (), 0, 5)(own, *received, mom)


def sum_four_kernel(x, out):
    total = (x[0].astype(f32) + x[1].astype(f32)) + (x[2].astype(f32) + x[3].astype(f32))
    out[...] = total.astype(bf16)


def sum_four(x):
    return kernel_call(sum_four_kernel, sds(x.shape[1:], bf16), (), 0, 1)(x)


def split_low(x):
    high = x.astype(bf16)
    return high, (x - high.astype(f32)).astype(bf16)


def dot_three_even(a, b):
    left = jnp.concatenate([a[0], a[0], a[1]], axis=1)
    right = jnp.concatenate([b[0], b[1], b[0]], axis=0)
    side = dot_nn(left, right[:, 0:256])
    low = dot_nn(left[256:], right[:, 256:])
    return jnp.concatenate([side, jnp.concatenate([side[256:].T, low], axis=0)], axis=1)


def sweeps(grams):
    row = lax.broadcasted_iota(jnp.int32, (D, D), 0)
    col = lax.broadcasted_iota(jnp.int32, (D, D), 1)
    eye = (row == col).astype(f32)
    scales, current, totals = [], [], [None] * len(grams)
    for gram in grams:
        trace = jnp.sum(jnp.sum(gram * eye, axis=1, keepdims=True), axis=0, keepdims=True)
        scales.append(1.0 / (jnp.sqrt(trace) + 1e-07))
        current.append(gram * (scales[-1] * scales[-1]))
    for sweep in range(5):
        parts = [split_low(a) for a in current]
        polys = [
            coeff_one * eye + coeff_two * a + coeff_three * dot_three_even(a2, a2) for a, a2 in zip(current, parts)
        ]
        halves = [split_low(poly) for poly in polys]
        if sweep < 4:
            turned = [dot_three_even(a2, p2) for a2, p2 in zip(parts, halves)]
        totals = [
            poly if total is None else dot_three_even(split_low(total), p2)
            for total, poly, p2 in zip(totals, polys, halves)
        ]
        if sweep < 4:
            current = [dot_three_even(split_low(t), p2) for t, p2 in zip(turned, halves)]
    return [total * scale for total, scale in zip(totals, scales)]


def gram_kernel(pos, a0, a1, a2, a3, keep, send, band_rows, shrink, expand):
    core, chip = pos[0], pos[2]
    for e, ref in enumerate((a0, a1, a2, a3)):
        for d in range(4):
            at = (e * 4 + d) * 48
            shrink[at : at + 48, :] = ref[d, 0:48, :]
            expand[at : at + 48, :] = ref[d, 48:96, :]
        at = pl.multiple_of(lax.bitwise_xor(chip, e) * 48, 16)
        band_rows[pl.ds(at, 48), :] = ref[0, 0:48, :]
        band_rows[pl.ds(pl.multiple_of(192 + at, 16), 48), :] = ref[0, 48:96, :]
    gram_s, gram_e = dot_tn(shrink[...], shrink[...]), dot_tn(expand[...], expand[...])
    keep[...] = jnp.where(core == 0, gram_s, gram_e)
    send[...] = jnp.where(core == 0, gram_e, gram_s)


def half_grams(pos, parts):
    outs = (sds((D, D), f32), sds((D, D), f32), sds((D, D), bf16))
    return kernel_call(gram_kernel, outs, [pltpu.VMEM((FF // 2, D), bf16)] * 2, 1, 4, extra=10)(pos, *parts)


def muon_kernel(pos, keep, recv, q0, q1, q2, q3, o0, o1, o2, o3, one, two, gram, rows):
    core = pos[0]
    pieces = (q0, q1, q2, q3, o0, o1, o2, o3)

    @pl.when(core == 0)
    def _():
        for e, ref in enumerate(pieces):
            rows[e * 144 : (e + 1) * 144, :] = ref[0:144, :]
        gram[...] = dot_tn(rows[...], rows[...])

    @pl.when(core != 0)
    def _():
        for e, ref in enumerate(pieces):
            rows[e * 48 : (e + 1) * 48, :] = ref[144:192, :]
        gram[...] = dot_tn(rows[0:D, :], rows[0:D, :])

    one[...], two[...] = sweeps([keep[...] + recv[...], gram[...]])


def muon(pos, keep, recv, own_q, oth_q):
    scratch = [pltpu.VMEM((D, D), f32), pltpu.VMEM((3 * D, D), bf16)]
    outs = (sds((D, D), f32),) * 2
    return kernel_call(muon_kernel, outs, scratch, 1, 10, extra=12)(pos, keep, recv, *own_q, *oth_q)


def final_kernel(
    pos, one, one_oth, two, two_oth, band_mine, band_oth, q0, q1, q2, q3, o0, o1, o2, o3,
    qkv_w, proj_w, expand_w, shrink_w,
    qkv_m, qkv_new, proj_m, proj_new, expand_m, expand_new, shrink_m, shrink_new,
    q_mine, q_oth, q_rows,
):
    core, band, chip = pos[0], pos[1], pos[2]
    first = core == 0

    def choose(when_first, a, b):
        return split_low(jnp.where(first == when_first, a[...], b[...]))

    for e in range(4):
        quarter = lax.bitwise_xor(chip, e)
        for refs, to in (((q0, q1, q2, q3), q_mine), ((o0, o1, o2, o3), q_oth)):
            to[pl.ds(pl.multiple_of(quarter * 144, 16), 144), :] = refs[e][0:144, :]
            to[pl.ds(pl.multiple_of(3 * OWN + quarter * 48, 16), 48), :] = refs[e][144:192, :]
    for j in range(4):
        whole = band * 3 + j
        at = pl.multiple_of(((whole // 4) * 2 + lax.rem(whole, 2)) * 96, 32)
        mine = lax.rem(whole, 4) // 2 == core
        if j == 3:
            at = pl.multiple_of(3 * OWN + lax.rem(band, 2) * 96, 32)
            mine = band // 2 == core

        @pl.when(mine)
        def _():
            q_rows[j * 96 : (j + 1) * 96, :] = q_mine[pl.ds(at, 96), :]

        @pl.when(jnp.logical_not(mine))
        def _():
            q_rows[j * 96 : (j + 1) * 96, :] = q_oth[pl.ds(at, 96), :]

    b_mine, b_oth = band_mine[...].astype(f32), band_oth[...].astype(f32)
    low_core, high_core = jnp.where(first, b_mine, b_oth), jnp.where(first, b_oth, b_mine)
    m_shrink = jnp.concatenate([low_core[0:192], high_core[0:192]], axis=0)
    m_expand = jnp.concatenate([low_core[192:], high_core[192:]], axis=0)
    t_shrink, t_expand = choose(True, one, one_oth), choose(False, one, one_oth)
    t_qkv, t_proj = choose(True, two, two_oth), choose(False, two, two_oth)
    for w, t, low, mom, new, size in (
        (qkv_w, t_qkv, q_rows[0:288, :], qkv_m, qkv_new, 3 * D),
        (proj_w, t_proj, q_rows[288:D, :], proj_m, proj_new, D),
        (shrink_w, t_shrink, m_shrink.astype(bf16), shrink_m, shrink_new, FF),
    ):
        mom[...] = low.astype(f32)
        new[...] = w[...] - 0.05 * math.sqrt(size) * (dot_nn(low, t[0]) + dot_nn(low, t[1]))
    low = m_expand.astype(bf16)
    expand_m[...] = m_expand.T
    expand_new[...] = expand_w[...] - 0.05 * math.sqrt(FF) * (dot_nt(t_expand[0], low) + dot_nt(t_expand[1], low))


def final(pos, one, one_oth, two, two_oth, band_mine, band_oth, own_q, oth_q, *weights):
    outs = []
    for w in weights:
        outs += [sds(w.shape, f32)] * 2
    v = pltpu.VMEM
    scratch = [v((4 * OWN, D), bf16), v((4 * OWN, D), bf16), v((D, D), bf16)]
    return kernel_call(final_kernel, tuple(outs), scratch, 1, 18, extra=10)(
        pos, one, one_oth, two, two_oth, band_mine, band_oth, *own_q, *oth_q, *weights
    )


def flip(x, bit):
    n = lax.axis_size("batch")
    return lax.ppermute(x, "batch", [(i, i ^ bit) for i in range(n)])


def swap_bands(x, d):
    return lax.ppermute(x, "rows", [(i, i ^ d) for i in range(4)])


def moves(which):
    pairs = []
    for k in range(lax.axis_size("batch") // 2):
        for c in range(2):
            for i in range(4):
                band = (i - 2 * c - which) % 4
                pairs.append(((2 * k + i // 2) * 4 + band, (2 * k + c) * 4 + i))
    return pairs


def to_image(parts):
    return [lax.ppermute(parts[which], AXES, moves(which)) for which in range(2)]


def from_image(part, which):
    return lax.ppermute(part, AXES, [(b, a) for a, b in moves(which)])


def other_chips(x):
    bit = 8
    while bit < lax.axis_size("batch"):
        x = x + flip(x.astype(f32), bit).astype(x.dtype)
        bit *= 2
    return x


def over_chips(x):
    return [flip(x, 2 * e) for e in range(1, 4)]


def over_bands(x):
    return [swap_bands(x, d) for d in range(1, 4)]


def local(
    patches,
    cotangent,
    heights,
    widths,
    qkv_weight,
    qkv_moment,
    proj_weight,
    proj_moment,
    expand_weight,
    expand_moment,
    shrink_weight,
    shrink_moment,
    norm_gains,
    gains_moment,
    all_biases,
    biases_moment,
    frequencies,
    freq_moment,
):
    images, band_rows, grid_w, _ = patches.shape
    slab = band_rows * grid_w
    batch = lax.axis_index("batch")
    band = lax.axis_index("rows")
    core = batch % 2
    chip = (batch // 2) % 4
    pos = jnp.stack([core, band, chip, batch // 2]).astype(jnp.int32)
    grid = (band_rows, grid_w)

    share = own_weights(pos, qkv_weight.T, proj_weight.T, expand_weight, shrink_weight)
    shares = over_bands(share)
    p_a, p_b, c_a, c_b = slabs(
        pos, heights, widths, patches.reshape(images, slab, D), cotangent.reshape(images, slab, D)
    )
    own = to_image((p_a, p_b))
    oth = [flip(x, 1) for x in own]
    biases = all_biases.reshape(-1, D)
    freq_own = lax.dynamic_slice_in_dim(frequencies.T, core * 96, 96, 0)
    cos, sin, rows_tok, cols_tok, bias_own, mom_big = setup(
        pos, freq_own, biases, expand_moment, shrink_moment, 4 * slab, *grid
    )
    n_bias = all_biases.shape[0]

    def placed(shape, part, axis):
        return lax.dynamic_update_slice_in_dim(
            jnp.zeros(shape, f32), part, band * (shape[axis] // 4), axis
        ).reshape(-1)

    vec_mom = jnp.concatenate(
        [
            placed((2, D), gains_moment, 1),
            placed((n_bias,), biases_moment, 0),
            placed((2, H * HALF), freq_moment, 1),
            jnp.zeros((2 * D,), f32),
        ]
    ).reshape(16, D)
    vec_mom = jnp.where(batch == 0, 0.5 * vec_mom, 0.0)
    shares, cos, vec_mom = lax.optimization_barrier((shares, cos, vec_mom))
    w_qkv, w_first, w_second = pack(share, shares)
    w_qkv = [w_qkv] + over_chips(w_qkv)
    w_first, oth = lax.optimization_barrier((w_first, oth))
    w_first = [w_first] + over_chips(w_first)
    c_a, c_b, w_second, w_qkv = lax.optimization_barrier((c_a, c_b, w_second, w_qkv))
    cot = to_image((c_a, c_b))
    w_second = [w_second] + over_chips(w_second)

    normed, w_own, qrot, krot, q_aug, k_aug, k_nat, v_nat, logs, *o_mine = front(
        pos, own + oth, w_qkv, bias_own, norm_gains, biases, cos, sin, rows_tok, cols_tok
    )
    o_oth = [flip(x, 1) for x in o_mine]
    cot, o_mine = lax.optimization_barrier((cot, o_mine))
    cot = cot + [flip(x, 1) for x in cot]
    resid, att, proj16, e_all, n2, hidden, slope = expand_layer(
        pos, own + oth, (*o_mine, *o_oth), w_first, norm_gains, biases, 2 * slab
    )
    g16, s_all, dpre, dn_two, dn_two_send = slope_layer(pos, own[0], cot, w_second, e_all, slope, *grid)
    dn_two_recv = flip(dn_two_send, 1)
    acc_own, acc_send, big, b1, b2, b3, vec = shrink_layer(pos, hidden, dpre, g16, n2, s_all)
    big_chips = [flip(x, 2 * e) for e, x in zip((1, 2, 3), (b1, b2, b3))]
    d_residual, d_mine, d_send, p_keep, p_send, vec = branch(
        pos, own[0], cot[:2], resid, att, proj16, dn_two, dn_two_recv, norm_gains, vec, *grid
    )
    d_recv = flip(d_send, 1)
    p_recv = flip(p_send, 1)
    dq_a, dk, dv = scores_back(0, q_aug, k_aug, k_nat, v_nat, logs, d_mine)
    acc_recv = flip(acc_send, 1)
    dq_b, dk, dv = scores_back(1, q_aug, k_aug, k_nat, v_nat, logs, d_recv, (dk, dv))

    big, dq_b = lax.optimization_barrier((big, dq_b))
    own_big, *to_bands = bands(pos, other_chips(big), big_chips)
    to_bands, dq_b, acc_recv = lax.optimization_barrier((to_bands, dq_b, acc_recv))
    from_bands = [swap_bands(x, d) for d, x in zip((1, 2, 3), to_bands)]
    q_parts, dn_own, dn_oth = back(
        pos, normed, w_own, qrot, krot, (dq_a, dq_b, dk, dv), cos, sin, rows_tok, cols_tok, own + oth,
        (qkv_moment.T, proj_moment.T), (p_keep, p_recv), (vec, vec_mom),
    )
    dn_recv = flip(dn_oth, 1)
    big_piece = piece_sum(own_big, from_bands, mom_big)
    q_parts, big_piece = lax.optimization_barrier((q_parts, big_piece))

    chips = [[8 * g + 2 * q + c for q in range(4)] for g in range(lax.axis_size("batch") // 8) for c in range(2)]
    q_low = other_chips(sum_four(lax.all_to_all(q_parts, "batch", 0, 0, axis_index_groups=chips, tiled=True)))
    big_bands = jnp.stack([big_piece] + over_bands(big_piece))
    results = tail(pos, own, d_residual, dn_own, dn_recv, resid, acc_own, acc_recv, norm_gains, biases, *grid)
    big_bands, q_low, results = lax.optimization_barrier((big_bands, q_low, results))
    big_all = [big_bands] + over_chips(big_bands)
    q_piece = sum_four(lax.all_gather(q_low, "rows", axis=0))
    own_q = [q_piece] + over_chips(q_piece)
    oth_q = [flip(x, 1) for x in own_q]

    gram_keep, gram_send, band_mine = half_grams(pos, big_all)
    image_a, image_b = from_image(results[0], 0), from_image(results[1], 1)
    one, two = muon(pos, gram_keep, flip(gram_send, 1), own_q, oth_q)
    one_oth, band_oth, two_oth = flip(one, 1), flip(band_mine, 1), flip(two, 1)
    two_oth, image_a, image_b = lax.optimization_barrier((two_oth, image_a, image_b))
    block_out, patch_grad = place(pos, (image_a, image_b))
    shape = (images, band_rows, grid_w, D)
    block_out, patch_grad = block_out.reshape(shape), patch_grad.reshape(shape)
    new = final(
        pos, one, one_oth, two, two_oth, band_mine, band_oth, own_q, oth_q,
        qkv_weight.T, proj_weight.T, expand_weight, shrink_weight,
    )
    new = [x.T for x in new[:4]] + list(new[4:])

    vec = (own_q[0][-16:].astype(f32) + oth_q[0][-16:].astype(f32)).reshape(-1)

    def vector_step(values, new, axis):
        stepped = values - 0.2 * new * lax.rsqrt(jnp.mean(new * new) + 1e-06)
        size_one = new.shape[axis] // 4
        return (
            lax.dynamic_slice_in_dim(new, band * size_one, size_one, axis),
            lax.dynamic_slice_in_dim(stepped, band * size_one, size_one, axis),
        )

    vectors = (
        vector_step(norm_gains, vec[: 2 * D].reshape(2, D), 1)
        + vector_step(all_biases, vec[2 * D : 2 * D + n_bias], 0)
        + vector_step(frequencies, vec[2 * D + n_bias : 2 * D + n_bias + H * HD].reshape(2, H * HALF), 1)
    )
    return (block_out, patch_grad) + tuple(new) + vectors


def solution(mesh):
    image = P("batch", "rows", None, None)
    cols, rows = P(None, "rows"), P("rows", None)
    return jax.shard_map(
        local,
        mesh=mesh,
        in_specs=(
            image, image, P("batch"), P("batch"), cols, cols, cols, cols, cols, cols, rows, rows,
            P(), cols, P(), P("rows"), P(), cols,
        ),
        out_specs=(
            image, image, cols, cols, cols, cols, cols, cols, rows, rows, cols, cols, P("rows"), P("rows"), cols, cols,
        ),
        check_vma=False,
    )
```

```python
import functools
import math

import jax
import jax.numpy as jnp
from jax import lax
from jax.experimental import pallas as pl
from jax.experimental.pallas import tpu as pltpu
from jax.sharding import PartitionSpec as P

D = 384
H = 6
HD = 64
FF = 1536
HALF = HD // 2
OWN_HEADS = H // 2
OWN = OWN_HEADS * HD
AUG = HD + 16

coeff_one = 3.4445
coeff_two = -4.775
coeff_three = 2.0315

bf16 = jnp.bfloat16
f32 = jnp.float32
AXES = ("batch", "rows")


def dot_nn(a, b):
    return lax.dot_general(a, b, (((1,), (0,)), ((), ())), preferred_element_type=f32)


def dot_nt(a, b):
    return lax.dot_general(a, b, (((1,), (1,)), ((), ())), preferred_element_type=f32)


def dot_tn(a, b):
    return lax.dot_general(a, b, (((0,), (0,)), ((), ())), preferred_element_type=f32)


def vmem_bytes(x):
    *lead, rows, lanes = (1,) * max(0, 2 - len(x.shape)) + tuple(x.shape)
    size = jnp.dtype(x.dtype).itemsize
    tile = 8 * 4 // size
    return math.prod(lead) * (-(-rows // tile) * tile) * (-(-lanes // 128) * 128) * size


def kernel_call(body, out_shape, scratch=(), smem=0, n_in=0, extra=4, cost=None):
    specs = [pl.BlockSpec(memory_space=pltpu.SMEM)] * smem
    specs += [pl.BlockSpec(memory_space=pltpu.VMEM)] * n_in

    def call(*args):
        held = list(args[smem:]) + jax.tree.leaves(out_shape) + [s for s in scratch]
        limit = sum(vmem_bytes(x) for x in held) + extra * 2**20
        return pl.pallas_call(
            body,
            out_shape=out_shape,
            in_specs=specs,
            out_specs=jax.tree.map(lambda _: pl.BlockSpec(memory_space=pltpu.VMEM), out_shape),
            scratch_shapes=list(scratch),
            compiler_params=pltpu.CompilerParams(vmem_limit_bytes=int(limit)),
            cost_estimate=cost and pl.CostEstimate(flops=cost, bytes_accessed=0, transcendentals=0),
        )(*args)

    return call


def sds(shape, dtype):
    return jax.ShapeDtypeStruct(shape, dtype)


def norm_rows(x):
    centered = x - jnp.mean(x, axis=-1, keepdims=True)
    rstd = lax.rsqrt(jnp.mean(centered * centered, axis=-1, keepdims=True) + 1e-06)
    return centered * rstd, rstd


def weights_kernel(pos, qkv_t, proj_t, expand, shrink, out, q_s, p_s, e_s, s_s, sem_q, sem_p, sem_e, sem_s):
    core, band, chip = pos[0], pos[1], pos[2]
    start = jnp.where(core == 0, jnp.where(band < 3, 2 * band, 0), jnp.where(band == 0, 4, jnp.where(band == 3, 2, 0)))
    count = jnp.where((core == 0) == (band < 2), 4, 2)
    at_q = pl.multiple_of((start + jnp.minimum(chip, count - 1)) * 48, 8)
    at_p = pl.multiple_of(jnp.minimum(chip, 2) * 32, 8)
    at = pl.multiple_of(core * 192 + chip * 48, 8)
    copies = (
        pltpu.make_async_copy(expand, e_s, sem_e),
        pltpu.make_async_copy(qkv_t.at[pl.ds(at_q, 48), :], q_s, sem_q),
        pltpu.make_async_copy(proj_t.at[pl.ds(at_p, 32), :], p_s, sem_p),
        pltpu.make_async_copy(shrink.at[pl.ds(at, 48), :], s_s, sem_s),
    )
    for copy in copies:
        copy.start()
    for copy in copies[1:]:
        copy.wait()
    out[0:48, :] = q_s[...].astype(bf16)
    out[48:80, :] = p_s[...].astype(bf16)
    out[128:176, :] = s_s[...].astype(bf16)
    copies[0].wait()
    e_s[...] = e_s[...].T
    out[80:128, :] = e_s[pl.ds(at, 48), :].astype(bf16)


def own_weights(pos, qkv_t, proj_t, expand, shrink):
    v = pltpu.VMEM
    dma = pltpu.SemaphoreType.DMA
    scratch = [v((48, D), f32), v((32, D), f32), v((D, D), f32), v((48, D), f32), dma, dma, dma, dma]
    hbm = pl.BlockSpec(memory_space=pltpu.HBM)
    return pl.pallas_call(
        weights_kernel,
        out_shape=sds((176, D), bf16),
        in_specs=[pl.BlockSpec(memory_space=pltpu.SMEM)] + [hbm] * 4,
        out_specs=pl.BlockSpec(memory_space=pltpu.VMEM),
        scratch_shapes=scratch,
        compiler_params=pltpu.CompilerParams(vmem_limit_bytes=56 * 2**20),
    )(pos, qkv_t, proj_t, expand, shrink)


def slabs_kernel(pos, heights, widths, patches, cot, p_a, p_b, c_a, c_b):
    band = pos[1]
    slab = patches.shape[1]
    row = lax.broadcasted_iota(jnp.int32, (16, D), 0)
    for which, (p, c) in enumerate(((p_a, c_a), (p_b, c_b))):
        image = lax.rem(band + which, 2)
        p[0:slab, :] = patches[image]
        size = jnp.where(row == 0, heights[image], widths[image])
        p[slab : slab + 16, :] = size.astype(f32).astype(bf16)
        c[...] = cot[image]


def slabs(pos, heights, widths, patches, cot):
    slab = patches.shape[1]
    outs = (sds((slab + 16, D), bf16),) * 2 + (sds((slab, D), bf16),) * 2
    return kernel_call(slabs_kernel, outs, (), 3, 2)(pos, heights, widths, patches, cot)


def setup_kernel(
    pos, freq, biases, expand_mom, shrink_mom, gains_mom, biases_mom, freq_mom,
    cos, sin, rows, cols, bias_own, mom_big, vec,
    column, turned, freq_one, freq_two, band_rows, grid_w,
):
    core, band, chip, group = pos[0], pos[1], pos[2], pos[3]
    tokens = rows.shape[1]
    slab = band_rows * grid_w
    token = lax.broadcasted_iota(jnp.int32, (1, tokens), 1)
    slot = token // slab
    d = jnp.where(slot < 2, 2 * core + slot, 2 - 2 * core + slot - 2)
    row = lax.bitwise_and(band + 4 - d, 3) * band_rows + lax.rem(token, slab) // grid_w
    rows[...] = row.astype(f32)
    cols[...] = lax.rem(token, grid_w).astype(f32)
    own = pl.ds(pl.multiple_of(core * 96, 8), 96)
    freq_one[...] = jnp.broadcast_to(freq[0:1, :], (128, H * HALF)).T
    freq_two[...] = jnp.broadcast_to(freq[1:2, :], (128, H * HALF)).T
    angle = freq_one[own, 0:1] * rows[...] + freq_two[own, 0:1] * cols[...]
    cos[...] = jnp.cos(angle)
    sin[...] = jnp.sin(angle)
    for t in range(3):
        column[...] = jnp.broadcast_to(biases[2 + t : 3 + t, :], (128, D)).T
        at = pl.multiple_of(core * OWN, 8)
        bias_own[t * OWN : (t + 1) * OWN, :] = column[pl.ds(at, OWN), 0:1]
    at = pl.multiple_of(core * 192 + chip * 48, 8)
    mom_big[0:48, :] = shrink_mom[pl.ds(at, 48), :]
    turned[...] = expand_mom[...].T
    mom_big[48:96, :] = turned[pl.ds(at, 48), :]
    share = jnp.where(jnp.logical_and(core == 0, group == 0), 0.5, 0.0)
    vec[...] = jnp.zeros_like(vec)
    none = jnp.zeros((8, 144), f32)

    def wide(x, lanes):
        return jnp.concatenate([x, jnp.zeros((x.shape[0], lanes), f32)], axis=1)

    gains = jnp.concatenate([wide(gains_mom[...], 288), jnp.zeros((6, D), f32)], axis=0)
    vec[0:2, :] = share * pltpu.roll(gains, 96 * band, 1)[0:2, :]
    freqs = jnp.concatenate([freq_mom[0:1, :], none[0:1], freq_mom[1:2, :], none[0:1]], axis=1)
    vec[13:14, :] = share * pltpu.roll(jnp.broadcast_to(freqs, (8, D)), 48 * band, 1)[0:1, :]
    for i in range(11):
        block = 11 * band + i
        line = jnp.broadcast_to(wide(biases_mom[i : i + 1, :], 288), (8, D))
        vec[pl.ds(2 + block // 4, 1), :] += share * pltpu.roll(line, 96 * lax.rem(block, 4), 1)[0:1, :]


def setup(pos, freq, biases, expand_mom, shrink_mom, gains_mom, biases_mom, freq_mom, tokens, band_rows, grid_w):
    v = pltpu.VMEM
    outs = (
        sds((96, tokens), f32),
        sds((96, tokens), f32),
        sds((1, tokens), f32),
        sds((1, tokens), f32),
        sds((3 * OWN, 1), f32),
        sds((96, D), f32),
        sds((16, D), f32),
    )
    scratch = [v((D, 128), f32), v((D, D), f32), v((H * HALF, 128), f32), v((H * HALF, 128), f32)]
    body = functools.partial(setup_kernel, band_rows=band_rows, grid_w=grid_w)
    return kernel_call(body, outs, scratch, 1, 7)(
        pos, freq, biases, expand_mom, shrink_mom, gains_mom, biases_mom, freq_mom
    )


def pack_kernel(own, r1, r2, r3, qkv, first, second):
    for d, ref in enumerate((own, r1, r2, r3)):
        qkv[d] = ref[0:48, :]
        first[d] = ref[48:128, :]
        second[d] = ref[128:176, :]


def pack(own, received):
    outs = (sds((4, 48, D), bf16), sds((4, 80, D), bf16), sds((4, 48, D), bf16))
    return kernel_call(pack_kernel, outs, (), 0, 4)(own, *received)


def front_kernel(
    pos, own_a, own_b, oth_a, oth_b, w0, w1, w2, w3, bias, gains, biases, cos, sin, rows, cols,
    normed, w_own, qrot, krot, q_aug, k_aug, k_nat, v_nat, logs, o_own, o_oth,
    w_all, v_t, o_all,
):
    core, band, chip = pos[0], pos[1], pos[2]
    tokens = normed.shape[0]
    block = tokens // 4
    for e, ref in enumerate((w0, w1, w2, w3)):
        quarter = lax.bitwise_xor(chip, e)
        for shard in range(4):
            base = jnp.where(core == 0, (0, 4, 8, 10)[shard], (0, 2, 4, 8)[shard])
            count = jnp.where(core == 0, (4, 4, 2, 2)[shard], (2, 2, 4, 4)[shard])
            at = jnp.where(quarter < count, base + quarter, 12)
            w_all[pl.ds(pl.multiple_of(at * 48, 16), 48), :] = ref[lax.bitwise_xor(band, shard)]
    w_own[...] = w_all[0 : 3 * OWN, :]
    for b, src in enumerate((own_a, own_b, oth_a, oth_b)):
        xhat, _ = norm_rows(src[0:block, :].astype(f32))
        normed[b * block : (b + 1) * block, :] = (xhat * gains[0:1, :] + biases[0:1, :]).astype(bf16)
    high = own_a[block : block + 1, 0:1].astype(f32)
    wide = own_a[block + 1 : block + 2, 0:1].astype(f32)
    inside = jnp.logical_and(rows[...] < high, cols[...] < wide)
    key_bias = jnp.where(inside, 0.0, -1e9).astype(f32)
    ones_row = (lax.broadcasted_iota(jnp.int32, (AUG - HD, block), 0) == 0).astype(f32)
    for b in range(4):
        here = slice(b * block, (b + 1) * block)
        mixed = dot_nt(w_own[...], normed[here, :]) + bias[...]
        for h in range(OWN_HEADS):
            c = cos[h * HALF : (h + 1) * HALF, here]
            s = sin[h * HALF : (h + 1) * HALF, here]
            qu = mixed[h * HD : h * HD + HALF, :]
            qw = mixed[h * HD + HALF : (h + 1) * HD, :]
            ku = mixed[OWN + h * HD : OWN + h * HD + HALF, :]
            kw = mixed[OWN + h * HD + HALF : OWN + (h + 1) * HD, :]
            qr = jnp.concatenate([qu * c - qw * s, qw * c + qu * s], axis=0)
            kr = jnp.concatenate([ku * c - kw * s, kw * c + ku * s], axis=0)
            qrot[h * HD : (h + 1) * HD, here] = qr
            krot[h * HD : (h + 1) * HD, here] = kr
            q_low = qr.astype(bf16).astype(f32) * 0.125
            q_aug[h, :, here] = jnp.concatenate([q_low, ones_row], axis=0).astype(bf16)
            k_full = jnp.concatenate([kr, ones_row * key_bias[:, here]], axis=0)
            k_aug[h, :, here] = k_full.astype(bf16)
            k_nat[h, here, :] = k_full.T.astype(bf16)
            vv = mixed[2 * OWN + h * HD : 2 * OWN + (h + 1) * HD, :]
            v_t[h, :, here] = vv.astype(bf16)
            v_nat[h, here, :] = vv.T.astype(bf16)

    half = tokens // 2

    def attend(item, carry):
        here = pl.ds(pl.multiple_of(item * half, half), half)
        scores = [dot_nn(k_nat[h], q_aug[h, :, here]) for h in range(OWN_HEADS)]
        for h in range(OWN_HEADS):
            peak = jnp.max(scores[h], axis=0, keepdims=True)
            e = jnp.exp(scores[h] - peak)
            total = jnp.sum(e, axis=0, keepdims=True)
            out = dot_nn(v_t[h], (e * (1.0 / total)).astype(bf16))
            logs[h, :, here] = peak + jnp.log(total)
            o_all[h * HD : (h + 1) * HD, here] = out.astype(bf16)
        return carry

    lax.fori_loop(0, 2, attend, 0)
    o_own[...] = o_all[:, 0:half]
    o_oth[...] = o_all[:, half:tokens]


def front(pos, slab_refs, weights, bias, gains, biases, cos, sin, rows, cols):
    tokens = rows.shape[1]
    nh = OWN_HEADS
    outs = (
        sds((tokens, D), bf16),
        sds((3 * OWN, D), bf16),
        sds((OWN, tokens), f32),
        sds((OWN, tokens), f32),
        sds((nh, AUG, tokens), bf16),
        sds((nh, AUG, tokens), bf16),
        sds((nh, tokens, AUG), bf16),
        sds((nh, tokens, HD), bf16),
        sds((nh, 1, tokens), f32),
        sds((OWN, tokens // 2), bf16),
        sds((OWN, tokens // 2), bf16),
    )
    scratch = [
        pltpu.VMEM((3 * OWN + 48, D), bf16),
        pltpu.VMEM((nh, HD, tokens), bf16),
        pltpu.VMEM((OWN, tokens), bf16),
    ]
    return kernel_call(front_kernel, outs, scratch, 1, 15, extra=24)(
        pos, *slab_refs, *weights, bias, gains, biases, cos, sin, rows, cols
    )


def valid_column(pos, sized, first_slot, band_rows, grid_w):
    core, band = pos[0], pos[1]
    slab = band_rows * grid_w
    d = 2 * core + first_slot if first_slot < 2 else 2 - 2 * core + first_slot - 2
    token = lax.broadcasted_iota(jnp.int32, (slab, 1), 0)
    row = lax.bitwise_and(band + 4 - d, 3) * band_rows + token // grid_w
    col = lax.rem(token, grid_w)
    high = sized[slab : slab + 1, 0:1].astype(f32)
    wide = sized[slab + 1 : slab + 2, 0:1].astype(f32)
    return jnp.logical_and(row.astype(f32) < high, col.astype(f32) < wide).astype(f32)


def expand_kernel(
    pos, own_a, own_b, oth_a, oth_b, mine_a, mine_b, far_a, far_b, w0, w1, w2, w3, gains, biases,
    resid_own, att_own, proj_out, e_all, n2, hidden, slope,
    p_all,
):
    core, band, chip = pos[0], pos[1], pos[2]
    half = resid_own.shape[0]
    slab = half // 2
    first = core == 0
    for e, ref in enumerate((w0, w1, w2, w3)):
        quarter = lax.bitwise_xor(chip, e)
        for shard in range(4):
            d = lax.bitwise_xor(band, shard)
            at = jnp.where(quarter < 3, shard * 96 + quarter * 32, D)
            p_all[pl.ds(pl.multiple_of(at, 16), 32), :] = ref[d, 0:32, :]
            at = pl.multiple_of(shard * 192 + quarter * 48, 16)
            e_all[pl.ds(at, 48), :] = ref[d, 32:80, :]
    proj = p_all[0:D, :]
    proj_out[...] = proj
    bias = jnp.concatenate(
        [jnp.where(first, biases[6 + s : 7 + s, 0:192], biases[6 + s : 7 + s, 192:384]) for s in range(4)], axis=1
    )
    for b, src in enumerate((own_a, own_b, oth_a, oth_b)):
        here = slice(b * slab, (b + 1) * slab)
        there = slice((b % 2) * slab, (b % 2 + 1) * slab)
        m, o = (mine_a, far_b) if b < 2 else (mine_b, far_a)
        m, o = m[:, there].astype(f32), o[:, there].astype(f32)
        att = jnp.concatenate([jnp.where(first, m, o), jnp.where(first, o, m)], axis=0).T.astype(bf16)
        res = src[0:slab, :].astype(f32) + dot_nt(att, proj) + biases[5:6, :]
        if b < 2:
            resid_own[here, :] = res
            att_own[here, :] = att
        xhat, _ = norm_rows(res)
        n2[here, :] = (xhat * gains[1:2, :] + biases[1:2, :]).astype(bf16)

    def part(b, carry):
        here = pl.ds(pl.multiple_of(b * slab, slab), slab)
        pre = dot_nt(n2[here, :], e_all[...]) + bias
        cdf = 0.5 * (1.0 + lax.erf(pre * math.sqrt(0.5)))
        hidden[here, :] = (pre * cdf).astype(bf16)
        slope[here, :] = cdf + pre * (jnp.exp(-0.5 * pre * pre) * (1.0 / math.sqrt(2.0 * math.pi)))
        return carry

    lax.fori_loop(0, 4, part, 0)


def expand_layer(pos, slab_refs, att, weights, gains, biases, half):
    v = pltpu.VMEM
    outs = (
        sds((half, D), f32),
        sds((half, D), bf16),
        sds((D, D), bf16),
        sds((FF // 2, D), bf16),
        sds((2 * half, D), bf16),
        sds((2 * half, FF // 2), bf16),
        sds((2 * half, FF // 2), f32),
    )
    return kernel_call(expand_kernel, outs, [v((D + 32, D), bf16)], 1, 14, extra=12)(
        pos, *slab_refs, *att, *weights, gains, biases
    )


def slope_kernel(
    pos, own_a, cot_a, cot_b, cot_c, cot_d, w0, w1, w2, w3, e_all, slope, g16, s_all, dpre, dn_own, dn_send,
    band_rows, grid_w,
):
    core, band, chip = pos[0], pos[1], pos[2]
    slab = band_rows * grid_w
    for e, ref in enumerate((w0, w1, w2, w3)):
        quarter = lax.bitwise_xor(chip, e)
        for shard in range(4):
            at = pl.multiple_of(shard * 192 + quarter * 48, 16)
            s_all[pl.ds(at, 48), :] = ref[lax.bitwise_xor(band, shard)]
    for b, cot in enumerate((cot_a, cot_b, cot_c, cot_d)):
        here = slice(b * slab, (b + 1) * slab)
        g16[here, :] = (cot[...].astype(f32) * valid_column(pos, own_a, b, band_rows, grid_w)).astype(bf16)
    for b in range(4):
        here = slice(b * slab, (b + 1) * slab)
        dpre[here, :] = (dot_nt(g16[here, :], s_all[...]) * slope[here, :]).astype(bf16)
    half = 2 * slab
    dn_send[...] = dot_nn(dpre[half : 2 * half, :], e_all[...]).astype(bf16)
    dn_own[...] = dot_nn(dpre[0:half, :], e_all[...])


def slope_layer(pos, own_a, cots, weights, e_all, slope, band_rows, grid_w):
    half = 2 * band_rows * grid_w
    outs = (
        sds((2 * half, D), bf16),
        sds((FF // 2, D), bf16),
        sds((2 * half, FF // 2), bf16),
        sds((half, D), f32),
        sds((half, D), bf16),
    )
    body = functools.partial(slope_kernel, band_rows=band_rows, grid_w=grid_w)
    return kernel_call(body, outs, (), 1, 11, extra=10)(pos, own_a, *cots, *weights, e_all, slope)


def shrink_kernel(pos, hidden, dpre, g16, n2, s_all, resid, biases, base, acc_send, mine, s1, s2, s3, vec, grads):
    core, chip = pos[0], pos[2]
    half = base.shape[0]
    first = core == 0
    grads[0] = dot_tn(hidden[...], g16[...])
    grads[1] = dot_tn(dpre[...], n2[...])
    for e, ref in ((0, mine), (1, s1), (2, s2), (3, s3)):
        for z in range(4):
            at = pl.ds(pl.multiple_of(z * 192 + lax.bitwise_xor(chip, e) * 48, 16), 48)
            ref[z, 0:48, :] = grads[0, at, :].astype(ref.dtype)
            ref[z, 48:96, :] = grads[1, at, :].astype(ref.dtype)
    base[...] = resid[...] + dot_nn(hidden[0:half, :], s_all[...]) + biases[10:11, :]
    acc_send[...] = dot_nn(hidden[half : 2 * half, :], s_all[...]).astype(bf16)
    vec[...] = jnp.zeros_like(vec)
    sums = dot_nn(jnp.ones((8, 2 * half), bf16), dpre[...])
    none = jnp.zeros((1, 192), f32)
    for s in range(4):
        x = sums[0:1, s * 192 : (s + 1) * 192]
        vec[8 + s : 9 + s, :] = jnp.where(
            first, jnp.concatenate([x, none], axis=1), jnp.concatenate([none, x], axis=1)
        )
    vec[12:13, :] = jnp.sum(g16[0:half, :].astype(f32), axis=0, keepdims=True)


def shrink_layer(pos, hidden, dpre, g16, n2, s_all, resid, biases):
    half = g16.shape[0] // 2
    outs = (
        sds((half, D), f32),
        sds((half, D), bf16),
        sds((4, 96, D), f32),
        sds((4, 96, D), bf16),
        sds((4, 96, D), bf16),
        sds((4, 96, D), bf16),
        sds((16, D), f32),
    )
    return kernel_call(shrink_kernel, outs, [pltpu.VMEM((2, FF // 2, D), f32)], 1, 7, extra=10)(
        pos, hidden, dpre, g16, n2, s_all, resid, biases
    )


def branch_kernel(
    pos, own_a, cot_a, cot_b, resid, att, proj, dn_one, dn_two, gains, vec_in,
    d_residual, d_mine, d_send, p_keep, p_send, vec,
    g_s, dat, grad_p, band_rows, grid_w,
):
    core = pos[0]
    slab = band_rows * grid_w
    for b, cot in enumerate((cot_a, cot_b)):
        here = slice(b * slab, (b + 1) * slab)
        g_s[here, :] = cot[...].astype(f32) * valid_column(pos, own_a, b, band_rows, grid_w)
    vec[...] = vec_in[...]
    xhat, rstd = norm_rows(resid[...])
    dn = dn_one[...] + dn_two[...].astype(f32)
    vec[3:4, :] = jnp.sum(dn, axis=0, keepdims=True)
    vec[1:2, :] = jnp.sum(dn * xhat, axis=0, keepdims=True)
    dx = dn * gains[1:2, :]
    back_x = rstd * (
        dx - jnp.mean(dx, axis=-1, keepdims=True) - xhat * jnp.mean(dx * xhat, axis=-1, keepdims=True)
    )
    d_res = g_s[...] + back_x
    d_residual[...] = d_res
    low = d_res.astype(bf16)
    dat[...] = dot_nn(low, proj[...]).T.astype(bf16)
    d_mine[...] = dat[pl.ds(pl.multiple_of(core * OWN, 16), OWN), :]
    d_send[...] = dat[pl.ds(pl.multiple_of((1 - core) * OWN, 16), OWN), :]
    vec[7:8, :] = jnp.sum(low.astype(f32), axis=0, keepdims=True)
    grad_p[...] = dot_tn(low, att[...])
    p_keep[...] = grad_p[pl.ds(pl.multiple_of(core * OWN, 8), OWN), :]
    p_send[...] = grad_p[pl.ds(pl.multiple_of((1 - core) * OWN, 8), OWN), :].astype(bf16)


def branch(pos, own_a, cots, resid, att, proj, dn_one, dn_two, gains, vec, band_rows, grid_w):
    half = resid.shape[0]
    v = pltpu.VMEM
    outs = (
        sds((half, D), f32),
        sds((OWN, half), bf16),
        sds((OWN, half), bf16),
        sds((OWN, D), f32),
        sds((OWN, D), bf16),
        sds((16, D), f32),
    )
    body = functools.partial(branch_kernel, band_rows=band_rows, grid_w=grid_w)
    return kernel_call(body, outs, [v((half, D), f32), v((D, half), bf16), v((D, D), f32)], 1, 10)(
        pos, own_a, *cots, resid, att, proj, dn_one, dn_two, gains, vec
    )


def scores_kernel(which, q_aug, k_aug, k_nat, v_nat, logs, d_out, *refs):
    before, (dq, dk, dv) = refs[:-3], refs[-3:]
    half = d_out.shape[1]
    here = slice(which * half, (which + 1) * half)
    for h in range(OWN_HEADS):
        q_t = q_aug[h, :, here]
        g = d_out[h * HD : (h + 1) * HD, :]
        p = jnp.exp(dot_nn(k_nat[h], q_t) - logs[h, :, here])
        dp = dot_nn(v_nat[h], g)
        inner = jnp.sum(p * dp, axis=0, keepdims=True)
        ds = (p * (dp - inner)).astype(bf16)
        dv_one = dot_nt(g, p.astype(bf16))
        dk_one = dot_nt(q_t[0:HD, :], ds)
        dq[h] = dot_nn(k_aug[h, 0:HD, :], ds) * 0.125
        dk[h] = dk_one + before[0][h] if before else dk_one
        dv[h] = dv_one + before[1][h] if before else dv_one


def scores_back(which, q_aug, k_aug, k_nat, v_nat, logs, d_out, before=()):
    tokens = q_aug.shape[2]
    outs = (sds((OWN_HEADS, HD, tokens // 2), f32),) + (sds((OWN_HEADS, HD, tokens), f32),) * 2
    return kernel_call(functools.partial(scores_kernel, which), outs, (), 0, 6 + len(before), extra=28)(
        q_aug, k_aug, k_nat, v_nat, logs, d_out, *before
    )


def back_kernel(
    pos, normed, w_own, qrot, krot, dq_a, dq_b, dk, dv, cos, sin, rows, cols, own_a, own_b, oth_a, oth_b,
    qkv_mom, proj_mom, p_keep, p_recv, vec_in, vec_mom,
    out, s1, s2, s3, dn_own, dn_oth,
    dm, dm_full, freq, d_w, d_p, vec,
):
    core, band, chip, group = pos[0], pos[1], pos[2], pos[3]
    tokens = normed.shape[0]
    half = tokens // 2
    slab = half // 2
    dm_full[...] = jnp.zeros_like(dm_full)
    freq[...] = jnp.zeros_like(freq)
    for h in range(OWN_HEADS):
        c = cos[h * HALF : (h + 1) * HALF, :]
        s = sin[h * HALF : (h + 1) * HALF, :]
        angle = None
        d_query = jnp.concatenate([dq_a[h], dq_b[h]], axis=1)
        for which, source, rotated in ((0, d_query, qrot), (1, dk[h], krot)):
            du = source[0:HALF, :]
            dw = source[HALF:HD, :]
            u = rotated[h * HD : h * HD + HALF, :]
            w = rotated[h * HD + HALF : (h + 1) * HD, :]
            turn = dw * u - du * w
            angle = turn if angle is None else angle + turn
            at = which * OWN + h * HD
            dm[at : at + HD, :] = jnp.concatenate([du * c + dw * s, dw * c - du * s], axis=0).astype(bf16)
        at = pl.multiple_of(core * 96 + h * HALF, 32)
        freq[pl.ds(at, HALF), :] = jnp.sum(angle * rows[...], axis=1, keepdims=True)
        at = pl.multiple_of(192 + core * 96 + h * HALF, 32)
        freq[pl.ds(at, HALF), :] = jnp.sum(angle * cols[...], axis=1, keepdims=True)
        at = 2 * OWN + h * HD
        dm[at : at + HD, :] = dv[h].astype(bf16)
    for t in range(3):
        at = pl.multiple_of(t * D + core * OWN, 16)
        dm_full[pl.ds(at, OWN), :] = dm[t * OWN : (t + 1) * OWN, :]
    d_w[...] = dot_nn(dm[...], normed[...])
    for j in range(3):
        whole = band * 3 + j
        here = jnp.logical_and(lax.rem(whole, 4) // 2 == core, group == 0)
        at = pl.multiple_of(((whole // 4) * 2 + lax.rem(whole, 2)) * 96, 32)

        @pl.when(here)
        def _():
            d_w[pl.ds(at, 96), :] += 0.5 * qkv_mom[j * 96 : (j + 1) * 96, :]

    d_p[...] = p_keep[...] + p_recv[...].astype(f32)

    @pl.when(jnp.logical_and(band // 2 == core, group == 0))
    def _():
        d_p[pl.ds(pl.multiple_of(lax.rem(band, 2) * 96, 32), 96), :] += 0.5 * proj_mom[...]

    vec[...] = vec_in[...] + vec_mom[...]
    sums = dot_nt(jnp.ones((8, tokens), bf16), dm_full[...])
    for t in range(3):
        vec[4 + t : 5 + t, :] += sums[0:1, t * D : (t + 1) * D]
    vec[13:14, :] += jnp.broadcast_to(freq[...], (D, 128)).T[0:1, :]
    for b, src in enumerate((own_a, own_b, oth_a, oth_b)):
        part = dot_tn(dm[:, b * slab : (b + 1) * slab], w_own[...])
        xhat, _ = norm_rows(src[0:slab, :].astype(f32))
        vec[0:1, :] += jnp.sum(part * xhat, axis=0, keepdims=True)
        vec[2:3, :] += jnp.sum(part, axis=0, keepdims=True)
        to, at = (dn_own, b) if b < 2 else (dn_oth, b - 2)
        to[at * slab : (at + 1) * slab, :] = part.astype(to.dtype)
    low = vec[...].astype(bf16)
    for e, ref in enumerate((out, s1, s2, s3)):
        quarter = lax.bitwise_xor(chip, e)
        ref[0:144, :] = d_w[pl.ds(pl.multiple_of(quarter * 144, 16), 144), :].astype(bf16)
        ref[144:192, :] = d_p[pl.ds(pl.multiple_of(quarter * 48, 16), 48), :].astype(bf16)
        ref[192:208, :] = low


def back(pos, normed, w_own, qrot, krot, grads, cos, sin, rows, cols, slab_refs, moms, projs, vecs):
    tokens = normed.shape[0]
    half = tokens // 2
    outs = (sds((208, D), bf16),) * 4 + (sds((half, D), f32), sds((half, D), bf16))
    v = pltpu.VMEM
    scratch = [
        v((3 * OWN, tokens), bf16),
        v((3 * D, tokens), bf16),
        v((D, 1), f32),
        v((3 * OWN, D), f32),
        v((OWN, D), f32),
        v((16, D), f32),
    ]
    return kernel_call(back_kernel, outs, scratch, 1, 22, extra=10)(
        pos, normed, w_own, qrot, krot, *grads, cos, sin, rows, cols, *slab_refs, *moms, *projs, *vecs
    )


def tail_kernel(
    pos, own_a, own_b, d_residual, dn_one, dn_two, base, acc_two, gains, out_a, out_b, band_rows, grid_w
):
    slab = band_rows * grid_w
    for b, (src, out) in enumerate(((own_a, out_a), (own_b, out_b))):
        here = slice(b * slab, (b + 1) * slab)
        total = base[here, :] + acc_two[here, :].astype(f32)
        out[0:slab, :] = (total * valid_column(pos, own_a, b, band_rows, grid_w)).astype(bf16)
        xhat, rstd = norm_rows(src[0:slab, :].astype(f32))
        dx = (dn_one[here, :] + dn_two[here, :].astype(f32)) * gains[0:1, :]
        back_x = rstd * (
            dx - jnp.mean(dx, axis=-1, keepdims=True) - xhat * jnp.mean(dx * xhat, axis=-1, keepdims=True)
        )
        out[slab : 2 * slab, :] = (d_residual[here, :] + back_x).astype(bf16)


def tail(pos, own, d_residual, dn_one, dn_two, base, acc_two, gains, band_rows, grid_w):
    outs = (sds((2 * band_rows * grid_w, D), bf16),) * 2
    body = functools.partial(tail_kernel, band_rows=band_rows, grid_w=grid_w)
    return kernel_call(body, outs, (), 1, 8)(
        pos, *own, d_residual, dn_one, dn_two, base, acc_two, gains
    )


def place_kernel(pos, a, b, block_out, patch_grad):
    band = pos[1]
    slab = block_out.shape[1]
    for which, ref in ((0, a), (1, b)):
        image = lax.rem(band + which, 2)
        block_out[image] = ref[0:slab, :]
        patch_grad[image] = ref[slab : 2 * slab, :].astype(f32)


def place(pos, got):
    slab = got[0].shape[0] // 2
    outs = (sds((2, slab, D), bf16), sds((2, slab, D), f32))
    return kernel_call(place_kernel, outs, (), 1, 2)(pos, *got)


def bands_kernel(pos, mine, r1, r2, r3, own, s1, s2, s3):
    band = pos[1]
    for d, ref in ((0, own), (1, s1), (2, s2), (3, s3)):
        z = lax.bitwise_xor(band, d)
        part = (mine[z] + r1[z].astype(f32)) + (r2[z].astype(f32) + r3[z].astype(f32))
        ref[...] = part.astype(ref.dtype)


def bands(pos, mine, received):
    shape = mine.shape[1:]
    outs = (sds(shape, f32),) + (sds(shape, bf16),) * 3
    return kernel_call(bands_kernel, outs, (), 1, 4)(pos, mine, *received)


def piece_kernel(own, r1, r2, r3, mom, out):
    total = (own[...] + r1[...].astype(f32)) + (r2[...].astype(f32) + r3[...].astype(f32)) + 0.5 * mom[...]
    out[...] = total.astype(bf16)


def piece_sum(own, received, mom):
    return kernel_call(piece_kernel, sds(own.shape, bf16), (), 0, 5)(own, *received, mom)


def sum_low_kernel(own, r1, r2, r3, out):
    total = (own[...].astype(f32) + r1[...].astype(f32)) + (r2[...].astype(f32) + r3[...].astype(f32))
    out[...] = total.astype(bf16)


def sum_low(own, received):
    return kernel_call(sum_low_kernel, sds(own.shape, bf16), (), 0, 4)(own, *received)


def split_low(x):
    high = x.astype(bf16)
    return high, (x - high.astype(f32)).astype(bf16)


def dot_three_even(a, b):
    left = jnp.concatenate([a[0], a[0], a[1]], axis=1)
    right = jnp.concatenate([b[0], b[1], b[0]], axis=0)
    side = dot_nn(left, right[:, 0:256])
    low = dot_nn(left[256:], right[:, 256:])
    return jnp.concatenate([side, jnp.concatenate([side[256:].T, low], axis=0)], axis=1)


def sweeps(grams):
    row = lax.broadcasted_iota(jnp.int32, (D, D), 0)
    col = lax.broadcasted_iota(jnp.int32, (D, D), 1)
    eye = (row == col).astype(f32)
    scales, current, totals = [], [], [None] * len(grams)
    for gram in grams:
        trace = jnp.sum(jnp.sum(gram * eye, axis=1, keepdims=True), axis=0, keepdims=True)
        scales.append(1.0 / (jnp.sqrt(trace) + 1e-07))
        current.append(gram * (scales[-1] * scales[-1]))
    for sweep in range(5):
        parts = [split_low(a) for a in current]
        polys = [
            coeff_one * eye + coeff_two * a + coeff_three * dot_three_even(a2, a2) for a, a2 in zip(current, parts)
        ]
        halves = [split_low(poly) for poly in polys]
        if sweep < 4:
            turned = [dot_three_even(a2, p2) for a2, p2 in zip(parts, halves)]
        totals = [
            poly if total is None else dot_three_even(split_low(total), p2)
            for total, poly, p2 in zip(totals, polys, halves)
        ]
        if sweep < 4:
            current = [dot_three_even(split_low(t), p2) for t, p2 in zip(turned, halves)]
    return [total * scale for total, scale in zip(totals, scales)]


def gram_kernel(pos, a0, a1, a2, a3, keep, send, band_rows, shrink, expand):
    core, chip = pos[0], pos[2]
    for e, ref in enumerate((a0, a1, a2, a3)):
        for d in range(4):
            at = (e * 4 + d) * 48
            shrink[at : at + 48, :] = ref[d, 0:48, :]
            expand[at : at + 48, :] = ref[d, 48:96, :]
        at = pl.multiple_of(lax.bitwise_xor(chip, e) * 48, 16)
        band_rows[pl.ds(at, 48), :] = ref[0, 0:48, :]
        band_rows[pl.ds(pl.multiple_of(192 + at, 16), 48), :] = ref[0, 48:96, :]
    gram_s, gram_e = dot_tn(shrink[...], shrink[...]), dot_tn(expand[...], expand[...])
    keep[...] = jnp.where(core == 0, gram_s, gram_e)
    send[...] = jnp.where(core == 0, gram_e, gram_s)


def half_grams(pos, parts):
    outs = (sds((D, D), f32), sds((D, D), f32), sds((D, D), bf16))
    return kernel_call(gram_kernel, outs, [pltpu.VMEM((FF // 2, D), bf16)] * 2, 1, 4, extra=10)(pos, *parts)


def muon_kernel(pos, keep, recv, q0, q1, q2, q3, o0, o1, o2, o3, w0, w1, w2, w3, one_out, two_out, gram, rows):
    core = pos[0]
    pieces = (q0, q1, q2, q3, o0, o1, o2, o3)

    @pl.when(core == 0)
    def _():
        for e, ref in enumerate(pieces):
            rows[e * 144 : (e + 1) * 144, :] = ref[0:144, :]
        gram[...] = dot_tn(rows[...], rows[...])

    @pl.when(core != 0)
    def _():
        for e, ref in enumerate(pieces):
            rows[e * 48 : (e + 1) * 48, :] = ref[144:192, :]
        gram[...] = dot_tn(rows[0:D, :], rows[0:D, :])

    one, two = sweeps([keep[...] + recv[...], gram[...]])
    one_out[...] = one
    two_out[...] = two


def muon(pos, keep, recv, own_q, oth_q, weights):
    scratch = [pltpu.VMEM((D, D), f32), pltpu.VMEM((3 * D, D), bf16)]
    outs = (sds((D, D), f32),) * 2
    return kernel_call(muon_kernel, outs, scratch, 1, 14, extra=12)(pos, keep, recv, *own_q, *oth_q, *weights)


def final_kernel(
    pos, one, two, one_oth, two_oth, band_mine, band_oth, q0, q1, q2, q3, o0, o1, o2, o3,
    qkv_w, proj_w, expand_w, shrink_w,
    qkv_m, qkv_new, proj_m, proj_new, expand_m, expand_new, shrink_m, shrink_new,
    q_mine, q_oth, q_rows,
):
    core, band, chip = pos[0], pos[1], pos[2]
    first = core == 0

    def choose(when_first, a, b):
        return split_low(jnp.where(first == when_first, a[...], b[...]))

    for e in range(4):
        quarter = lax.bitwise_xor(chip, e)
        for refs, to in (((q0, q1, q2, q3), q_mine), ((o0, o1, o2, o3), q_oth)):
            to[pl.ds(pl.multiple_of(quarter * 144, 16), 144), :] = refs[e][0:144, :]
            to[pl.ds(pl.multiple_of(3 * OWN + quarter * 48, 16), 48), :] = refs[e][144:192, :]
    for j in range(4):
        whole = band * 3 + j
        at = pl.multiple_of(((whole // 4) * 2 + lax.rem(whole, 2)) * 96, 32)
        mine = lax.rem(whole, 4) // 2 == core
        if j == 3:
            at = pl.multiple_of(3 * OWN + lax.rem(band, 2) * 96, 32)
            mine = band // 2 == core

        @pl.when(mine)
        def _():
            q_rows[j * 96 : (j + 1) * 96, :] = q_mine[pl.ds(at, 96), :]

        @pl.when(jnp.logical_not(mine))
        def _():
            q_rows[j * 96 : (j + 1) * 96, :] = q_oth[pl.ds(at, 96), :]

    b_mine, b_oth = band_mine[...].astype(f32), band_oth[...].astype(f32)
    low_core, high_core = jnp.where(first, b_mine, b_oth), jnp.where(first, b_oth, b_mine)
    m_shrink = jnp.concatenate([low_core[0:192], high_core[0:192]], axis=0)
    m_expand = jnp.concatenate([low_core[192:], high_core[192:]], axis=0)
    t_shrink, t_expand = choose(True, one, one_oth), choose(False, one, one_oth)
    t_qkv, t_proj = choose(True, two, two_oth), choose(False, two, two_oth)
    for w, t, low, mom, new, size in (
        (qkv_w, t_qkv, q_rows[0:288, :], qkv_m, qkv_new, 3 * D),
        (proj_w, t_proj, q_rows[288:D, :], proj_m, proj_new, D),
        (shrink_w, t_shrink, m_shrink.astype(bf16), shrink_m, shrink_new, FF),
    ):
        mom[...] = low.astype(f32)
        new[...] = w[...] - 0.05 * math.sqrt(size) * (dot_nn(low, t[0]) + dot_nn(low, t[1]))
    low = m_expand.astype(bf16)
    expand_m[...] = m_expand.T
    expand_new[...] = expand_w[...] - 0.05 * math.sqrt(FF) * (dot_nt(t_expand[0], low) + dot_nt(t_expand[1], low))


def final(pos, turns, far_turns, band_mine, band_oth, own_q, oth_q, *weights):
    outs = []
    for w in weights:
        outs += [sds(w.shape, f32)] * 2
    v = pltpu.VMEM
    scratch = [v((4 * OWN, D), bf16), v((4 * OWN, D), bf16), v((D, D), bf16)]
    return kernel_call(final_kernel, tuple(outs), scratch, 1, 18, extra=10)(
        pos, *turns, *far_turns, band_mine, band_oth, *own_q, *oth_q, *weights
    )


def vector_kernel(pos, mine, other, gains, biases, freq, g_mom, g_new, b_mom, b_new, f_mom, f_new, mom, new):
    band = pos[1]
    n = mine.shape[0] - 16
    total = mine[n : n + 16, :].astype(f32) + other[n : n + 16, :].astype(f32)
    mom[...] = total
    new[...] = jnp.zeros_like(new)
    freqs = jnp.concatenate([freq[0:1, :], freq[1:2, :]], axis=1)
    for at, values in ((0, gains[...]), (2, biases[...]), (13, freqs)):
        here = slice(at, at + values.shape[0])
        part = total[here, :]
        square = jnp.sum(jnp.sum(part * part, axis=1, keepdims=True), axis=0, keepdims=True)
        new[here, :] = values - 0.2 * part * lax.rsqrt(square * (1.0 / (values.shape[0] * D)) + 1e-06)
    for whole, g_out, b_out, f_out in ((mom, g_mom, b_mom, f_mom), (new, g_new, b_new, f_new)):
        g_out[...] = pltpu.roll(whole[0:8, :], lax.rem(D - 96 * band, D), 1)[0:2, 0:96]
        rows = pltpu.roll(jnp.broadcast_to(whole[13:14, :], (8, D)), lax.rem(D - 48 * band, D), 1)
        f_out[...] = jnp.concatenate([rows[0:1, 0:48], rows[0:1, 192:240]], axis=0)
        for i in range(11):
            block = 11 * band + i
            row = jnp.broadcast_to(whole[pl.ds(2 + block // 4, 1), :], (8, D))
            b_out[i : i + 1, :] = pltpu.roll(row, lax.rem(D - 96 * lax.rem(block, 4), D), 1)[0:1, 0:96]


def vector_step(pos, mine, other, gains, biases, freq):
    outs = (sds((2, 96), f32),) * 2 + (sds((11, 96), f32),) * 2 + (sds((2, 48), f32),) * 2
    scratch = [pltpu.VMEM((16, D), f32)] * 2
    return kernel_call(vector_kernel, outs, scratch, 1, 5, cost=10**10)(pos, mine, other, gains, biases, freq)


def flip(x, bit):
    n = lax.axis_size("batch")
    return lax.ppermute(x, "batch", [(i, i ^ bit) for i in range(n)])


def swap_bands(x, d):
    return lax.ppermute(x, "rows", [(i, i ^ d) for i in range(4)])


def moves(which):
    pairs = []
    for k in range(lax.axis_size("batch") // 2):
        for c in range(2):
            for i in range(4):
                band = (i - 2 * c - which) % 4
                pairs.append(((2 * k + i // 2) * 4 + band, (2 * k + c) * 4 + i))
    return pairs


def to_image(parts):
    return [lax.ppermute(parts[which], AXES, moves(which)) for which in range(2)]


def from_image(part, which):
    return lax.ppermute(part, AXES, [(b, a) for a, b in moves(which)])


def other_chips(x):
    bit = 8
    while bit < lax.axis_size("batch"):
        x = x + flip(x.astype(f32), bit).astype(x.dtype)
        bit *= 2
    return x


def over_chips(x):
    return [flip(x, 2 * e) for e in range(1, 4)]


def over_bands(x):
    return [swap_bands(x, d) for d in range(1, 4)]


def local(
    patches,
    cotangent,
    heights,
    widths,
    qkv_weight,
    qkv_moment,
    proj_weight,
    proj_moment,
    expand_weight,
    expand_moment,
    shrink_weight,
    shrink_moment,
    norm_gains,
    gains_moment,
    all_biases,
    biases_moment,
    frequencies,
    freq_moment,
):
    images, band_rows, grid_w, _ = patches.shape
    slab = band_rows * grid_w
    batch = lax.axis_index("batch")
    band = lax.axis_index("rows")
    core = batch % 2
    chip = (batch // 2) % 4
    pos = jnp.stack([core, band, chip, batch // 2]).astype(jnp.int32)
    grid = (band_rows, grid_w)

    share = own_weights(pos, qkv_weight.T, proj_weight.T, expand_weight, shrink_weight)
    shares = over_bands(share)
    p_a, p_b, c_a, c_b = slabs(
        pos, heights, widths, patches.reshape(images, slab, D), cotangent.reshape(images, slab, D)
    )
    own = to_image((p_a, p_b))
    oth = [flip(x, 1) for x in own]
    biases = all_biases.reshape(-1, D)
    cos, sin, rows_tok, cols_tok, bias_own, mom_big, vec_mom = setup(
        pos, frequencies, biases, expand_moment, shrink_moment,
        gains_moment, biases_moment.reshape(11, 96), freq_moment, 4 * slab, *grid,
    )
    shares, cos, vec_mom = lax.optimization_barrier((shares, cos, vec_mom))
    w_qkv, w_first, w_second = pack(share, shares)
    w_qkv = [w_qkv] + over_chips(w_qkv)
    w_first, oth = lax.optimization_barrier((w_first, oth))
    w_first = [w_first] + over_chips(w_first)
    c_a, c_b, w_second, w_qkv = lax.optimization_barrier((c_a, c_b, w_second, w_qkv))
    cot = to_image((c_a, c_b))
    w_second = [w_second] + over_chips(w_second)

    normed, w_own, qrot, krot, q_aug, k_aug, k_nat, v_nat, logs, *o_mine = front(
        pos, own + oth, w_qkv, bias_own, norm_gains, biases, cos, sin, rows_tok, cols_tok
    )
    o_oth = [flip(x, 1) for x in o_mine]
    cot, o_mine = lax.optimization_barrier((cot, o_mine))
    cot = cot + [flip(x, 1) for x in cot]
    resid, att, proj16, e_all, n2, hidden, slope = expand_layer(
        pos, own + oth, (*o_mine, *o_oth), w_first, norm_gains, biases, 2 * slab
    )
    g16, s_all, dpre, dn_two, dn_two_send = slope_layer(pos, own[0], cot, w_second, e_all, slope, *grid)
    dn_two_recv = flip(dn_two_send, 1)
    base, acc_send, big, b1, b2, b3, vec = shrink_layer(pos, hidden, dpre, g16, n2, s_all, resid, biases)
    big_chips = [flip(x, 2 * e) for e, x in zip((1, 2, 3), (b1, b2, b3))]
    d_residual, d_mine, d_send, p_keep, p_send, vec = branch(
        pos, own[0], cot[:2], resid, att, proj16, dn_two, dn_two_recv, norm_gains, vec, *grid
    )
    d_recv = flip(d_send, 1)
    p_recv = flip(p_send, 1)
    dq_a, dk, dv = scores_back(0, q_aug, k_aug, k_nat, v_nat, logs, d_mine)
    acc_recv = flip(acc_send, 1)
    dq_b, dk, dv = scores_back(1, q_aug, k_aug, k_nat, v_nat, logs, d_recv, (dk, dv))

    big, dq_b = lax.optimization_barrier((big, dq_b))
    own_big, *to_bands = bands(pos, other_chips(big), big_chips)
    to_bands, dq_b, acc_recv = lax.optimization_barrier((to_bands, dq_b, acc_recv))
    from_bands = [swap_bands(x, d) for d, x in zip((1, 2, 3), to_bands)]
    q_mine, *q_sends, dn_own, dn_oth = back(
        pos, normed, w_own, qrot, krot, (dq_a, dq_b, dk, dv), cos, sin, rows_tok, cols_tok, own + oth,
        (qkv_moment.T, proj_moment.T), (p_keep, p_recv), (vec, vec_mom),
    )
    dn_recv = flip(dn_oth, 1)
    big_piece = piece_sum(own_big, from_bands, mom_big)
    q_sends, big_piece = lax.optimization_barrier((q_sends, big_piece))

    q_low = other_chips(sum_low(q_mine, [flip(x, 2 * e) for e, x in zip((1, 2, 3), q_sends)]))
    big_bands = jnp.stack([big_piece, swap_bands(big_piece, 1)])
    big_bands = jnp.concatenate([big_bands, swap_bands(big_bands, 2)])
    big_bands, q_low = lax.optimization_barrier((big_bands, q_low))
    big_all = [big_bands] + over_chips(big_bands)
    q_recv = over_bands(q_low)
    results = tail(pos, own, d_residual, dn_own, dn_recv, base, acc_recv, norm_gains, *grid)
    q_recv, results = lax.optimization_barrier((q_recv, results))
    q_piece = sum_low(q_low, q_recv)
    big_all, q_piece = lax.optimization_barrier((big_all, q_piece))
    own_q = [q_piece] + over_chips(q_piece)
    oth_q = [flip(x, 1) for x in own_q]

    gram_keep, gram_send, band_mine = half_grams(pos, big_all)
    image_a, image_b = from_image(results[0], 0), from_image(results[1], 1)
    weights = (qkv_weight.T, proj_weight.T, expand_weight, shrink_weight)
    turns = muon(pos, gram_keep, flip(gram_send, 1), own_q, oth_q, weights)
    images_back = [from_image(part, which) for which, part in enumerate(results)]
    images_back, _ = lax.optimization_barrier((images_back, turns))
    block_out, patch_grad = place(pos, images_back)
    vec_q, block_out = lax.optimization_barrier((own_q[0], block_out))
    vector_steps = vector_step(pos, vec_q, oth_q[0], norm_gains, biases, frequencies)
    shape = (images, band_rows, grid_w, D)
    block_out, patch_grad = block_out.reshape(shape), patch_grad.reshape(shape)
    far_turns, band_oth = [flip(x, 1) for x in turns], flip(band_mine, 1)
    far_turns, block_out, vector_steps = lax.optimization_barrier((far_turns, block_out, vector_steps))
    new = final(pos, turns, far_turns, band_mine, band_oth, own_q, oth_q, *weights)
    new = [x.T for x in new[:4]] + list(new[4:])

    new, vectors = lax.optimization_barrier((new, list(vector_steps)))
    vectors[2], vectors[3] = vectors[2].reshape(-1), vectors[3].reshape(-1)
    return (block_out, patch_grad) + tuple(new) + tuple(vectors)


def solution(mesh):
    image = P("batch", "rows", None, None)
    cols, rows = P(None, "rows"), P("rows", None)
    return jax.shard_map(
        local,
        mesh=mesh,
        in_specs=(
            image, image, P("batch"), P("batch"), cols, cols, cols, cols, cols, cols, rows, rows,
            P(), cols, P(), P("rows"), P(), cols,
        ),
        out_specs=(
            image, image, cols, cols, cols, cols, cols, cols, rows, rows, cols, cols, P("rows"), P("rows"), cols, cols,
        ),
        check_vma=False,
    )
```

```python
import functools
import math

import jax
import jax.numpy as jnp
from jax import lax
from jax.experimental import pallas as pl
from jax.experimental.pallas import tpu as pltpu
from jax.sharding import PartitionSpec as P

D = 384
H = 6
HD = 64
FF = 1536
HALF = HD // 2
OWN_HEADS = H // 2
OWN = OWN_HEADS * HD
AUG = HD + 16

coeff_one = 3.4445
coeff_two = -4.775
coeff_three = 2.0315

bf16 = jnp.bfloat16
f32 = jnp.float32
AXES = ("batch", "rows")


def dot_nn(a, b):
    return lax.dot_general(a, b, (((1,), (0,)), ((), ())), preferred_element_type=f32)


def dot_nt(a, b):
    return lax.dot_general(a, b, (((1,), (1,)), ((), ())), preferred_element_type=f32)


def dot_tn(a, b):
    return lax.dot_general(a, b, (((0,), (0,)), ((), ())), preferred_element_type=f32)


def vmem_bytes(x):
    *lead, rows, lanes = (1,) * max(0, 2 - len(x.shape)) + tuple(x.shape)
    size = jnp.dtype(x.dtype).itemsize
    tile = 8 * 4 // size
    return math.prod(lead) * (-(-rows // tile) * tile) * (-(-lanes // 128) * 128) * size


def kernel_call(body, out_shape, scratch=(), smem=0, n_in=0, extra=4, cost=None):
    specs = [pl.BlockSpec(memory_space=pltpu.SMEM)] * smem
    specs += [pl.BlockSpec(memory_space=pltpu.VMEM)] * n_in

    def call(*args):
        held = list(args[smem:]) + jax.tree.leaves(out_shape) + [s for s in scratch]
        limit = sum(vmem_bytes(x) for x in held) + extra * 2**20
        return pl.pallas_call(
            body,
            out_shape=out_shape,
            in_specs=specs,
            out_specs=jax.tree.map(lambda _: pl.BlockSpec(memory_space=pltpu.VMEM), out_shape),
            scratch_shapes=list(scratch),
            compiler_params=pltpu.CompilerParams(vmem_limit_bytes=int(limit)),
            cost_estimate=cost and pl.CostEstimate(flops=cost, bytes_accessed=0, transcendentals=0),
        )(*args)

    return call


def sds(shape, dtype):
    return jax.ShapeDtypeStruct(shape, dtype)


def norm_rows(x):
    centered = x - jnp.mean(x, axis=-1, keepdims=True)
    rstd = lax.rsqrt(jnp.mean(centered * centered, axis=-1, keepdims=True) + 1e-06)
    return centered * rstd, rstd


def weights_kernel(pos, qkv_t, proj_t, expand, shrink, out, q_s, p_s, e_s, s_s, sem_q, sem_p, sem_e, sem_s):
    core, band, chip = pos[0], pos[1], pos[2]
    start = jnp.where(core == 0, jnp.where(band < 3, 2 * band, 0), jnp.where(band == 0, 4, jnp.where(band == 3, 2, 0)))
    count = jnp.where((core == 0) == (band < 2), 4, 2)
    at_q = pl.multiple_of((start + jnp.minimum(chip, count - 1)) * 48, 8)
    at_p = pl.multiple_of(jnp.minimum(chip, 2) * 32, 8)
    at = pl.multiple_of(core * 192 + chip * 48, 8)
    copies = (
        pltpu.make_async_copy(expand, e_s, sem_e),
        pltpu.make_async_copy(qkv_t.at[pl.ds(at_q, 48), :], q_s, sem_q),
        pltpu.make_async_copy(proj_t.at[pl.ds(at_p, 32), :], p_s, sem_p),
        pltpu.make_async_copy(shrink.at[pl.ds(at, 48), :], s_s, sem_s),
    )
    for copy in copies:
        copy.start()
    for copy in copies[1:]:
        copy.wait()
    out[0:48, :] = q_s[...].astype(bf16)
    out[48:80, :] = p_s[...].astype(bf16)
    out[128:176, :] = s_s[...].astype(bf16)
    copies[0].wait()
    e_s[...] = e_s[...].T
    out[80:128, :] = e_s[pl.ds(at, 48), :].astype(bf16)


def own_weights(pos, qkv_t, proj_t, expand, shrink):
    v = pltpu.VMEM
    dma = pltpu.SemaphoreType.DMA
    scratch = [v((48, D), f32), v((32, D), f32), v((D, D), f32), v((48, D), f32), dma, dma, dma, dma]
    hbm = pl.BlockSpec(memory_space=pltpu.HBM)
    return pl.pallas_call(
        weights_kernel,
        out_shape=sds((176, D), bf16),
        in_specs=[pl.BlockSpec(memory_space=pltpu.SMEM)] + [hbm] * 4,
        out_specs=pl.BlockSpec(memory_space=pltpu.VMEM),
        scratch_shapes=scratch,
        compiler_params=pltpu.CompilerParams(vmem_limit_bytes=56 * 2**20),
    )(pos, qkv_t, proj_t, expand, shrink)


def slabs_kernel(pos, heights, widths, patches, cot, p_a, p_b, c_a, c_b):
    band = pos[1]
    slab = patches.shape[1]
    row = lax.broadcasted_iota(jnp.int32, (16, D), 0)
    for which, (p, c) in enumerate(((p_a, c_a), (p_b, c_b))):
        image = lax.rem(band + which, 2)
        p[0:slab, :] = patches[image]
        size = jnp.where(row == 0, heights[image], widths[image])
        p[slab : slab + 16, :] = size.astype(f32).astype(bf16)
        c[...] = cot[image]


def slabs(pos, heights, widths, patches, cot):
    slab = patches.shape[1]
    outs = (sds((slab + 16, D), bf16),) * 2 + (sds((slab, D), bf16),) * 2
    return kernel_call(slabs_kernel, outs, (), 3, 2)(pos, heights, widths, patches, cot)


def setup_kernel(
    pos, freq, biases, expand_mom, shrink_mom, gains_mom, biases_mom, freq_mom,
    cos, sin, rows, cols, bias_own, mom_big, vec,
    column, turned, freq_one, freq_two, band_rows, grid_w,
):
    core, band, chip, group = pos[0], pos[1], pos[2], pos[3]
    tokens = rows.shape[1]
    slab = band_rows * grid_w
    token = lax.broadcasted_iota(jnp.int32, (1, tokens), 1)
    slot = token // slab
    d = jnp.where(slot < 2, 2 * core + slot, 2 - 2 * core + slot - 2)
    row = lax.bitwise_and(band + 4 - d, 3) * band_rows + lax.rem(token, slab) // grid_w
    rows[...] = row.astype(f32)
    cols[...] = lax.rem(token, grid_w).astype(f32)
    own = pl.ds(pl.multiple_of(core * 96, 8), 96)
    freq_one[...] = jnp.broadcast_to(freq[0:1, :], (128, H * HALF)).T
    freq_two[...] = jnp.broadcast_to(freq[1:2, :], (128, H * HALF)).T
    angle = freq_one[own, 0:1] * rows[...] + freq_two[own, 0:1] * cols[...]
    cos[...] = jnp.cos(angle)
    sin[...] = jnp.sin(angle)
    for t in range(3):
        column[...] = jnp.broadcast_to(biases[2 + t : 3 + t, :], (128, D)).T
        at = pl.multiple_of(core * OWN, 8)
        bias_own[t * OWN : (t + 1) * OWN, :] = column[pl.ds(at, OWN), 0:1]
    at = pl.multiple_of(core * 192 + chip * 48, 8)
    mom_big[0:48, :] = shrink_mom[pl.ds(at, 48), :]
    turned[...] = expand_mom[...].T
    mom_big[48:96, :] = turned[pl.ds(at, 48), :]
    share = jnp.where(jnp.logical_and(core == 0, group == 0), 0.5, 0.0)
    vec[...] = jnp.zeros_like(vec)
    none = jnp.zeros((8, 144), f32)

    def wide(x, lanes):
        return jnp.concatenate([x, jnp.zeros((x.shape[0], lanes), f32)], axis=1)

    gains = jnp.concatenate([wide(gains_mom[...], 288), jnp.zeros((6, D), f32)], axis=0)
    vec[0:2, :] = share * pltpu.roll(gains, 96 * band, 1)[0:2, :]
    freqs = jnp.concatenate([freq_mom[0:1, :], none[0:1], freq_mom[1:2, :], none[0:1]], axis=1)
    vec[13:14, :] = share * pltpu.roll(jnp.broadcast_to(freqs, (8, D)), 48 * band, 1)[0:1, :]
    for i in range(11):
        block = 11 * band + i
        line = jnp.broadcast_to(wide(biases_mom[i : i + 1, :], 288), (8, D))
        vec[pl.ds(2 + block // 4, 1), :] += share * pltpu.roll(line, 96 * lax.rem(block, 4), 1)[0:1, :]


def setup(pos, freq, biases, expand_mom, shrink_mom, gains_mom, biases_mom, freq_mom, tokens, band_rows, grid_w):
    v = pltpu.VMEM
    outs = (
        sds((96, tokens), f32),
        sds((96, tokens), f32),
        sds((1, tokens), f32),
        sds((1, tokens), f32),
        sds((3 * OWN, 1), f32),
        sds((96, D), f32),
        sds((16, D), f32),
    )
    scratch = [v((D, 128), f32), v((D, D), f32), v((H * HALF, 128), f32), v((H * HALF, 128), f32)]
    body = functools.partial(setup_kernel, band_rows=band_rows, grid_w=grid_w)
    return kernel_call(body, outs, scratch, 1, 7)(
        pos, freq, biases, expand_mom, shrink_mom, gains_mom, biases_mom, freq_mom
    )


def pack_kernel(own, r1, r2, r3, qkv, first, second):
    for d, ref in enumerate((own, r1, r2, r3)):
        qkv[d] = ref[0:48, :]
        first[d] = ref[48:128, :]
        second[d] = ref[128:176, :]


def pack(own, received):
    outs = (sds((4, 48, D), bf16), sds((4, 80, D), bf16), sds((4, 48, D), bf16))
    return kernel_call(pack_kernel, outs, (), 0, 4)(own, *received)


def front_kernel(
    pos, own_a, own_b, oth_a, oth_b, w0, w1, w2, w3, bias, gains, biases, cos, sin, rows, cols,
    normed, w_own, qrot, krot, q_aug, k_aug, k_nat, v_nat, logs, o_own, o_oth,
    w_all, v_t, o_all,
):
    core, band, chip = pos[0], pos[1], pos[2]
    tokens = normed.shape[0]
    block = tokens // 4
    for e, ref in enumerate((w0, w1, w2, w3)):
        quarter = lax.bitwise_xor(chip, e)
        for shard in range(4):
            base = jnp.where(core == 0, (0, 4, 8, 10)[shard], (0, 2, 4, 8)[shard])
            count = jnp.where(core == 0, (4, 4, 2, 2)[shard], (2, 2, 4, 4)[shard])
            at = jnp.where(quarter < count, base + quarter, 12)
            w_all[pl.ds(pl.multiple_of(at * 48, 16), 48), :] = ref[lax.bitwise_xor(band, shard)]
    w_own[...] = w_all[0 : 3 * OWN, :]
    for b, src in enumerate((own_a, own_b, oth_a, oth_b)):
        xhat, _ = norm_rows(src[0:block, :].astype(f32))
        normed[b * block : (b + 1) * block, :] = (xhat * gains[0:1, :] + biases[0:1, :]).astype(bf16)
    high = own_a[block : block + 1, 0:1].astype(f32)
    wide = own_a[block + 1 : block + 2, 0:1].astype(f32)
    inside = jnp.logical_and(rows[...] < high, cols[...] < wide)
    key_bias = jnp.where(inside, 0.0, -1e9).astype(f32)
    ones_row = (lax.broadcasted_iota(jnp.int32, (AUG - HD, block), 0) == 0).astype(f32)
    for b in range(4):
        here = slice(b * block, (b + 1) * block)
        mixed = dot_nt(w_own[...], normed[here, :]) + bias[...]
        for h in range(OWN_HEADS):
            c = cos[h * HALF : (h + 1) * HALF, here]
            s = sin[h * HALF : (h + 1) * HALF, here]
            qu = mixed[h * HD : h * HD + HALF, :]
            qw = mixed[h * HD + HALF : (h + 1) * HD, :]
            ku = mixed[OWN + h * HD : OWN + h * HD + HALF, :]
            kw = mixed[OWN + h * HD + HALF : OWN + (h + 1) * HD, :]
            qr = jnp.concatenate([qu * c - qw * s, qw * c + qu * s], axis=0)
            kr = jnp.concatenate([ku * c - kw * s, kw * c + ku * s], axis=0)
            qrot[h * HD : (h + 1) * HD, here] = qr
            krot[h * HD : (h + 1) * HD, here] = kr
            q_low = qr.astype(bf16).astype(f32) * 0.125
            q_aug[h, :, here] = jnp.concatenate([q_low, ones_row], axis=0).astype(bf16)
            k_full = jnp.concatenate([kr, ones_row * key_bias[:, here]], axis=0)
            k_aug[h, :, here] = k_full.astype(bf16)
            k_nat[h, here, :] = k_full.T.astype(bf16)
            vv = mixed[2 * OWN + h * HD : 2 * OWN + (h + 1) * HD, :]
            v_t[h, :, here] = vv.astype(bf16)
            v_nat[h, here, :] = vv.T.astype(bf16)

    half = tokens // 2

    def attend(item, carry):
        here = pl.ds(pl.multiple_of(item * half, half), half)
        scores = [dot_nn(k_nat[h], q_aug[h, :, here]) for h in range(OWN_HEADS)]
        for h in range(OWN_HEADS):
            peak = jnp.max(scores[h], axis=0, keepdims=True)
            e = jnp.exp(scores[h] - peak)
            total = jnp.sum(e, axis=0, keepdims=True)
            out = dot_nn(v_t[h], (e * (1.0 / total)).astype(bf16))
            logs[h, :, here] = peak + jnp.log(total)
            o_all[h * HD : (h + 1) * HD, here] = out.astype(bf16)
        return carry

    lax.fori_loop(0, 2, attend, 0)
    o_own[...] = o_all[:, 0:half]
    o_oth[...] = o_all[:, half:tokens]


def front(pos, slab_refs, weights, bias, gains, biases, cos, sin, rows, cols):
    tokens = rows.shape[1]
    nh = OWN_HEADS
    outs = (
        sds((tokens, D), bf16),
        sds((3 * OWN, D), bf16),
        sds((OWN, tokens), f32),
        sds((OWN, tokens), f32),
        sds((nh, AUG, tokens), bf16),
        sds((nh, AUG, tokens), bf16),
        sds((nh, tokens, AUG), bf16),
        sds((nh, tokens, HD), bf16),
        sds((nh, 1, tokens), f32),
        sds((OWN, tokens // 2), bf16),
        sds((OWN, tokens // 2), bf16),
    )
    scratch = [
        pltpu.VMEM((3 * OWN + 48, D), bf16),
        pltpu.VMEM((nh, HD, tokens), bf16),
        pltpu.VMEM((OWN, tokens), bf16),
    ]
    return kernel_call(front_kernel, outs, scratch, 1, 15, extra=24)(
        pos, *slab_refs, *weights, bias, gains, biases, cos, sin, rows, cols
    )


def valid_column(pos, sized, first_slot, band_rows, grid_w):
    core, band = pos[0], pos[1]
    slab = band_rows * grid_w
    d = 2 * core + first_slot if first_slot < 2 else 2 - 2 * core + first_slot - 2
    token = lax.broadcasted_iota(jnp.int32, (slab, 1), 0)
    row = lax.bitwise_and(band + 4 - d, 3) * band_rows + token // grid_w
    col = lax.rem(token, grid_w)
    high = sized[slab : slab + 1, 0:1].astype(f32)
    wide = sized[slab + 1 : slab + 2, 0:1].astype(f32)
    return jnp.logical_and(row.astype(f32) < high, col.astype(f32) < wide).astype(f32)


def expand_kernel(
    pos, own_a, own_b, oth_a, oth_b, mine_a, mine_b, far_a, far_b, w0, w1, w2, w3, gains, biases,
    resid_own, att_own, proj_out, e_all, n2, hidden, slope,
    p_all,
):
    core, band, chip = pos[0], pos[1], pos[2]
    half = resid_own.shape[0]
    slab = half // 2
    first = core == 0
    for e, ref in enumerate((w0, w1, w2, w3)):
        quarter = lax.bitwise_xor(chip, e)
        for shard in range(4):
            d = lax.bitwise_xor(band, shard)
            at = jnp.where(quarter < 3, shard * 96 + quarter * 32, D)
            p_all[pl.ds(pl.multiple_of(at, 16), 32), :] = ref[d, 0:32, :]
            at = pl.multiple_of(shard * 192 + quarter * 48, 16)
            e_all[pl.ds(at, 48), :] = ref[d, 32:80, :]
    proj = p_all[0:D, :]
    proj_out[...] = proj
    bias = jnp.concatenate(
        [jnp.where(first, biases[6 + s : 7 + s, 0:192], biases[6 + s : 7 + s, 192:384]) for s in range(4)], axis=1
    )
    for b, src in enumerate((own_a, own_b, oth_a, oth_b)):
        here = slice(b * slab, (b + 1) * slab)
        there = slice((b % 2) * slab, (b % 2 + 1) * slab)
        m, o = (mine_a, far_b) if b < 2 else (mine_b, far_a)
        m, o = m[:, there].astype(f32), o[:, there].astype(f32)
        att = jnp.concatenate([jnp.where(first, m, o), jnp.where(first, o, m)], axis=0).T.astype(bf16)
        res = src[0:slab, :].astype(f32) + dot_nt(att, proj) + biases[5:6, :]
        if b < 2:
            resid_own[here, :] = res
            att_own[here, :] = att
        xhat, _ = norm_rows(res)
        n2[here, :] = (xhat * gains[1:2, :] + biases[1:2, :]).astype(bf16)

    def part(b, carry):
        here = pl.ds(pl.multiple_of(b * slab, slab), slab)
        pre = dot_nt(n2[here, :], e_all[...]) + bias
        cdf = 0.5 * (1.0 + lax.erf(pre * math.sqrt(0.5)))
        hidden[here, :] = (pre * cdf).astype(bf16)
        slope[here, :] = cdf + pre * (jnp.exp(-0.5 * pre * pre) * (1.0 / math.sqrt(2.0 * math.pi)))
        return carry

    lax.fori_loop(0, 4, part, 0)


def expand_layer(pos, slab_refs, att, weights, gains, biases, half):
    v = pltpu.VMEM
    outs = (
        sds((half, D), f32),
        sds((half, D), bf16),
        sds((D, D), bf16),
        sds((FF // 2, D), bf16),
        sds((2 * half, D), bf16),
        sds((2 * half, FF // 2), bf16),
        sds((2 * half, FF // 2), f32),
    )
    return kernel_call(expand_kernel, outs, [v((D + 32, D), bf16)], 1, 14, extra=12)(
        pos, *slab_refs, *att, *weights, gains, biases
    )


def slope_kernel(
    pos, own_a, cot_a, cot_b, cot_c, cot_d, w0, w1, w2, w3, e_all, slope, g16, s_all, dpre, dn_own, dn_send,
    band_rows, grid_w,
):
    core, band, chip = pos[0], pos[1], pos[2]
    slab = band_rows * grid_w
    for e, ref in enumerate((w0, w1, w2, w3)):
        quarter = lax.bitwise_xor(chip, e)
        for shard in range(4):
            at = pl.multiple_of(shard * 192 + quarter * 48, 16)
            s_all[pl.ds(at, 48), :] = ref[lax.bitwise_xor(band, shard)]
    for b, cot in enumerate((cot_a, cot_b, cot_c, cot_d)):
        here = slice(b * slab, (b + 1) * slab)
        g16[here, :] = (cot[...].astype(f32) * valid_column(pos, own_a, b, band_rows, grid_w)).astype(bf16)
    for b in range(4):
        here = slice(b * slab, (b + 1) * slab)
        dpre[here, :] = (dot_nt(g16[here, :], s_all[...]) * slope[here, :]).astype(bf16)
    half = 2 * slab
    dn_send[...] = dot_nn(dpre[half : 2 * half, :], e_all[...]).astype(bf16)
    dn_own[...] = dot_nn(dpre[0:half, :], e_all[...])


def slope_layer(pos, own_a, cots, weights, e_all, slope, band_rows, grid_w):
    half = 2 * band_rows * grid_w
    outs = (
        sds((2 * half, D), bf16),
        sds((FF // 2, D), bf16),
        sds((2 * half, FF // 2), bf16),
        sds((half, D), f32),
        sds((half, D), bf16),
    )
    body = functools.partial(slope_kernel, band_rows=band_rows, grid_w=grid_w)
    return kernel_call(body, outs, (), 1, 11, extra=10)(pos, own_a, *cots, *weights, e_all, slope)


def shrink_kernel(pos, hidden, dpre, g16, n2, s_all, resid, biases, base, acc_send, mine, s1, s2, s3, vec, grads):
    core, chip = pos[0], pos[2]
    half = base.shape[0]
    first = core == 0
    grads[0] = dot_tn(hidden[...], g16[...])
    grads[1] = dot_tn(dpre[...], n2[...])
    for e, ref in ((0, mine), (1, s1), (2, s2), (3, s3)):
        for z in range(4):
            at = pl.ds(pl.multiple_of(z * 192 + lax.bitwise_xor(chip, e) * 48, 16), 48)
            ref[z, 0:48, :] = grads[0, at, :].astype(ref.dtype)
            ref[z, 48:96, :] = grads[1, at, :].astype(ref.dtype)
    base[...] = resid[...] + dot_nn(hidden[0:half, :], s_all[...]) + biases[10:11, :]
    acc_send[...] = dot_nn(hidden[half : 2 * half, :], s_all[...]).astype(bf16)
    vec[...] = jnp.zeros_like(vec)
    sums = dot_nn(jnp.ones((8, 2 * half), bf16), dpre[...])
    none = jnp.zeros((1, 192), f32)
    for s in range(4):
        x = sums[0:1, s * 192 : (s + 1) * 192]
        vec[8 + s : 9 + s, :] = jnp.where(
            first, jnp.concatenate([x, none], axis=1), jnp.concatenate([none, x], axis=1)
        )
    vec[12:13, :] = jnp.sum(g16[0:half, :].astype(f32), axis=0, keepdims=True)


def shrink_layer(pos, hidden, dpre, g16, n2, s_all, resid, biases):
    half = g16.shape[0] // 2
    outs = (
        sds((half, D), f32),
        sds((half, D), bf16),
        sds((4, 96, D), f32),
        sds((4, 96, D), bf16),
        sds((4, 96, D), bf16),
        sds((4, 96, D), bf16),
        sds((16, D), f32),
    )
    return kernel_call(shrink_kernel, outs, [pltpu.VMEM((2, FF // 2, D), f32)], 1, 7, extra=10)(
        pos, hidden, dpre, g16, n2, s_all, resid, biases
    )


def branch_kernel(
    pos, own_a, cot_a, cot_b, resid, att, proj, dn_one, dn_two, gains, vec_in,
    d_residual, d_mine, d_send, p_keep, p_send, vec,
    g_s, dat, grad_p, band_rows, grid_w,
):
    core = pos[0]
    slab = band_rows * grid_w
    for b, cot in enumerate((cot_a, cot_b)):
        here = slice(b * slab, (b + 1) * slab)
        g_s[here, :] = cot[...].astype(f32) * valid_column(pos, own_a, b, band_rows, grid_w)
    vec[...] = vec_in[...]
    xhat, rstd = norm_rows(resid[...])
    dn = dn_one[...] + dn_two[...].astype(f32)
    vec[3:4, :] = jnp.sum(dn, axis=0, keepdims=True)
    vec[1:2, :] = jnp.sum(dn * xhat, axis=0, keepdims=True)
    dx = dn * gains[1:2, :]
    back_x = rstd * (
        dx - jnp.mean(dx, axis=-1, keepdims=True) - xhat * jnp.mean(dx * xhat, axis=-1, keepdims=True)
    )
    d_res = g_s[...] + back_x
    d_residual[...] = d_res
    low = d_res.astype(bf16)
    dat[...] = dot_nn(low, proj[...]).T.astype(bf16)
    d_mine[...] = dat[pl.ds(pl.multiple_of(core * OWN, 16), OWN), :]
    d_send[...] = dat[pl.ds(pl.multiple_of((1 - core) * OWN, 16), OWN), :]
    vec[7:8, :] = jnp.sum(low.astype(f32), axis=0, keepdims=True)
    grad_p[...] = dot_tn(low, att[...])
    p_keep[...] = grad_p[pl.ds(pl.multiple_of(core * OWN, 8), OWN), :]
    p_send[...] = grad_p[pl.ds(pl.multiple_of((1 - core) * OWN, 8), OWN), :].astype(bf16)


def branch(pos, own_a, cots, resid, att, proj, dn_one, dn_two, gains, vec, band_rows, grid_w):
    half = resid.shape[0]
    v = pltpu.VMEM
    outs = (
        sds((half, D), f32),
        sds((OWN, half), bf16),
        sds((OWN, half), bf16),
        sds((OWN, D), f32),
        sds((OWN, D), bf16),
        sds((16, D), f32),
    )
    body = functools.partial(branch_kernel, band_rows=band_rows, grid_w=grid_w)
    return kernel_call(body, outs, [v((half, D), f32), v((D, half), bf16), v((D, D), f32)], 1, 10)(
        pos, own_a, *cots, resid, att, proj, dn_one, dn_two, gains, vec
    )


def scores_kernel(which, q_aug, k_aug, k_nat, v_nat, logs, d_out, *refs):
    before, (dq, dk, dv) = refs[:-3], refs[-3:]
    half = d_out.shape[1]
    here = slice(which * half, (which + 1) * half)
    for h in range(OWN_HEADS):
        q_t = q_aug[h, :, here]
        g = d_out[h * HD : (h + 1) * HD, :]
        p = jnp.exp(dot_nn(k_nat[h], q_t) - logs[h, :, here])
        dp = dot_nn(v_nat[h], g)
        inner = jnp.sum(p * dp, axis=0, keepdims=True)
        ds = (p * (dp - inner)).astype(bf16)
        dv_one = dot_nt(g, p.astype(bf16))
        dk_one = dot_nt(q_t[0:HD, :], ds)
        dq[h] = dot_nn(k_aug[h, 0:HD, :], ds) * 0.125
        dk[h] = dk_one + before[0][h] if before else dk_one
        dv[h] = dv_one + before[1][h] if before else dv_one


def scores_back(which, q_aug, k_aug, k_nat, v_nat, logs, d_out, before=()):
    tokens = q_aug.shape[2]
    outs = (sds((OWN_HEADS, HD, tokens // 2), f32),) + (sds((OWN_HEADS, HD, tokens), f32),) * 2
    return kernel_call(functools.partial(scores_kernel, which), outs, (), 0, 6 + len(before), extra=28)(
        q_aug, k_aug, k_nat, v_nat, logs, d_out, *before
    )


def back_kernel(
    pos, normed, w_own, qrot, krot, dq_a, dq_b, dk, dv, cos, sin, rows, cols, own_a, own_b, oth_a, oth_b,
    qkv_mom, proj_mom, p_keep, p_recv, vec_in, vec_mom,
    out, s1, s2, s3, dn_own, dn_oth,
    dm, dm_full, freq, d_w, d_p, vec,
):
    core, band, chip, group = pos[0], pos[1], pos[2], pos[3]
    tokens = normed.shape[0]
    half = tokens // 2
    slab = half // 2
    dm_full[...] = jnp.zeros_like(dm_full)
    freq[...] = jnp.zeros_like(freq)
    for h in range(OWN_HEADS):
        c = cos[h * HALF : (h + 1) * HALF, :]
        s = sin[h * HALF : (h + 1) * HALF, :]
        angle = None
        d_query = jnp.concatenate([dq_a[h], dq_b[h]], axis=1)
        for which, source, rotated in ((0, d_query, qrot), (1, dk[h], krot)):
            du = source[0:HALF, :]
            dw = source[HALF:HD, :]
            u = rotated[h * HD : h * HD + HALF, :]
            w = rotated[h * HD + HALF : (h + 1) * HD, :]
            turn = dw * u - du * w
            angle = turn if angle is None else angle + turn
            at = which * OWN + h * HD
            dm[at : at + HD, :] = jnp.concatenate([du * c + dw * s, dw * c - du * s], axis=0).astype(bf16)
        at = pl.multiple_of(core * 96 + h * HALF, 32)
        freq[pl.ds(at, HALF), :] = jnp.sum(angle * rows[...], axis=1, keepdims=True)
        at = pl.multiple_of(192 + core * 96 + h * HALF, 32)
        freq[pl.ds(at, HALF), :] = jnp.sum(angle * cols[...], axis=1, keepdims=True)
        at = 2 * OWN + h * HD
        dm[at : at + HD, :] = dv[h].astype(bf16)
    for t in range(3):
        at = pl.multiple_of(t * D + core * OWN, 16)
        dm_full[pl.ds(at, OWN), :] = dm[t * OWN : (t + 1) * OWN, :]
    d_w[...] = dot_nn(dm[...], normed[...])
    for j in range(3):
        whole = band * 3 + j
        here = jnp.logical_and(lax.rem(whole, 4) // 2 == core, group == 0)
        at = pl.multiple_of(((whole // 4) * 2 + lax.rem(whole, 2)) * 96, 32)

        @pl.when(here)
        def _():
            d_w[pl.ds(at, 96), :] += 0.5 * qkv_mom[j * 96 : (j + 1) * 96, :]

    d_p[...] = p_keep[...] + p_recv[...].astype(f32)

    @pl.when(jnp.logical_and(band // 2 == core, group == 0))
    def _():
        d_p[pl.ds(pl.multiple_of(lax.rem(band, 2) * 96, 32), 96), :] += 0.5 * proj_mom[...]

    vec[...] = vec_in[...] + vec_mom[...]
    sums = dot_nt(jnp.ones((8, tokens), bf16), dm_full[...])
    for t in range(3):
        vec[4 + t : 5 + t, :] += sums[0:1, t * D : (t + 1) * D]
    vec[13:14, :] += jnp.broadcast_to(freq[...], (D, 128)).T[0:1, :]
    for b, src in enumerate((own_a, own_b, oth_a, oth_b)):
        part = dot_tn(dm[:, b * slab : (b + 1) * slab], w_own[...])
        xhat, _ = norm_rows(src[0:slab, :].astype(f32))
        vec[0:1, :] += jnp.sum(part * xhat, axis=0, keepdims=True)
        vec[2:3, :] += jnp.sum(part, axis=0, keepdims=True)
        to, at = (dn_own, b) if b < 2 else (dn_oth, b - 2)
        to[at * slab : (at + 1) * slab, :] = part.astype(to.dtype)
    low = vec[...].astype(bf16)
    for e, ref in enumerate((out, s1, s2, s3)):
        quarter = lax.bitwise_xor(chip, e)
        ref[0:144, :] = d_w[pl.ds(pl.multiple_of(quarter * 144, 16), 144), :].astype(bf16)
        ref[144:192, :] = d_p[pl.ds(pl.multiple_of(quarter * 48, 16), 48), :].astype(bf16)
        ref[192:208, :] = low


def back(pos, normed, w_own, qrot, krot, grads, cos, sin, rows, cols, slab_refs, moms, projs, vecs):
    tokens = normed.shape[0]
    half = tokens // 2
    outs = (sds((208, D), bf16),) * 4 + (sds((half, D), f32), sds((half, D), bf16))
    v = pltpu.VMEM
    scratch = [
        v((3 * OWN, tokens), bf16),
        v((3 * D, tokens), bf16),
        v((D, 1), f32),
        v((3 * OWN, D), f32),
        v((OWN, D), f32),
        v((16, D), f32),
    ]
    return kernel_call(back_kernel, outs, scratch, 1, 22, extra=10)(
        pos, normed, w_own, qrot, krot, *grads, cos, sin, rows, cols, *slab_refs, *moms, *projs, *vecs
    )


def tail_kernel(
    pos, own_a, own_b, d_residual, dn_one, dn_two, base, acc_two, gains, out_a, out_b, band_rows, grid_w
):
    slab = band_rows * grid_w
    for b, (src, out) in enumerate(((own_a, out_a), (own_b, out_b))):
        here = slice(b * slab, (b + 1) * slab)
        total = base[here, :] + acc_two[here, :].astype(f32)
        out[0:slab, :] = (total * valid_column(pos, own_a, b, band_rows, grid_w)).astype(bf16)
        xhat, rstd = norm_rows(src[0:slab, :].astype(f32))
        dx = (dn_one[here, :] + dn_two[here, :].astype(f32)) * gains[0:1, :]
        back_x = rstd * (
            dx - jnp.mean(dx, axis=-1, keepdims=True) - xhat * jnp.mean(dx * xhat, axis=-1, keepdims=True)
        )
        out[slab : 2 * slab, :] = (d_residual[here, :] + back_x).astype(bf16)


def tail(pos, own, d_residual, dn_one, dn_two, base, acc_two, gains, band_rows, grid_w):
    outs = (sds((2 * band_rows * grid_w, D), bf16),) * 2
    body = functools.partial(tail_kernel, band_rows=band_rows, grid_w=grid_w)
    return kernel_call(body, outs, (), 1, 8)(
        pos, *own, d_residual, dn_one, dn_two, base, acc_two, gains
    )


def place_kernel(pos, a, b, block_out, patch_grad):
    band = pos[1]
    slab = block_out.shape[1]
    for which, ref in ((0, a), (1, b)):
        image = lax.rem(band + which, 2)
        block_out[image] = ref[0:slab, :]
        patch_grad[image] = ref[slab : 2 * slab, :].astype(f32)


def place(pos, got):
    slab = got[0].shape[0] // 2
    outs = (sds((2, slab, D), bf16), sds((2, slab, D), f32))
    return kernel_call(place_kernel, outs, (), 1, 2)(pos, *got)


def bands_kernel(pos, mine, r1, r2, r3, own, s1, s2, s3):
    band = pos[1]
    for d, ref in ((0, own), (1, s1), (2, s2), (3, s3)):
        z = lax.bitwise_xor(band, d)
        part = (mine[z] + r1[z].astype(f32)) + (r2[z].astype(f32) + r3[z].astype(f32))
        ref[...] = part.astype(ref.dtype)


def bands(pos, mine, received):
    shape = mine.shape[1:]
    outs = (sds(shape, f32),) + (sds(shape, bf16),) * 3
    return kernel_call(bands_kernel, outs, (), 1, 4)(pos, mine, *received)


def piece_kernel(own, r1, r2, r3, mom, out):
    total = (own[...] + r1[...].astype(f32)) + (r2[...].astype(f32) + r3[...].astype(f32)) + 0.5 * mom[...]
    out[...] = total.astype(bf16)


def piece_sum(own, received, mom):
    return kernel_call(piece_kernel, sds(own.shape, bf16), (), 0, 5)(own, *received, mom)


def sum_low_kernel(own, r1, r2, r3, out):
    total = (own[...].astype(f32) + r1[...].astype(f32)) + (r2[...].astype(f32) + r3[...].astype(f32))
    out[...] = total.astype(bf16)


def sum_low(own, received):
    return kernel_call(sum_low_kernel, sds(own.shape, bf16), (), 0, 4)(own, *received)


def split_low(x):
    high = x.astype(bf16)
    return high, (x - high.astype(f32)).astype(bf16)


def dot_three_even(a, b):
    left = jnp.concatenate([a[0], a[0], a[1]], axis=1)
    right = jnp.concatenate([b[0], b[1], b[0]], axis=0)
    side = dot_nn(left, right[:, 0:256])
    low = dot_nn(left[256:], right[:, 256:])
    return jnp.concatenate([side, jnp.concatenate([side[256:].T, low], axis=0)], axis=1)


def sweeps(grams):
    row = lax.broadcasted_iota(jnp.int32, (D, D), 0)
    col = lax.broadcasted_iota(jnp.int32, (D, D), 1)
    eye = (row == col).astype(f32)
    scales, current, totals = [], [], [None] * len(grams)
    for gram in grams:
        trace = jnp.sum(jnp.sum(gram * eye, axis=1, keepdims=True), axis=0, keepdims=True)
        scales.append(1.0 / (jnp.sqrt(trace) + 1e-07))
        current.append(gram * (scales[-1] * scales[-1]))
    for sweep in range(5):
        parts = [split_low(a) for a in current]
        polys = [
            coeff_one * eye + coeff_two * a + coeff_three * dot_three_even(a2, a2) for a, a2 in zip(current, parts)
        ]
        halves = [split_low(poly) for poly in polys]
        if sweep < 4:
            turned = [dot_three_even(a2, p2) for a2, p2 in zip(parts, halves)]
        totals = [
            poly if total is None else dot_three_even(split_low(total), p2)
            for total, poly, p2 in zip(totals, polys, halves)
        ]
        if sweep < 4:
            current = [dot_three_even(split_low(t), p2) for t, p2 in zip(turned, halves)]
    return [total * scale for total, scale in zip(totals, scales)]


def gram_kernel(pos, a0, a1, a2, a3, keep, send, band_rows, shrink, expand):
    core, chip = pos[0], pos[2]
    for e, ref in enumerate((a0, a1, a2, a3)):
        for d in range(4):
            at = (e * 4 + d) * 48
            shrink[at : at + 48, :] = ref[d, 0:48, :]
            expand[at : at + 48, :] = ref[d, 48:96, :]
        at = pl.multiple_of(lax.bitwise_xor(chip, e) * 48, 16)
        band_rows[pl.ds(at, 48), :] = ref[0, 0:48, :]
        band_rows[pl.ds(pl.multiple_of(192 + at, 16), 48), :] = ref[0, 48:96, :]
    gram_s, gram_e = dot_tn(shrink[...], shrink[...]), dot_tn(expand[...], expand[...])
    keep[...] = jnp.where(core == 0, gram_s, gram_e)
    send[...] = jnp.where(core == 0, gram_e, gram_s)


def half_grams(pos, parts):
    outs = (sds((D, D), f32), sds((D, D), f32), sds((D, D), bf16))
    return kernel_call(gram_kernel, outs, [pltpu.VMEM((FF // 2, D), bf16)] * 2, 1, 4, extra=10)(pos, *parts)


def muon_kernel(pos, keep, recv, q0, q1, q2, q3, o0, o1, o2, o3, w0, w1, w2, w3, one_out, two_out, gram, rows):
    core = pos[0]
    pieces = (q0, q1, q2, q3, o0, o1, o2, o3)

    @pl.when(core == 0)
    def _():
        for e, ref in enumerate(pieces):
            rows[e * 144 : (e + 1) * 144, :] = ref[0:144, :]
        gram[...] = dot_tn(rows[...], rows[...])

    @pl.when(core != 0)
    def _():
        for e, ref in enumerate(pieces):
            rows[e * 48 : (e + 1) * 48, :] = ref[144:192, :]
        gram[...] = dot_tn(rows[0:D, :], rows[0:D, :])

    one, two = sweeps([keep[...] + recv[...], gram[...]])
    one_out[...] = one
    two_out[...] = two


def muon(pos, keep, recv, own_q, oth_q, weights):
    scratch = [pltpu.VMEM((D, D), f32), pltpu.VMEM((3 * D, D), bf16)]
    outs = (sds((D, D), f32),) * 2
    return kernel_call(muon_kernel, outs, scratch, 1, 14, extra=12)(pos, keep, recv, *own_q, *oth_q, *weights)


def final_kernel(
    pos, one, two, one_oth, two_oth, band_mine, band_oth, q0, q1, q2, q3, o0, o1, o2, o3,
    qkv_w, proj_w, expand_w, shrink_w,
    qkv_m, qkv_new, proj_m, proj_new, expand_m, expand_new, shrink_m, shrink_new,
    q_mine, q_oth, q_rows,
):
    core, band, chip = pos[0], pos[1], pos[2]
    first = core == 0

    def choose(when_first, a, b):
        return split_low(jnp.where(first == when_first, a[...], b[...]))

    for e in range(4):
        quarter = lax.bitwise_xor(chip, e)
        for refs, to in (((q0, q1, q2, q3), q_mine), ((o0, o1, o2, o3), q_oth)):
            to[pl.ds(pl.multiple_of(quarter * 144, 16), 144), :] = refs[e][0:144, :]
            to[pl.ds(pl.multiple_of(3 * OWN + quarter * 48, 16), 48), :] = refs[e][144:192, :]
    for j in range(4):
        whole = band * 3 + j
        at = pl.multiple_of(((whole // 4) * 2 + lax.rem(whole, 2)) * 96, 32)
        mine = lax.rem(whole, 4) // 2 == core
        if j == 3:
            at = pl.multiple_of(3 * OWN + lax.rem(band, 2) * 96, 32)
            mine = band // 2 == core

        @pl.when(mine)
        def _():
            q_rows[j * 96 : (j + 1) * 96, :] = q_mine[pl.ds(at, 96), :]

        @pl.when(jnp.logical_not(mine))
        def _():
            q_rows[j * 96 : (j + 1) * 96, :] = q_oth[pl.ds(at, 96), :]

    b_mine, b_oth = band_mine[...].astype(f32), band_oth[...].astype(f32)
    low_core, high_core = jnp.where(first, b_mine, b_oth), jnp.where(first, b_oth, b_mine)
    m_shrink = jnp.concatenate([low_core[0:192], high_core[0:192]], axis=0)
    m_expand = jnp.concatenate([low_core[192:], high_core[192:]], axis=0)
    t_shrink, t_expand = choose(True, one, one_oth), choose(False, one, one_oth)
    t_qkv, t_proj = choose(True, two, two_oth), choose(False, two, two_oth)
    for w, t, low, mom, new, size in (
        (qkv_w, t_qkv, q_rows[0:288, :], qkv_m, qkv_new, 3 * D),
        (proj_w, t_proj, q_rows[288:D, :], proj_m, proj_new, D),
        (shrink_w, t_shrink, m_shrink.astype(bf16), shrink_m, shrink_new, FF),
    ):
        mom[...] = low.astype(f32)
        new[...] = w[...] - 0.05 * math.sqrt(size) * (dot_nn(low, t[0]) + dot_nn(low, t[1]))
    low = m_expand.astype(bf16)
    expand_m[...] = m_expand.T
    expand_new[...] = expand_w[...] - 0.05 * math.sqrt(FF) * (dot_nt(t_expand[0], low) + dot_nt(t_expand[1], low))


def final(pos, turns, far_turns, band_mine, band_oth, own_q, oth_q, *weights):
    outs = []
    for w in weights:
        outs += [sds(w.shape, f32)] * 2
    v = pltpu.VMEM
    scratch = [v((4 * OWN, D), bf16), v((4 * OWN, D), bf16), v((D, D), bf16)]
    return kernel_call(final_kernel, tuple(outs), scratch, 1, 18, extra=10)(
        pos, *turns, *far_turns, band_mine, band_oth, *own_q, *oth_q, *weights
    )


def vector_kernel(pos, mine, other, gains, biases, freq, g_mom, g_new, b_mom, b_new, f_mom, f_new, mom, new):
    band = pos[1]
    n = mine.shape[0] - 16
    total = mine[n : n + 16, :].astype(f32) + other[n : n + 16, :].astype(f32)
    mom[...] = total
    new[...] = jnp.zeros_like(new)
    freqs = jnp.concatenate([freq[0:1, :], freq[1:2, :]], axis=1)
    for at, values in ((0, gains[...]), (2, biases[...]), (13, freqs)):
        here = slice(at, at + values.shape[0])
        part = total[here, :]
        square = jnp.sum(jnp.sum(part * part, axis=1, keepdims=True), axis=0, keepdims=True)
        new[here, :] = values - 0.2 * part * lax.rsqrt(square * (1.0 / (values.shape[0] * D)) + 1e-06)
    for whole, g_out, b_out, f_out in ((mom, g_mom, b_mom, f_mom), (new, g_new, b_new, f_new)):
        g_out[...] = pltpu.roll(whole[0:8, :], lax.rem(D - 96 * band, D), 1)[0:2, 0:96]
        rows = pltpu.roll(jnp.broadcast_to(whole[13:14, :], (8, D)), lax.rem(D - 48 * band, D), 1)
        f_out[...] = jnp.concatenate([rows[0:1, 0:48], rows[0:1, 192:240]], axis=0)
        blocks = []
        for i in range(11):
            block = 11 * band + i
            row = jnp.broadcast_to(whole[pl.ds(2 + block // 4, 1), :], (8, D))
            blocks.append(pltpu.roll(row, lax.rem(D - 96 * lax.rem(block, 4), D), 1)[0:1, 0:96])
        b_out[...] = jnp.concatenate(blocks, axis=1).reshape(b_out.shape)


def vector_step(pos, mine, other, gains, biases, freq):
    outs = (sds((2, 96), f32),) * 2 + (sds((11 * 96,), f32),) * 2 + (sds((2, 48), f32),) * 2
    scratch = [pltpu.VMEM((16, D), f32)] * 2
    return kernel_call(vector_kernel, outs, scratch, 1, 5, cost=10**10)(pos, mine, other, gains, biases, freq)


def flip(x, bit):
    n = lax.axis_size("batch")
    return lax.ppermute(x, "batch", [(i, i ^ bit) for i in range(n)])


def swap_bands(x, d):
    return lax.ppermute(x, "rows", [(i, i ^ d) for i in range(4)])


def moves(which):
    pairs = []
    for k in range(lax.axis_size("batch") // 2):
        for c in range(2):
            for i in range(4):
                band = (i - 2 * c - which) % 4
                pairs.append(((2 * k + i // 2) * 4 + band, (2 * k + c) * 4 + i))
    return pairs


def to_image(parts):
    return [lax.ppermute(parts[which], AXES, moves(which)) for which in range(2)]


def from_image(part, which):
    return lax.ppermute(part, AXES, [(b, a) for a, b in moves(which)])


def other_chips(x):
    bit = 8
    while bit < lax.axis_size("batch"):
        x = x + flip(x.astype(f32), bit).astype(x.dtype)
        bit *= 2
    return x


def over_chips(x):
    return [flip(x, 2 * e) for e in range(1, 4)]


def over_bands(x):
    return [swap_bands(x, d) for d in range(1, 4)]


def local(
    patches,
    cotangent,
    heights,
    widths,
    qkv_weight,
    qkv_moment,
    proj_weight,
    proj_moment,
    expand_weight,
    expand_moment,
    shrink_weight,
    shrink_moment,
    norm_gains,
    gains_moment,
    all_biases,
    biases_moment,
    frequencies,
    freq_moment,
):
    images, band_rows, grid_w, _ = patches.shape
    slab = band_rows * grid_w
    batch = lax.axis_index("batch")
    band = lax.axis_index("rows")
    core = batch % 2
    chip = (batch // 2) % 4
    pos = jnp.stack([core, band, chip, batch // 2]).astype(jnp.int32)
    grid = (band_rows, grid_w)

    share = own_weights(pos, qkv_weight.T, proj_weight.T, expand_weight, shrink_weight)
    shares = over_bands(share)
    p_a, p_b, c_a, c_b = slabs(
        pos, heights, widths, patches.reshape(images, slab, D), cotangent.reshape(images, slab, D)
    )
    own = to_image((p_a, p_b))
    oth = [flip(x, 1) for x in own]
    biases = all_biases.reshape(-1, D)
    cos, sin, rows_tok, cols_tok, bias_own, mom_big, vec_mom = setup(
        pos, frequencies, biases, expand_moment, shrink_moment,
        gains_moment, biases_moment.reshape(11, 96), freq_moment, 4 * slab, *grid,
    )
    shares, cos, vec_mom = lax.optimization_barrier((shares, cos, vec_mom))
    w_qkv, w_first, w_second = pack(share, shares)
    w_qkv = [w_qkv] + over_chips(w_qkv)
    w_first, oth = lax.optimization_barrier((w_first, oth))
    w_first = [w_first] + over_chips(w_first)
    c_a, c_b, w_second, w_qkv = lax.optimization_barrier((c_a, c_b, w_second, w_qkv))
    cot = to_image((c_a, c_b))
    w_second = [w_second] + over_chips(w_second)

    normed, w_own, qrot, krot, q_aug, k_aug, k_nat, v_nat, logs, *o_mine = front(
        pos, own + oth, w_qkv, bias_own, norm_gains, biases, cos, sin, rows_tok, cols_tok
    )
    o_oth = [flip(x, 1) for x in o_mine]
    cot, _ = lax.optimization_barrier((cot, o_mine))
    cot = cot + [flip(x, 1) for x in cot]
    resid, att, proj16, e_all, n2, hidden, slope = expand_layer(
        pos, own + oth, (*o_mine, *o_oth), w_first, norm_gains, biases, 2 * slab
    )
    g16, s_all, dpre, dn_two, dn_two_send = slope_layer(pos, own[0], cot, w_second, e_all, slope, *grid)
    base, acc_send, big, b1, b2, b3, vec = shrink_layer(pos, hidden, dpre, g16, n2, s_all, resid, biases)
    dn_two_recv, acc_recv = flip(dn_two_send, 1), flip(acc_send, 1)
    dn_two_recv, _ = lax.optimization_barrier((dn_two_recv, acc_recv))
    big_chips = [flip(x, 2 * e) for e, x in zip((1, 2, 3), (b1, b2, b3))]
    d_residual, d_mine, d_send, p_keep, p_send, vec = branch(
        pos, own[0], cot[:2], resid, att, proj16, dn_two, dn_two_recv, norm_gains, vec, *grid
    )
    d_recv = flip(d_send, 1)
    p_recv = flip(p_send, 1)
    dq_a, dk, dv = scores_back(0, q_aug, k_aug, k_nat, v_nat, logs, d_mine)
    dq_b, dk, dv = scores_back(1, q_aug, k_aug, k_nat, v_nat, logs, d_recv, (dk, dv))

    big, dq_b = lax.optimization_barrier((big, dq_b))
    own_big, *to_bands = bands(pos, other_chips(big), big_chips)
    to_bands, dq_b, acc_recv = lax.optimization_barrier((to_bands, dq_b, acc_recv))
    from_bands = [swap_bands(x, d) for d, x in zip((1, 2, 3), to_bands)]
    q_mine, *q_sends, dn_own, dn_oth = back(
        pos, normed, w_own, qrot, krot, (dq_a, dq_b, dk, dv), cos, sin, rows_tok, cols_tok, own + oth,
        (qkv_moment.T, proj_moment.T), (p_keep, p_recv), (vec, vec_mom),
    )
    dn_recv = flip(dn_oth, 1)
    big_piece = piece_sum(own_big, from_bands, mom_big)
    q_sends, big_piece = lax.optimization_barrier((q_sends, big_piece))

    q_low = other_chips(sum_low(q_mine, [flip(x, 2 * e) for e, x in zip((1, 2, 3), q_sends)]))
    big_bands = jnp.stack([big_piece, swap_bands(big_piece, 1)])
    big_bands = jnp.concatenate([big_bands, swap_bands(big_bands, 2)])
    big_bands, q_low = lax.optimization_barrier((big_bands, q_low))
    big_all = [big_bands] + over_chips(big_bands)
    q_recv = over_bands(q_low)
    results = tail(pos, own, d_residual, dn_own, dn_recv, base, acc_recv, norm_gains, *grid)
    q_recv, results = lax.optimization_barrier((q_recv, results))
    q_piece = sum_low(q_low, q_recv)
    big_all, q_piece = lax.optimization_barrier((big_all, q_piece))
    own_q = [q_piece] + over_chips(q_piece)
    oth_q = [flip(x, 1) for x in own_q]

    gram_keep, gram_send, band_mine = half_grams(pos, big_all)
    image_a, image_b = from_image(results[0], 0), from_image(results[1], 1)
    weights = (qkv_weight.T, proj_weight.T, expand_weight, shrink_weight)
    turns = muon(pos, gram_keep, flip(gram_send, 1), own_q, oth_q, weights)
    images_back = [from_image(part, which) for which, part in enumerate(results)]
    images_back, _ = lax.optimization_barrier((images_back, turns))
    block_out, patch_grad = place(pos, images_back)
    vec_q, block_out = lax.optimization_barrier((own_q[0], block_out))
    vector_steps = vector_step(pos, vec_q, oth_q[0], norm_gains, biases, frequencies)
    shape = (images, band_rows, grid_w, D)
    block_out, patch_grad = block_out.reshape(shape), patch_grad.reshape(shape)
    far_turns, band_oth = [flip(x, 1) for x in turns], flip(band_mine, 1)
    far_turns, block_out, vector_steps = lax.optimization_barrier((far_turns, block_out, vector_steps))
    new = final(pos, turns, far_turns, band_mine, band_oth, own_q, oth_q, *weights)
    new = [x.T for x in new[:4]] + list(new[4:])

    return (block_out, patch_grad) + tuple(new) + tuple(vector_steps)


def solution(mesh):
    image = P("batch", "rows", None, None)
    cols, rows = P(None, "rows"), P("rows", None)
    return jax.shard_map(
        local,
        mesh=mesh,
        in_specs=(
            image, image, P("batch"), P("batch"), cols, cols, cols, cols, cols, cols, rows, rows,
            P(), cols, P(), P("rows"), P(), cols,
        ),
        out_specs=(
            image, image, cols, cols, cols, cols, cols, cols, rows, rows, cols, cols, P("rows"), P("rows"), cols, cols,
        ),
        check_vma=False,
    )
```

```python
import functools
import math

import jax
import jax.numpy as jnp
from jax import lax
from jax.experimental import pallas as pl
from jax.experimental.pallas import tpu as pltpu
from jax.sharding import PartitionSpec as P

D = 384
H = 6
HD = 64
FF = 1536
HALF = HD // 2
OWN_HEADS = H // 2
OWN = OWN_HEADS * HD
AUG = HD + 16

coeff_one = 3.4445
coeff_two = -4.775
coeff_three = 2.0315

bf16 = jnp.bfloat16
f32 = jnp.float32
AXES = ("batch", "rows")


def dot_nn(a, b):
    return lax.dot_general(a, b, (((1,), (0,)), ((), ())), preferred_element_type=f32)


def dot_nt(a, b):
    return lax.dot_general(a, b, (((1,), (1,)), ((), ())), preferred_element_type=f32)


def dot_tn(a, b):
    return lax.dot_general(a, b, (((0,), (0,)), ((), ())), preferred_element_type=f32)


def vmem_bytes(x):
    *lead, rows, lanes = (1,) * max(0, 2 - len(x.shape)) + tuple(x.shape)
    size = jnp.dtype(x.dtype).itemsize
    tile = 8 * 4 // size
    return math.prod(lead) * (-(-rows // tile) * tile) * (-(-lanes // 128) * 128) * size


def kernel_call(body, out_shape, scratch=(), smem=0, n_in=0, extra=4, cost=None):
    specs = [pl.BlockSpec(memory_space=pltpu.SMEM)] * smem
    specs += [pl.BlockSpec(memory_space=pltpu.VMEM)] * n_in

    def call(*args):
        held = list(args[smem:]) + jax.tree.leaves(out_shape) + [s for s in scratch]
        limit = sum(vmem_bytes(x) for x in held) + extra * 2**20
        return pl.pallas_call(
            body,
            out_shape=out_shape,
            in_specs=specs,
            out_specs=jax.tree.map(lambda _: pl.BlockSpec(memory_space=pltpu.VMEM), out_shape),
            scratch_shapes=list(scratch),
            compiler_params=pltpu.CompilerParams(vmem_limit_bytes=int(limit)),
            cost_estimate=cost and pl.CostEstimate(flops=cost, bytes_accessed=0, transcendentals=0),
        )(*args)

    return call


def sds(shape, dtype):
    return jax.ShapeDtypeStruct(shape, dtype)


def norm_rows(x):
    centered = x - jnp.mean(x, axis=-1, keepdims=True)
    rstd = lax.rsqrt(jnp.mean(centered * centered, axis=-1, keepdims=True) + 1e-06)
    return centered * rstd, rstd


i16 = jnp.int16
STEPS = 32000.0


def as_row(column):
    n = column.shape[0]
    row = jnp.broadcast_to(column, (n, 128)).T[0:1, :]
    return row if n == D else jnp.concatenate([row, jnp.zeros((1, D - n), f32)], axis=1)


def coded(x):
    top = jnp.maximum(jnp.max(jnp.abs(x), axis=1, keepdims=True), 1e-30)
    power = jnp.floor(jnp.log(top) * 1.4426950408889634 + 1.01)
    steps = jnp.floor(x * (STEPS / jnp.exp2(power)) + 0.5)
    return jnp.clip(steps, -32767.0, 32767.0), power


def decoded(codes, power):
    return codes.astype(jnp.int32).astype(f32) * (jnp.exp2(power) * (1.0 / STEPS))


def whole16(x):
    return x.astype(jnp.int32).astype(i16)


def write_rows(out, x):
    n = x.shape[0]
    codes, power = coded(x)
    out[0:n, :] = whole16(codes)
    out[n : n + 16, :] = whole16(jnp.broadcast_to(as_row(power), (16, D)))


def write_bundle(out, x):
    codes, power = coded(x)
    row = lax.broadcasted_iota(jnp.int32, (16, D), 0)
    out[0:192, :] = whole16(codes[0:192])
    out[192:208, :] = whole16(jnp.where(row == 15, as_row(power), codes[192:208]))


def columns(rows):
    rows = list(rows)
    turned = jnp.concatenate(rows + [jnp.zeros((128 - len(rows), D), f32)], axis=0).T
    return [turned[:, i : i + 1] for i in range(len(rows))]


def message_powers(refs):
    tiles = [ref[ref.shape[0] - 16 :, :].astype(jnp.int32).astype(f32) for ref in refs]
    return columns(tile[0:1, :] for tile in tiles)


def bundle_powers(refs):
    return columns(ref[192:208, :].astype(jnp.int32).astype(f32)[15:16, :] for ref in refs)


def weights_kernel(pos, qkv_t, proj_t, expand, shrink, out, q_s, p_s, e_s, s_s, sem_q, sem_p, sem_e, sem_s):
    core, band, chip = pos[0], pos[1], pos[2]
    start = jnp.where(core == 0, jnp.where(band < 3, 2 * band, 0), jnp.where(band == 0, 4, jnp.where(band == 3, 2, 0)))
    count = jnp.where((core == 0) == (band < 2), 4, 2)
    at_q = pl.multiple_of((start + jnp.minimum(chip, count - 1)) * 48, 8)
    at_p = pl.multiple_of(jnp.minimum(chip, 2) * 32, 8)
    at = pl.multiple_of(core * 192 + chip * 48, 8)
    copies = (
        pltpu.make_async_copy(expand, e_s, sem_e),
        pltpu.make_async_copy(qkv_t.at[pl.ds(at_q, 48), :], q_s, sem_q),
        pltpu.make_async_copy(proj_t.at[pl.ds(at_p, 32), :], p_s, sem_p),
        pltpu.make_async_copy(shrink.at[pl.ds(at, 48), :], s_s, sem_s),
    )
    for copy in copies:
        copy.start()
    for copy in copies[1:]:
        copy.wait()
    out[0:48, :] = q_s[...].astype(bf16)
    out[48:80, :] = p_s[...].astype(bf16)
    out[128:176, :] = s_s[...].astype(bf16)
    copies[0].wait()
    e_s[...] = e_s[...].T
    out[80:128, :] = e_s[pl.ds(at, 48), :].astype(bf16)


def own_weights(pos, qkv_t, proj_t, expand, shrink):
    v = pltpu.VMEM
    dma = pltpu.SemaphoreType.DMA
    scratch = [v((48, D), f32), v((32, D), f32), v((D, D), f32), v((48, D), f32), dma, dma, dma, dma]
    hbm = pl.BlockSpec(memory_space=pltpu.HBM)
    return pl.pallas_call(
        weights_kernel,
        out_shape=sds((176, D), bf16),
        in_specs=[pl.BlockSpec(memory_space=pltpu.SMEM)] + [hbm] * 4,
        out_specs=pl.BlockSpec(memory_space=pltpu.VMEM),
        scratch_shapes=scratch,
        compiler_params=pltpu.CompilerParams(vmem_limit_bytes=56 * 2**20),
    )(pos, qkv_t, proj_t, expand, shrink)


def slabs_kernel(pos, heights, widths, patches, cot, p_a, p_b, c_a, c_b):
    band = pos[1]
    slab = patches.shape[1]
    row = lax.broadcasted_iota(jnp.int32, (16, D), 0)
    for which, (p, c) in enumerate(((p_a, c_a), (p_b, c_b))):
        image = lax.rem(band + which, 2)
        p[0:slab, :] = patches[image]
        size = jnp.where(row == 0, heights[image], widths[image])
        p[slab : slab + 16, :] = size.astype(f32).astype(bf16)
        c[...] = cot[image]


def slabs(pos, heights, widths, patches, cot):
    slab = patches.shape[1]
    outs = (sds((slab + 16, D), bf16),) * 2 + (sds((slab, D), bf16),) * 2
    return kernel_call(slabs_kernel, outs, (), 3, 2)(pos, heights, widths, patches, cot)


def setup_kernel(
    pos, freq, biases, expand_mom, shrink_mom, gains_mom, biases_mom, freq_mom,
    cos, sin, rows, cols, bias_own, mom_big, vec,
    column, turned, freq_one, freq_two, band_rows, grid_w,
):
    core, band, chip, group = pos[0], pos[1], pos[2], pos[3]
    tokens = rows.shape[1]
    slab = band_rows * grid_w
    token = lax.broadcasted_iota(jnp.int32, (1, tokens), 1)
    slot = token // slab
    d = jnp.where(slot < 2, 2 * core + slot, 2 - 2 * core + slot - 2)
    row = lax.bitwise_and(band + 4 - d, 3) * band_rows + lax.rem(token, slab) // grid_w
    rows[...] = row.astype(f32)
    cols[...] = lax.rem(token, grid_w).astype(f32)
    own = pl.ds(pl.multiple_of(core * 96, 8), 96)
    freq_one[...] = jnp.broadcast_to(freq[0:1, :], (128, H * HALF)).T
    freq_two[...] = jnp.broadcast_to(freq[1:2, :], (128, H * HALF)).T
    angle = freq_one[own, 0:1] * rows[...] + freq_two[own, 0:1] * cols[...]
    cos[...] = jnp.cos(angle)
    sin[...] = jnp.sin(angle)
    for t in range(3):
        column[...] = jnp.broadcast_to(biases[2 + t : 3 + t, :], (128, D)).T
        at = pl.multiple_of(core * OWN, 8)
        bias_own[t * OWN : (t + 1) * OWN, :] = column[pl.ds(at, OWN), 0:1]
    at = pl.multiple_of(core * 192 + chip * 48, 8)
    mom_big[0:48, :] = shrink_mom[pl.ds(at, 48), :]
    turned[...] = expand_mom[...].T
    mom_big[48:96, :] = turned[pl.ds(at, 48), :]
    share = jnp.where(jnp.logical_and(core == 0, group == 0), 0.5, 0.0)
    vec[...] = jnp.zeros_like(vec)
    none = jnp.zeros((8, 144), f32)

    def wide(x, lanes):
        return jnp.concatenate([x, jnp.zeros((x.shape[0], lanes), f32)], axis=1)

    gains = jnp.concatenate([wide(gains_mom[...], 288), jnp.zeros((6, D), f32)], axis=0)
    vec[0:2, :] = share * pltpu.roll(gains, 96 * band, 1)[0:2, :]
    freqs = jnp.concatenate([freq_mom[0:1, :], none[0:1], freq_mom[1:2, :], none[0:1]], axis=1)
    vec[13:14, :] = share * pltpu.roll(jnp.broadcast_to(freqs, (8, D)), 48 * band, 1)[0:1, :]
    for i in range(11):
        block = 11 * band + i
        line = jnp.broadcast_to(wide(biases_mom[i : i + 1, :], 288), (8, D))
        vec[pl.ds(2 + block // 4, 1), :] += share * pltpu.roll(line, 96 * lax.rem(block, 4), 1)[0:1, :]


def setup(pos, freq, biases, expand_mom, shrink_mom, gains_mom, biases_mom, freq_mom, tokens, band_rows, grid_w):
    v = pltpu.VMEM
    outs = (
        sds((96, tokens), f32),
        sds((96, tokens), f32),
        sds((1, tokens), f32),
        sds((1, tokens), f32),
        sds((3 * OWN, 1), f32),
        sds((96, D), f32),
        sds((16, D), f32),
    )
    scratch = [v((D, 128), f32), v((D, D), f32), v((H * HALF, 128), f32), v((H * HALF, 128), f32)]
    body = functools.partial(setup_kernel, band_rows=band_rows, grid_w=grid_w)
    return kernel_call(body, outs, scratch, 1, 7)(
        pos, freq, biases, expand_mom, shrink_mom, gains_mom, biases_mom, freq_mom
    )


def pack_kernel(own, r1, r2, r3, qkv, first, second):
    for d, ref in enumerate((own, r1, r2, r3)):
        qkv[d] = ref[0:48, :]
        first[d] = ref[48:128, :]
        second[d] = ref[128:176, :]


def pack(own, received):
    outs = (sds((4, 48, D), bf16), sds((4, 80, D), bf16), sds((4, 48, D), bf16))
    return kernel_call(pack_kernel, outs, (), 0, 4)(own, *received)


def front_kernel(
    pos, own_a, own_b, oth_a, oth_b, w0, w1, w2, w3, bias, gains, biases, cos, sin, rows, cols,
    normed, w_own, qrot, krot, q_aug, k_aug, k_nat, v_nat, logs, o_own, o_oth,
    w_all, v_t, o_all,
):
    core, band, chip = pos[0], pos[1], pos[2]
    tokens = normed.shape[0]
    block = tokens // 4
    for e, ref in enumerate((w0, w1, w2, w3)):
        quarter = lax.bitwise_xor(chip, e)
        for shard in range(4):
            base = jnp.where(core == 0, (0, 4, 8, 10)[shard], (0, 2, 4, 8)[shard])
            count = jnp.where(core == 0, (4, 4, 2, 2)[shard], (2, 2, 4, 4)[shard])
            at = jnp.where(quarter < count, base + quarter, 12)
            w_all[pl.ds(pl.multiple_of(at * 48, 16), 48), :] = ref[lax.bitwise_xor(band, shard)]
    w_own[...] = w_all[0 : 3 * OWN, :]
    for b, src in enumerate((own_a, own_b, oth_a, oth_b)):
        xhat, _ = norm_rows(src[0:block, :].astype(f32))
        normed[b * block : (b + 1) * block, :] = (xhat * gains[0:1, :] + biases[0:1, :]).astype(bf16)
    high = own_a[block : block + 1, 0:1].astype(f32)
    wide = own_a[block + 1 : block + 2, 0:1].astype(f32)
    inside = jnp.logical_and(rows[...] < high, cols[...] < wide)
    key_bias = jnp.where(inside, 0.0, -1e9).astype(f32)
    ones_row = (lax.broadcasted_iota(jnp.int32, (AUG - HD, block), 0) == 0).astype(f32)
    for b in range(4):
        here = slice(b * block, (b + 1) * block)
        mixed = dot_nt(w_own[...], normed[here, :]) + bias[...]
        for h in range(OWN_HEADS):
            c = cos[h * HALF : (h + 1) * HALF, here]
            s = sin[h * HALF : (h + 1) * HALF, here]
            qu = mixed[h * HD : h * HD + HALF, :]
            qw = mixed[h * HD + HALF : (h + 1) * HD, :]
            ku = mixed[OWN + h * HD : OWN + h * HD + HALF, :]
            kw = mixed[OWN + h * HD + HALF : OWN + (h + 1) * HD, :]
            qr = jnp.concatenate([qu * c - qw * s, qw * c + qu * s], axis=0)
            kr = jnp.concatenate([ku * c - kw * s, kw * c + ku * s], axis=0)
            qrot[h * HD : (h + 1) * HD, here] = qr
            krot[h * HD : (h + 1) * HD, here] = kr
            q_low = qr.astype(bf16).astype(f32) * 0.125
            q_aug[h, :, here] = jnp.concatenate([q_low, ones_row], axis=0).astype(bf16)
            k_full = jnp.concatenate([kr, ones_row * key_bias[:, here]], axis=0)
            k_aug[h, :, here] = k_full.astype(bf16)
            k_nat[h, here, :] = k_full.T.astype(bf16)
            vv = mixed[2 * OWN + h * HD : 2 * OWN + (h + 1) * HD, :]
            v_t[h, :, here] = vv.astype(bf16)
            v_nat[h, here, :] = vv.T.astype(bf16)

    half = tokens // 2

    def attend(item, carry):
        here = pl.ds(pl.multiple_of(item * half, half), half)
        scores = [dot_nn(k_nat[h], q_aug[h, :, here]) for h in range(OWN_HEADS)]
        for h in range(OWN_HEADS):
            peak = jnp.max(scores[h], axis=0, keepdims=True)
            e = jnp.exp(scores[h] - peak)
            total = jnp.sum(e, axis=0, keepdims=True)
            out = dot_nn(v_t[h], (e * (1.0 / total)).astype(bf16))
            logs[h, :, here] = peak + jnp.log(total)
            o_all[h * HD : (h + 1) * HD, here] = out.astype(bf16)
        return carry

    lax.fori_loop(0, 2, attend, 0)
    o_own[...] = o_all[:, 0:half]
    o_oth[...] = o_all[:, half:tokens]


def front(pos, slab_refs, weights, bias, gains, biases, cos, sin, rows, cols):
    tokens = rows.shape[1]
    nh = OWN_HEADS
    outs = (
        sds((tokens, D), bf16),
        sds((3 * OWN, D), bf16),
        sds((OWN, tokens), f32),
        sds((OWN, tokens), f32),
        sds((nh, AUG, tokens), bf16),
        sds((nh, AUG, tokens), bf16),
        sds((nh, tokens, AUG), bf16),
        sds((nh, tokens, HD), bf16),
        sds((nh, 1, tokens), f32),
        sds((OWN, tokens // 2), bf16),
        sds((OWN, tokens // 2), bf16),
    )
    scratch = [
        pltpu.VMEM((3 * OWN + 48, D), bf16),
        pltpu.VMEM((nh, HD, tokens), bf16),
        pltpu.VMEM((OWN, tokens), bf16),
    ]
    return kernel_call(front_kernel, outs, scratch, 1, 15, extra=24)(
        pos, *slab_refs, *weights, bias, gains, biases, cos, sin, rows, cols
    )


def valid_column(pos, sized, first_slot, band_rows, grid_w):
    core, band = pos[0], pos[1]
    slab = band_rows * grid_w
    d = 2 * core + first_slot if first_slot < 2 else 2 - 2 * core + first_slot - 2
    token = lax.broadcasted_iota(jnp.int32, (slab, 1), 0)
    row = lax.bitwise_and(band + 4 - d, 3) * band_rows + token // grid_w
    col = lax.rem(token, grid_w)
    high = sized[slab : slab + 1, 0:1].astype(f32)
    wide = sized[slab + 1 : slab + 2, 0:1].astype(f32)
    return jnp.logical_and(row.astype(f32) < high, col.astype(f32) < wide).astype(f32)


def expand_kernel(
    pos, own_a, own_b, oth_a, oth_b, mine_a, mine_b, far_a, far_b, w0, w1, w2, w3, gains, biases,
    resid_own, att_own, proj_out, e_all, n2, hidden, slope,
    p_all,
):
    core, band, chip = pos[0], pos[1], pos[2]
    half = resid_own.shape[0]
    slab = half // 2
    first = core == 0
    for e, ref in enumerate((w0, w1, w2, w3)):
        quarter = lax.bitwise_xor(chip, e)
        for shard in range(4):
            d = lax.bitwise_xor(band, shard)
            at = jnp.where(quarter < 3, shard * 96 + quarter * 32, D)
            p_all[pl.ds(pl.multiple_of(at, 16), 32), :] = ref[d, 0:32, :]
            at = pl.multiple_of(shard * 192 + quarter * 48, 16)
            e_all[pl.ds(at, 48), :] = ref[d, 32:80, :]
    proj = p_all[0:D, :]
    proj_out[...] = proj
    bias = jnp.concatenate(
        [jnp.where(first, biases[6 + s : 7 + s, 0:192], biases[6 + s : 7 + s, 192:384]) for s in range(4)], axis=1
    )
    for b, src in enumerate((own_a, own_b, oth_a, oth_b)):
        here = slice(b * slab, (b + 1) * slab)
        there = slice((b % 2) * slab, (b % 2 + 1) * slab)
        m, o = (mine_a, far_b) if b < 2 else (mine_b, far_a)
        m, o = m[:, there].astype(f32), o[:, there].astype(f32)
        att = jnp.concatenate([jnp.where(first, m, o), jnp.where(first, o, m)], axis=0).T.astype(bf16)
        res = src[0:slab, :].astype(f32) + dot_nt(att, proj) + biases[5:6, :]
        if b < 2:
            resid_own[here, :] = res
            att_own[here, :] = att
        xhat, _ = norm_rows(res)
        n2[here, :] = (xhat * gains[1:2, :] + biases[1:2, :]).astype(bf16)

    def part(b, carry):
        here = pl.ds(pl.multiple_of(b * slab, slab), slab)
        pre = dot_nt(n2[here, :], e_all[...]) + bias
        cdf = 0.5 * (1.0 + lax.erf(pre * math.sqrt(0.5)))
        hidden[here, :] = (pre * cdf).astype(bf16)
        slope[here, :] = cdf + pre * (jnp.exp(-0.5 * pre * pre) * (1.0 / math.sqrt(2.0 * math.pi)))
        return carry

    lax.fori_loop(0, 4, part, 0)


def expand_layer(pos, slab_refs, att, weights, gains, biases, half):
    v = pltpu.VMEM
    outs = (
        sds((half, D), f32),
        sds((half, D), bf16),
        sds((D, D), bf16),
        sds((FF // 2, D), bf16),
        sds((2 * half, D), bf16),
        sds((2 * half, FF // 2), bf16),
        sds((2 * half, FF // 2), f32),
    )
    return kernel_call(expand_kernel, outs, [v((D + 32, D), bf16)], 1, 14, extra=12)(
        pos, *slab_refs, *att, *weights, gains, biases
    )


def slope_kernel(
    pos, own_a, cot_a, cot_b, cot_c, cot_d, w0, w1, w2, w3, e_all, slope, g16, s_all, dpre, dn_own, dn_send,
    band_rows, grid_w,
):
    core, band, chip = pos[0], pos[1], pos[2]
    slab = band_rows * grid_w
    for e, ref in enumerate((w0, w1, w2, w3)):
        quarter = lax.bitwise_xor(chip, e)
        for shard in range(4):
            at = pl.multiple_of(shard * 192 + quarter * 48, 16)
            s_all[pl.ds(at, 48), :] = ref[lax.bitwise_xor(band, shard)]
    for b, cot in enumerate((cot_a, cot_b, cot_c, cot_d)):
        here = slice(b * slab, (b + 1) * slab)
        g16[here, :] = (cot[...].astype(f32) * valid_column(pos, own_a, b, band_rows, grid_w)).astype(bf16)
    for b in range(4):
        here = slice(b * slab, (b + 1) * slab)
        dpre[here, :] = (dot_nt(g16[here, :], s_all[...]) * slope[here, :]).astype(bf16)
    half = 2 * slab
    dn_send[...] = dot_nn(dpre[half : 2 * half, :], e_all[...]).astype(bf16)
    dn_own[...] = dot_nn(dpre[0:half, :], e_all[...])


def slope_layer(pos, own_a, cots, weights, e_all, slope, band_rows, grid_w):
    half = 2 * band_rows * grid_w
    outs = (
        sds((2 * half, D), bf16),
        sds((FF // 2, D), bf16),
        sds((2 * half, FF // 2), bf16),
        sds((half, D), f32),
        sds((half, D), bf16),
    )
    body = functools.partial(slope_kernel, band_rows=band_rows, grid_w=grid_w)
    return kernel_call(body, outs, (), 1, 11, extra=10)(pos, own_a, *cots, *weights, e_all, slope)


def shrink_kernel(pos, hidden, dpre, g16, n2, s_all, resid, biases, base, acc_send, mine, s1, s2, s3, vec, grads, part):
    core, chip = pos[0], pos[2]
    half = base.shape[0]
    first = core == 0
    grads[0] = dot_tn(hidden[...], g16[...])
    grads[1] = dot_tn(dpre[...], n2[...])
    for e, ref in ((0, mine), (1, s1), (2, s2), (3, s3)):
        for z in range(4):
            at = pl.ds(pl.multiple_of(z * 192 + lax.bitwise_xor(chip, e) * 48, 16), 48)
            part[z * 96 : z * 96 + 48, :] = grads[0, at, :]
            part[z * 96 + 48 : z * 96 + 96, :] = grads[1, at, :]
        if e == 0:
            for z in range(4):
                ref[z] = part[z * 96 : (z + 1) * 96, :]
        else:
            write_rows(ref, part[...])
    base[...] = resid[...] + dot_nn(hidden[0:half, :], s_all[...]) + biases[10:11, :]
    acc_send[...] = dot_nn(hidden[half : 2 * half, :], s_all[...]).astype(bf16)
    vec[...] = jnp.zeros_like(vec)
    sums = dot_nn(jnp.ones((8, 2 * half), bf16), dpre[...])
    none = jnp.zeros((1, 192), f32)
    for s in range(4):
        x = sums[0:1, s * 192 : (s + 1) * 192]
        vec[8 + s : 9 + s, :] = jnp.where(
            first, jnp.concatenate([x, none], axis=1), jnp.concatenate([none, x], axis=1)
        )
    vec[12:13, :] = jnp.sum(g16[0:half, :].astype(f32), axis=0, keepdims=True)


def shrink_layer(pos, hidden, dpre, g16, n2, s_all, resid, biases):
    half = g16.shape[0] // 2
    outs = (
        sds((half, D), f32),
        sds((half, D), bf16),
        sds((4, 96, D), f32),
        sds((400, D), i16),
        sds((400, D), i16),
        sds((400, D), i16),
        sds((16, D), f32),
    )
    return kernel_call(shrink_kernel, outs, [pltpu.VMEM((2, FF // 2, D), f32), pltpu.VMEM((D, D), f32)], 1, 7, extra=10)(
        pos, hidden, dpre, g16, n2, s_all, resid, biases
    )


def branch_kernel(
    pos, own_a, cot_a, cot_b, resid, att, proj, dn_one, dn_two, gains, vec_in,
    d_residual, d_mine, d_send, p_keep, p_send, vec,
    g_s, dat, grad_p, band_rows, grid_w,
):
    core = pos[0]
    slab = band_rows * grid_w
    for b, cot in enumerate((cot_a, cot_b)):
        here = slice(b * slab, (b + 1) * slab)
        g_s[here, :] = cot[...].astype(f32) * valid_column(pos, own_a, b, band_rows, grid_w)
    vec[...] = vec_in[...]
    xhat, rstd = norm_rows(resid[...])
    dn = dn_one[...] + dn_two[...].astype(f32)
    vec[3:4, :] = jnp.sum(dn, axis=0, keepdims=True)
    vec[1:2, :] = jnp.sum(dn * xhat, axis=0, keepdims=True)
    dx = dn * gains[1:2, :]
    back_x = rstd * (
        dx - jnp.mean(dx, axis=-1, keepdims=True) - xhat * jnp.mean(dx * xhat, axis=-1, keepdims=True)
    )
    d_res = g_s[...] + back_x
    d_residual[...] = d_res
    low = d_res.astype(bf16)
    dat[...] = dot_nn(low, proj[...]).T.astype(bf16)
    d_mine[...] = dat[pl.ds(pl.multiple_of(core * OWN, 16), OWN), :]
    d_send[...] = dat[pl.ds(pl.multiple_of((1 - core) * OWN, 16), OWN), :]
    vec[7:8, :] = jnp.sum(low.astype(f32), axis=0, keepdims=True)
    grad_p[...] = dot_tn(low, att[...])
    p_keep[...] = grad_p[pl.ds(pl.multiple_of(core * OWN, 8), OWN), :]
    p_send[...] = grad_p[pl.ds(pl.multiple_of((1 - core) * OWN, 8), OWN), :]


def branch(pos, own_a, cots, resid, att, proj, dn_one, dn_two, gains, vec, band_rows, grid_w):
    half = resid.shape[0]
    v = pltpu.VMEM
    outs = (
        sds((half, D), f32),
        sds((OWN, half), bf16),
        sds((OWN, half), bf16),
        sds((OWN, D), f32),
        sds((OWN, D), f32),
        sds((16, D), f32),
    )
    body = functools.partial(branch_kernel, band_rows=band_rows, grid_w=grid_w)
    return kernel_call(body, outs, [v((half, D), f32), v((D, half), bf16), v((D, D), f32)], 1, 10)(
        pos, own_a, *cots, resid, att, proj, dn_one, dn_two, gains, vec
    )


def scores_kernel(which, q_aug, k_aug, k_nat, v_nat, logs, d_out, *refs):
    before, (dq, dk, dv) = refs[:-3], refs[-3:]
    half = d_out.shape[1]
    here = slice(which * half, (which + 1) * half)
    for h in range(OWN_HEADS):
        q_t = q_aug[h, :, here]
        g = d_out[h * HD : (h + 1) * HD, :]
        p = jnp.exp(dot_nn(k_nat[h], q_t) - logs[h, :, here])
        dp = dot_nn(v_nat[h], g)
        inner = jnp.sum(p * dp, axis=0, keepdims=True)
        ds = (p * (dp - inner)).astype(bf16)
        dv_one = dot_nt(g, p.astype(bf16))
        dk_one = dot_nt(q_t[0:HD, :], ds)
        dq[h] = dot_nn(k_aug[h, 0:HD, :], ds) * 0.125
        dk[h] = dk_one + before[0][h] if before else dk_one
        dv[h] = dv_one + before[1][h] if before else dv_one


def scores_back(which, q_aug, k_aug, k_nat, v_nat, logs, d_out, before=()):
    tokens = q_aug.shape[2]
    outs = (sds((OWN_HEADS, HD, tokens // 2), f32),) + (sds((OWN_HEADS, HD, tokens), f32),) * 2
    return kernel_call(functools.partial(scores_kernel, which), outs, (), 0, 6 + len(before), extra=28)(
        q_aug, k_aug, k_nat, v_nat, logs, d_out, *before
    )


def back_kernel(
    pos, normed, w_own, qrot, krot, dq_a, dq_b, dk, dv, cos, sin, rows, cols, own_a, own_b, oth_a, oth_b,
    qkv_mom, proj_mom, p_keep, p_recv, vec_in, vec_mom,
    out, s1, s2, s3, dn_own, dn_oth,
    dm, dm_full, freq, d_w, d_p, vec, bundle,
):
    core, band, chip, group = pos[0], pos[1], pos[2], pos[3]
    tokens = normed.shape[0]
    half = tokens // 2
    slab = half // 2
    dm_full[...] = jnp.zeros_like(dm_full)
    freq[...] = jnp.zeros_like(freq)
    for h in range(OWN_HEADS):
        c = cos[h * HALF : (h + 1) * HALF, :]
        s = sin[h * HALF : (h + 1) * HALF, :]
        angle = None
        d_query = jnp.concatenate([dq_a[h], dq_b[h]], axis=1)
        for which, source, rotated in ((0, d_query, qrot), (1, dk[h], krot)):
            du = source[0:HALF, :]
            dw = source[HALF:HD, :]
            u = rotated[h * HD : h * HD + HALF, :]
            w = rotated[h * HD + HALF : (h + 1) * HD, :]
            turn = dw * u - du * w
            angle = turn if angle is None else angle + turn
            at = which * OWN + h * HD
            dm[at : at + HD, :] = jnp.concatenate([du * c + dw * s, dw * c - du * s], axis=0).astype(bf16)
        at = pl.multiple_of(core * 96 + h * HALF, 32)
        freq[pl.ds(at, HALF), :] = jnp.sum(angle * rows[...], axis=1, keepdims=True)
        at = pl.multiple_of(192 + core * 96 + h * HALF, 32)
        freq[pl.ds(at, HALF), :] = jnp.sum(angle * cols[...], axis=1, keepdims=True)
        at = 2 * OWN + h * HD
        dm[at : at + HD, :] = dv[h].astype(bf16)
    for t in range(3):
        at = pl.multiple_of(t * D + core * OWN, 16)
        dm_full[pl.ds(at, OWN), :] = dm[t * OWN : (t + 1) * OWN, :]
    d_w[...] = dot_nn(dm[...], normed[...])
    for j in range(3):
        whole = band * 3 + j
        here = jnp.logical_and(lax.rem(whole, 4) // 2 == core, group == 0)
        at = pl.multiple_of(((whole // 4) * 2 + lax.rem(whole, 2)) * 96, 32)

        @pl.when(here)
        def _():
            d_w[pl.ds(at, 96), :] += 0.5 * qkv_mom[j * 96 : (j + 1) * 96, :]

    d_p[...] = p_keep[...] + p_recv[...]

    @pl.when(jnp.logical_and(band // 2 == core, group == 0))
    def _():
        d_p[pl.ds(pl.multiple_of(lax.rem(band, 2) * 96, 32), 96), :] += 0.5 * proj_mom[...]

    vec[...] = vec_in[...] + vec_mom[...]
    sums = dot_nt(jnp.ones((8, tokens), bf16), dm_full[...])
    for t in range(3):
        vec[4 + t : 5 + t, :] += sums[0:1, t * D : (t + 1) * D]
    vec[13:14, :] += jnp.broadcast_to(freq[...], (D, 128)).T[0:1, :]
    for b, src in enumerate((own_a, own_b, oth_a, oth_b)):
        part = dot_tn(dm[:, b * slab : (b + 1) * slab], w_own[...])
        xhat, _ = norm_rows(src[0:slab, :].astype(f32))
        vec[0:1, :] += jnp.sum(part * xhat, axis=0, keepdims=True)
        vec[2:3, :] += jnp.sum(part, axis=0, keepdims=True)
        to, at = (dn_own, b) if b < 2 else (dn_oth, b - 2)
        to[at * slab : (at + 1) * slab, :] = part.astype(to.dtype)
    row = lax.broadcasted_iota(jnp.int32, (16, D), 0)
    bundle[192:208, :] = jnp.where(row < 14, vec[...], 0.0)
    for e, ref in enumerate((out, s1, s2, s3)):
        quarter = lax.bitwise_xor(chip, e)
        bundle[0:144, :] = d_w[pl.ds(pl.multiple_of(quarter * 144, 16), 144), :]
        bundle[144:192, :] = d_p[pl.ds(pl.multiple_of(quarter * 48, 16), 48), :]
        write_bundle(ref, bundle[...])


def back(pos, normed, w_own, qrot, krot, grads, cos, sin, rows, cols, slab_refs, moms, projs, vecs):
    tokens = normed.shape[0]
    half = tokens // 2
    outs = (sds((208, D), i16),) * 4 + (sds((half, D), f32), sds((half, D), bf16))
    v = pltpu.VMEM
    scratch = [
        v((3 * OWN, tokens), bf16),
        v((3 * D, tokens), bf16),
        v((D, 1), f32),
        v((3 * OWN, D), f32),
        v((OWN, D), f32),
        v((16, D), f32),
        v((208, D), f32),
    ]
    return kernel_call(back_kernel, outs, scratch, 1, 22, extra=10)(
        pos, normed, w_own, qrot, krot, *grads, cos, sin, rows, cols, *slab_refs, *moms, *projs, *vecs
    )


def tail_kernel(
    pos, own_a, own_b, d_residual, dn_one, dn_two, base, acc_two, gains, out_a, out_b, band_rows, grid_w
):
    slab = band_rows * grid_w
    for b, (src, out) in enumerate(((own_a, out_a), (own_b, out_b))):
        here = slice(b * slab, (b + 1) * slab)
        total = base[here, :] + acc_two[here, :].astype(f32)
        out[0:slab, :] = (total * valid_column(pos, own_a, b, band_rows, grid_w)).astype(bf16)
        xhat, rstd = norm_rows(src[0:slab, :].astype(f32))
        dx = (dn_one[here, :] + dn_two[here, :].astype(f32)) * gains[0:1, :]
        back_x = rstd * (
            dx - jnp.mean(dx, axis=-1, keepdims=True) - xhat * jnp.mean(dx * xhat, axis=-1, keepdims=True)
        )
        out[slab : 2 * slab, :] = (d_residual[here, :] + back_x).astype(bf16)


def tail(pos, own, d_residual, dn_one, dn_two, base, acc_two, gains, band_rows, grid_w):
    outs = (sds((2 * band_rows * grid_w, D), bf16),) * 2
    body = functools.partial(tail_kernel, band_rows=band_rows, grid_w=grid_w)
    return kernel_call(body, outs, (), 1, 8)(
        pos, *own, d_residual, dn_one, dn_two, base, acc_two, gains
    )


def place_kernel(pos, a, b, block_out, patch_grad):
    band = pos[1]
    slab = block_out.shape[1]
    for which, ref in ((0, a), (1, b)):
        image = lax.rem(band + which, 2)
        block_out[image] = ref[0:slab, :]
        patch_grad[image] = ref[slab : 2 * slab, :].astype(f32)


def place(pos, got):
    slab = got[0].shape[0] // 2
    outs = (sds((2, slab, D), bf16), sds((2, slab, D), f32))
    return kernel_call(place_kernel, outs, (), 1, 2)(pos, *got)


def bands_kernel(pos, mine, r1, r2, r3, own, s1, s2, s3, power):
    band = pos[1]
    for i, column in enumerate(message_powers((r1, r2, r3))):
        power[i] = column
    for d, ref in ((0, own), (1, s1), (2, s2), (3, s3)):
        z = lax.bitwise_xor(band, d)
        rows = pl.ds(pl.multiple_of(z * 96, 32), 96)
        parts = [decoded(x[rows, :], power[i, rows, :]) for i, x in enumerate((r1, r2, r3))]
        total = (mine[z] + parts[0]) + (parts[1] + parts[2])
        if d == 0:
            ref[...] = total
        else:
            write_rows(ref, total)


def bands(pos, mine, received):
    outs = (sds((96, D), f32),) + (sds((112, D), i16),) * 3
    return kernel_call(bands_kernel, outs, [pltpu.VMEM((3, D, 1), f32)], 1, 4)(pos, mine, *received)


def piece_kernel(own, r1, r2, r3, mom, out, total):
    parts = [decoded(x[0:96, :], p[0:96]) for x, p in zip((r1, r2, r3), message_powers((r1, r2, r3)))]
    total[...] = (own[...] + parts[0]) + (parts[1] + parts[2])
    write_rows(out, total[...] + 0.5 * mom[...])


def piece_sum(own, received, mom):
    outs = (sds((112, D), i16), sds((96, D), f32))
    return kernel_call(piece_kernel, outs, (), 0, 5)(own, *received, mom)


def join_kernel(a, b, out):
    n = a.shape[0] - 16
    out[0:n, :] = a[0:n, :]
    out[n : 2 * n, :] = b[0:n, :]
    first = a[n : n + 16, :].astype(jnp.int32).astype(f32)
    second = b[n : n + 16, :].astype(jnp.int32).astype(f32)
    lanes = [first[:, 0:n], second[:, 0:n]]
    if 2 * n < D:
        lanes.append(jnp.zeros((16, D - 2 * n), f32))
    out[2 * n : 2 * n + 16, :] = whole16(jnp.concatenate(lanes, axis=1))


def join(a, b):
    return kernel_call(join_kernel, sds((2 * a.shape[0] - 16, D), i16), (), 0, 2)(a, b)


def recode_kernel(total, mom, out):
    write_rows(out, total[...] + 0.5 * mom[...])


def recode(total, mom):
    return kernel_call(recode_kernel, sds((112, D), i16), (), 0, 2)(total, mom)


def sum_low_kernel(own, r1, r2, r3, out, total):
    refs = (own, r1, r2, r3)
    x = [decoded(ref[...], p[0:208]) for ref, p in zip(refs, bundle_powers(refs))]
    whole = (x[0] + x[1]) + (x[2] + x[3])
    total[...] = whole
    write_bundle(out, whole)


def sum_low(own, received):
    outs = (sds(own.shape, i16), sds(own.shape, f32))
    return kernel_call(sum_low_kernel, outs, (), 0, 4)(own, *received)


def recode_bundle_kernel(total, out):
    write_bundle(out, total[...])


def recode_bundle(total):
    return kernel_call(recode_bundle_kernel, sds(total.shape, i16), (), 0, 1)(total)


def split_low(x):
    high = x.astype(bf16)
    return high, (x - high.astype(f32)).astype(bf16)


def dot_three_even(a, b):
    left = jnp.concatenate([a[0], a[0], a[1]], axis=1)
    right = jnp.concatenate([b[0], b[1], b[0]], axis=0)
    side = dot_nn(left, right[:, 0:256])
    low = dot_nn(left[256:], right[:, 256:])
    return jnp.concatenate([side, jnp.concatenate([side[256:].T, low], axis=0)], axis=1)


def split_three(x):
    high, rest = split_low(x)
    return high, rest, ((x - high.astype(f32)) - rest.astype(f32)).astype(bf16)


def dot_six_even(a, b):
    left = jnp.concatenate([a[0], a[0], a[1], a[1], a[0], a[2]], axis=1)
    right = jnp.concatenate([b[0], b[1], b[0], b[1], b[2], b[0]], axis=0)
    side = dot_nn(left, right[:, 0:256])
    low = dot_nn(left[256:], right[:, 256:])
    return jnp.concatenate([side, jnp.concatenate([side[256:].T, low], axis=0)], axis=1)


def sweeps(grams):
    row = lax.broadcasted_iota(jnp.int32, (D, D), 0)
    col = lax.broadcasted_iota(jnp.int32, (D, D), 1)
    eye = (row == col).astype(f32)
    scales, current, totals = [], [], [None] * len(grams)
    for gram in grams:
        trace = jnp.sum(jnp.sum(gram * eye, axis=1, keepdims=True), axis=0, keepdims=True)
        scales.append(1.0 / (jnp.sqrt(trace) + 1e-07))
        current.append(gram * (scales[-1] * scales[-1]))
    for sweep in range(5):
        split, dot = (split_three, dot_six_even) if sweep < 1 else (split_low, dot_three_even)
        parts = [split(a) for a in current]
        polys = [coeff_one * eye + coeff_two * a + coeff_three * dot(a2, a2) for a, a2 in zip(current, parts)]
        halves = [split(poly) for poly in polys]
        if sweep < 4:
            turned = [dot(a2, p2) for a2, p2 in zip(parts, halves)]
        totals = [
            poly if total is None else dot_three_even(split_low(total), p2)
            for total, poly, p2 in zip(totals, polys, halves)
        ]
        if sweep < 4:
            current = [dot(split(t), p2) for t, p2 in zip(turned, halves)]
    return [total * scale for total, scale in zip(totals, scales)]


def gram_of(high, low):
    cross = dot_tn(high, low)
    return dot_tn(high, high) + (cross + cross.T)


def gram_kernel(pos, a0, a1, a2, a3, keep, send, band_rows, s_high, s_low, e_high, e_low):
    core, chip = pos[0], pos[2]
    refs = (a0, a1, a2, a3)
    for e, (ref, power) in enumerate(zip(refs, message_powers(refs))):
        x = decoded(ref[0:D, :], power)
        high, low = split_low(x)
        for d in range(4):
            at, of = (e * 4 + d) * 48, d * 96
            s_high[at : at + 48, :], e_high[at : at + 48, :] = high[of : of + 48], high[of + 48 : of + 96]
            s_low[at : at + 48, :], e_low[at : at + 48, :] = low[of : of + 48], low[of + 48 : of + 96]
        to = pl.multiple_of(lax.bitwise_xor(chip, e) * 48, 16)
        band_rows[pl.ds(to, 48), :] = x[0:48]
        band_rows[pl.ds(pl.multiple_of(192 + to, 16), 48), :] = x[48:96]
    gram_s, gram_e = gram_of(s_high[...], s_low[...]), gram_of(e_high[...], e_low[...])
    keep[...] = jnp.where(core == 0, gram_s, gram_e)
    send[...] = jnp.where(core == 0, gram_e, gram_s)


def half_grams(pos, parts):
    outs = (sds((D, D), f32),) * 3
    scratch = [pltpu.VMEM((FF // 2, D), bf16)] * 4
    return kernel_call(gram_kernel, outs, scratch, 1, 4, extra=10)(pos, *parts)


def muon_kernel(pos, keep, recv, q0, q1, q2, q3, o0, o1, o2, o3, w0, w1, w2, w3, one_out, two_out, gram, rows, lows):
    core = pos[0]
    pieces = (q0, q1, q2, q3, o0, o1, o2, o3)
    power = bundle_powers(pieces)

    @pl.when(core == 0)
    def _():
        for e, ref in enumerate(pieces):
            x = split_low(decoded(ref[0:144, :], power[e][0:144]))
            rows[e * 144 : (e + 1) * 144, :], lows[e * 144 : (e + 1) * 144, :] = x
        gram[...] = gram_of(rows[...], lows[...])

    @pl.when(core != 0)
    def _():
        for e, ref in enumerate(pieces):
            x = split_low(decoded(ref[144:192, :], power[e][144:192]))
            rows[e * 48 : (e + 1) * 48, :], lows[e * 48 : (e + 1) * 48, :] = x
        gram[...] = gram_of(rows[0:D, :], lows[0:D, :])

    one, two = sweeps([keep[...] + recv[...], gram[...]])
    one_out[...] = one
    two_out[...] = two


def muon(pos, keep, recv, own_q, oth_q, weights):
    scratch = [pltpu.VMEM((D, D), f32), pltpu.VMEM((3 * D, D), bf16), pltpu.VMEM((3 * D, D), bf16)]
    outs = (sds((D, D), f32),) * 2
    return kernel_call(muon_kernel, outs, scratch, 1, 14, extra=12)(pos, keep, recv, *own_q, *oth_q, *weights)


def final_kernel(
    pos, one, two, one_oth, two_oth, band_mine, band_oth, q0, q1, q2, q3, o0, o1, o2, o3,
    qkv_w, proj_w, expand_w, shrink_w,
    qkv_m, qkv_new, proj_m, proj_new, expand_m, expand_new, shrink_m, shrink_new,
    q_mine, q_oth, q_rows,
):
    core, band, chip = pos[0], pos[1], pos[2]
    first = core == 0

    def choose(when_first, a, b):
        return split_low(jnp.where(first == when_first, a[...], b[...]))

    pieces = (q0, q1, q2, q3, o0, o1, o2, o3)
    power = bundle_powers(pieces)
    for e in range(4):
        quarter = lax.bitwise_xor(chip, e)
        for i, to in ((e, q_mine), (4 + e, q_oth)):
            x = decoded(pieces[i][0:192, :], power[i][0:192])
            to[pl.ds(pl.multiple_of(quarter * 144, 16), 144), :] = x[0:144]
            to[pl.ds(pl.multiple_of(3 * OWN + quarter * 48, 16), 48), :] = x[144:192]
    for j in range(4):
        whole = band * 3 + j
        at = pl.multiple_of(((whole // 4) * 2 + lax.rem(whole, 2)) * 96, 32)
        mine = lax.rem(whole, 4) // 2 == core
        if j == 3:
            at = pl.multiple_of(3 * OWN + lax.rem(band, 2) * 96, 32)
            mine = band // 2 == core

        @pl.when(mine)
        def _():
            q_rows[j * 96 : (j + 1) * 96, :] = q_mine[pl.ds(at, 96), :]

        @pl.when(jnp.logical_not(mine))
        def _():
            q_rows[j * 96 : (j + 1) * 96, :] = q_oth[pl.ds(at, 96), :]

    b_mine, b_oth = band_mine[...], band_oth[...]
    low_core, high_core = jnp.where(first, b_mine, b_oth), jnp.where(first, b_oth, b_mine)
    m_shrink = jnp.concatenate([low_core[0:192], high_core[0:192]], axis=0)
    m_expand = jnp.concatenate([low_core[192:], high_core[192:]], axis=0)
    t_shrink, t_expand = choose(True, one, one_oth), choose(False, one, one_oth)
    t_qkv, t_proj = choose(True, two, two_oth), choose(False, two, two_oth)
    for w, t, m, mom, new, size in (
        (qkv_w, t_qkv, q_rows[0:288, :], qkv_m, qkv_new, 3 * D),
        (proj_w, t_proj, q_rows[288:D, :], proj_m, proj_new, D),
        (shrink_w, t_shrink, m_shrink, shrink_m, shrink_new, FF),
    ):
        high, low = split_low(m)
        mom[...] = m
        new[...] = w[...] - 0.05 * math.sqrt(size) * (dot_nn(high, t[0]) + (dot_nn(high, t[1]) + dot_nn(low, t[0])))
    high, low = split_low(m_expand)
    expand_m[...] = m_expand.T
    ortho = dot_nt(t_expand[0], high) + (dot_nt(t_expand[1], high) + dot_nt(t_expand[0], low))
    expand_new[...] = expand_w[...] - 0.05 * math.sqrt(FF) * ortho


def final(pos, turns, far_turns, band_mine, band_oth, own_q, oth_q, *weights):
    outs = []
    for w in weights:
        outs += [sds(w.shape, f32)] * 2
    v = pltpu.VMEM
    scratch = [v((4 * OWN, D), f32), v((4 * OWN, D), f32), v((D, D), f32)]
    return kernel_call(final_kernel, tuple(outs), scratch, 1, 18, extra=10)(
        pos, *turns, *far_turns, band_mine, band_oth, *own_q, *oth_q, *weights
    )


def vector_kernel(pos, mine, other, gains, biases, freq, g_mom, g_new, b_mom, b_new, f_mom, f_new, mom, new):
    band = pos[1]
    n = mine.shape[0] - 16
    power = bundle_powers((mine, other))
    total = decoded(mine[n : n + 16, :], power[0][n : n + 16]) + decoded(other[n : n + 16, :], power[1][n : n + 16])
    mom[...] = total
    new[...] = jnp.zeros_like(new)
    freqs = jnp.concatenate([freq[0:1, :], freq[1:2, :]], axis=1)
    for at, values in ((0, gains[...]), (2, biases[...]), (13, freqs)):
        here = slice(at, at + values.shape[0])
        part = total[here, :]
        square = jnp.sum(jnp.sum(part * part, axis=1, keepdims=True), axis=0, keepdims=True)
        new[here, :] = values - 0.2 * part * lax.rsqrt(square * (1.0 / (values.shape[0] * D)) + 1e-06)
    for whole, g_out, b_out, f_out in ((mom, g_mom, b_mom, f_mom), (new, g_new, b_new, f_new)):
        g_out[...] = pltpu.roll(whole[0:8, :], lax.rem(D - 96 * band, D), 1)[0:2, 0:96]
        rows = pltpu.roll(jnp.broadcast_to(whole[13:14, :], (8, D)), lax.rem(D - 48 * band, D), 1)
        f_out[...] = jnp.concatenate([rows[0:1, 0:48], rows[0:1, 192:240]], axis=0)
        blocks = []
        for i in range(11):
            block = 11 * band + i
            row = jnp.broadcast_to(whole[pl.ds(2 + block // 4, 1), :], (8, D))
            blocks.append(pltpu.roll(row, lax.rem(D - 96 * lax.rem(block, 4), D), 1)[0:1, 0:96])
        b_out[...] = jnp.concatenate(blocks, axis=1).reshape(b_out.shape)


def vector_step(pos, mine, other, gains, biases, freq):
    outs = (sds((2, 96), f32),) * 2 + (sds((11 * 96,), f32),) * 2 + (sds((2, 48), f32),) * 2
    scratch = [pltpu.VMEM((16, D), f32)] * 2
    return kernel_call(vector_kernel, outs, scratch, 1, 5, cost=10**10)(pos, mine, other, gains, biases, freq)


def flip(x, bit):
    n = lax.axis_size("batch")
    return lax.ppermute(x, "batch", [(i, i ^ bit) for i in range(n)])


def swap_bands(x, d):
    return lax.ppermute(x, "rows", [(i, i ^ d) for i in range(4)])


def moves(which):
    pairs = []
    for k in range(lax.axis_size("batch") // 2):
        for c in range(2):
            for i in range(4):
                band = (i - 2 * c - which) % 4
                pairs.append(((2 * k + i // 2) * 4 + band, (2 * k + c) * 4 + i))
    return pairs


def to_image(parts):
    return [lax.ppermute(parts[which], AXES, moves(which)) for which in range(2)]


def from_image(part, which):
    return lax.ppermute(part, AXES, [(b, a) for a, b in moves(which)])


def other_chips(x):
    bit = 8
    while bit < lax.axis_size("batch"):
        x = x + flip(x.astype(f32), bit).astype(x.dtype)
        bit *= 2
    return x


def over_chips(x):
    return [flip(x, 2 * e) for e in range(1, 4)]


def over_bands(x):
    return [swap_bands(x, d) for d in range(1, 4)]


def local(
    patches,
    cotangent,
    heights,
    widths,
    qkv_weight,
    qkv_moment,
    proj_weight,
    proj_moment,
    expand_weight,
    expand_moment,
    shrink_weight,
    shrink_moment,
    norm_gains,
    gains_moment,
    all_biases,
    biases_moment,
    frequencies,
    freq_moment,
):
    images, band_rows, grid_w, _ = patches.shape
    slab = band_rows * grid_w
    batch = lax.axis_index("batch")
    band = lax.axis_index("rows")
    core = batch % 2
    chip = (batch // 2) % 4
    pos = jnp.stack([core, band, chip, batch // 2]).astype(jnp.int32)
    grid = (band_rows, grid_w)
    more_chips = lax.axis_size("batch") > 8

    share = own_weights(pos, qkv_weight.T, proj_weight.T, expand_weight, shrink_weight)
    shares = over_bands(share)
    p_a, p_b, c_a, c_b = slabs(
        pos, heights, widths, patches.reshape(images, slab, D), cotangent.reshape(images, slab, D)
    )
    own = to_image((p_a, p_b))
    oth = [flip(x, 1) for x in own]
    biases = all_biases.reshape(-1, D)
    cos, sin, rows_tok, cols_tok, bias_own, mom_big, vec_mom = setup(
        pos, frequencies, biases, expand_moment, shrink_moment,
        gains_moment, biases_moment.reshape(11, 96), freq_moment, 4 * slab, *grid,
    )
    shares, cos, vec_mom = lax.optimization_barrier((shares, cos, vec_mom))
    w_qkv, w_first, w_second = pack(share, shares)
    w_qkv = [w_qkv] + over_chips(w_qkv)
    w_first, oth = lax.optimization_barrier((w_first, oth))
    w_first = [w_first] + over_chips(w_first)
    c_a, c_b, w_second, w_qkv = lax.optimization_barrier((c_a, c_b, w_second, w_qkv))
    cot = to_image((c_a, c_b))
    w_second = [w_second] + over_chips(w_second)

    normed, w_own, qrot, krot, q_aug, k_aug, k_nat, v_nat, logs, *o_mine = front(
        pos, own + oth, w_qkv, bias_own, norm_gains, biases, cos, sin, rows_tok, cols_tok
    )
    o_oth = [flip(x, 1) for x in o_mine]
    cot, _ = lax.optimization_barrier((cot, o_mine))
    cot = cot + [flip(x, 1) for x in cot]
    resid, att, proj16, e_all, n2, hidden, slope = expand_layer(
        pos, own + oth, (*o_mine, *o_oth), w_first, norm_gains, biases, 2 * slab
    )
    g16, s_all, dpre, dn_two, dn_two_send = slope_layer(pos, own[0], cot, w_second, e_all, slope, *grid)
    base, acc_send, big, b1, b2, b3, vec = shrink_layer(pos, hidden, dpre, g16, n2, s_all, resid, biases)
    dn_two_recv, acc_recv = flip(dn_two_send, 1), flip(acc_send, 1)
    dn_two_recv, _ = lax.optimization_barrier((dn_two_recv, acc_recv))
    big_chips = [flip(x, 2 * e) for e, x in zip((1, 2, 3), (b1, b2, b3))]
    d_residual, d_mine, d_send, p_keep, p_send, vec = branch(
        pos, own[0], cot[:2], resid, att, proj16, dn_two, dn_two_recv, norm_gains, vec, *grid
    )
    d_recv = flip(d_send, 1)
    p_recv = flip(p_send, 1)
    dq_a, dk, dv = scores_back(0, q_aug, k_aug, k_nat, v_nat, logs, d_mine)
    dq_b, dk, dv = scores_back(1, q_aug, k_aug, k_nat, v_nat, logs, d_recv, (dk, dv))

    big, dq_b = lax.optimization_barrier((big, dq_b))
    own_big, *to_bands = bands(pos, big, big_chips)
    to_bands, dq_b, acc_recv = lax.optimization_barrier((to_bands, dq_b, acc_recv))
    from_bands = [swap_bands(x, d) for d, x in zip((1, 2, 3), to_bands)]
    q_mine, *q_sends, dn_own, dn_oth = back(
        pos, normed, w_own, qrot, krot, (dq_a, dq_b, dk, dv), cos, sin, rows_tok, cols_tok, own + oth,
        (qkv_moment.T, proj_moment.T), (p_keep, p_recv), (vec, vec_mom),
    )
    dn_recv = flip(dn_oth, 1)
    from_bands, _ = lax.optimization_barrier((from_bands, q_mine))
    big_piece, piece_total = piece_sum(own_big, from_bands, mom_big)
    if more_chips:
        big_piece = recode(other_chips(piece_total), mom_big)
    q_sends, big_piece = lax.optimization_barrier((q_sends, big_piece))

    q_low, q_total = sum_low(q_mine, [flip(x, 2 * e) for e, x in zip((1, 2, 3), q_sends)])
    if more_chips:
        q_low = recode_bundle(other_chips(q_total))
    big_pair = join(big_piece, swap_bands(big_piece, 1))
    big_bands = join(big_pair, swap_bands(big_pair, 2))
    big_bands, q_low = lax.optimization_barrier((big_bands, q_low))
    big_all = [big_bands] + over_chips(big_bands)
    q_recv = over_bands(q_low)
    results = tail(pos, own, d_residual, dn_own, dn_recv, base, acc_recv, norm_gains, *grid)
    q_recv, results = lax.optimization_barrier((q_recv, results))
    q_piece, _ = sum_low(q_low, q_recv)
    big_all, q_piece = lax.optimization_barrier((big_all, q_piece))
    own_q = [q_piece] + over_chips(q_piece)
    oth_q = [flip(x, 1) for x in own_q]

    gram_keep, gram_send, band_mine = half_grams(pos, big_all)
    image_a, image_b = from_image(results[0], 0), from_image(results[1], 1)
    weights = (qkv_weight.T, proj_weight.T, expand_weight, shrink_weight)
    turns = muon(pos, gram_keep, flip(gram_send, 1), own_q, oth_q, weights)
    images_back = [from_image(part, which) for which, part in enumerate(results)]
    images_back, _ = lax.optimization_barrier((images_back, turns))
    block_out, patch_grad = place(pos, images_back)
    vec_q, block_out = lax.optimization_barrier((own_q[0], block_out))
    vector_steps = vector_step(pos, vec_q, oth_q[0], norm_gains, biases, frequencies)
    shape = (images, band_rows, grid_w, D)
    block_out, patch_grad = block_out.reshape(shape), patch_grad.reshape(shape)
    far_turns, band_oth = [flip(x, 1) for x in turns], flip(band_mine, 1)
    far_turns, block_out, vector_steps = lax.optimization_barrier((far_turns, block_out, vector_steps))
    new = final(pos, turns, far_turns, band_mine, band_oth, own_q, oth_q, *weights)
    new = [x.T for x in new[:4]] + list(new[4:])

    return (block_out, patch_grad) + tuple(new) + tuple(vector_steps)


def solution(mesh):
    image = P("batch", "rows", None, None)
    cols, rows = P(None, "rows"), P("rows", None)
    return jax.shard_map(
        local,
        mesh=mesh,
        in_specs=(
            image, image, P("batch"), P("batch"), cols, cols, cols, cols, cols, cols, rows, rows,
            P(), cols, P(), P("rows"), P(), cols,
        ),
        out_specs=(
            image, image, cols, cols, cols, cols, cols, cols, rows, rows, cols, cols, P("rows"), P("rows"), cols, cols,
        ),
        check_vma=False,
    )
```

```python
import functools
import math

import jax
import jax.numpy as jnp
from jax import lax
from jax.experimental import pallas as pl
from jax.experimental.pallas import tpu as pltpu
from jax.sharding import PartitionSpec as P

D = 384
H = 6
HD = 64
FF = 1536
HALF = HD // 2
OWN_HEADS = H // 2
OWN = OWN_HEADS * HD
AUG = HD + 16

coeff_one = 3.4445
coeff_two = -4.775
coeff_three = 2.0315

bf16 = jnp.bfloat16
f32 = jnp.float32
AXES = ("batch", "rows")


def dot_nn(a, b):
    return lax.dot_general(a, b, (((1,), (0,)), ((), ())), preferred_element_type=f32)


def dot_nt(a, b):
    return lax.dot_general(a, b, (((1,), (1,)), ((), ())), preferred_element_type=f32)


def dot_tn(a, b):
    return lax.dot_general(a, b, (((0,), (0,)), ((), ())), preferred_element_type=f32)


def vmem_bytes(x):
    *lead, rows, lanes = (1,) * max(0, 2 - len(x.shape)) + tuple(x.shape)
    size = jnp.dtype(x.dtype).itemsize
    tile = 8 * 4 // size
    return math.prod(lead) * (-(-rows // tile) * tile) * (-(-lanes // 128) * 128) * size


def kernel_call(body, out_shape, scratch=(), smem=0, n_in=0, extra=4, cost=None):
    specs = [pl.BlockSpec(memory_space=pltpu.SMEM)] * smem
    specs += [pl.BlockSpec(memory_space=pltpu.VMEM)] * n_in

    def call(*args):
        held = list(args[smem:]) + jax.tree.leaves(out_shape) + [s for s in scratch]
        limit = sum(vmem_bytes(x) for x in held) + extra * 2**20
        return pl.pallas_call(
            body,
            out_shape=out_shape,
            in_specs=specs,
            out_specs=jax.tree.map(lambda _: pl.BlockSpec(memory_space=pltpu.VMEM), out_shape),
            scratch_shapes=list(scratch),
            compiler_params=pltpu.CompilerParams(vmem_limit_bytes=int(limit)),
            cost_estimate=cost and pl.CostEstimate(flops=cost, bytes_accessed=0, transcendentals=0),
        )(*args)

    return call


def sds(shape, dtype):
    return jax.ShapeDtypeStruct(shape, dtype)


def norm_rows(x):
    centered = x - jnp.mean(x, axis=-1, keepdims=True)
    rstd = lax.rsqrt(jnp.mean(centered * centered, axis=-1, keepdims=True) + 1e-06)
    return centered * rstd, rstd


i16 = jnp.int16
STEPS = 32000.0


def as_row(column):
    n = column.shape[0]
    row = jnp.broadcast_to(column, (n, 128)).T[0:1, :]
    return row if n == D else jnp.concatenate([row, jnp.zeros((1, D - n), f32)], axis=1)


def coded(x):
    top = jnp.maximum(jnp.max(jnp.abs(x), axis=1, keepdims=True), 1e-30)
    power = jnp.floor(jnp.log(top) * 1.4426950408889634 + 1.01)
    steps = jnp.floor(x * (STEPS / jnp.exp2(power)) + 0.5)
    return jnp.clip(steps, -32767.0, 32767.0), power


def decoded(codes, power):
    return codes.astype(jnp.int32).astype(f32) * (jnp.exp2(power) * (1.0 / STEPS))


def whole16(x):
    return x.astype(jnp.int32).astype(i16)


def write_rows(out, x):
    n = x.shape[0]
    codes, power = coded(x)
    out[0:n, :] = whole16(codes)
    out[n : n + 16, :] = whole16(jnp.broadcast_to(as_row(power), (16, D)))


def write_bundle(out, x):
    codes, power = coded(x)
    row = lax.broadcasted_iota(jnp.int32, (16, D), 0)
    out[0:192, :] = whole16(codes[0:192])
    out[192:208, :] = whole16(jnp.where(row == 15, as_row(power), codes[192:208]))


def columns(rows):
    rows = list(rows)
    turned = jnp.concatenate(rows + [jnp.zeros((128 - len(rows), D), f32)], axis=0).T
    return [turned[:, i : i + 1] for i in range(len(rows))]


def turned_powers(refs):
    tiles = [ref[ref.shape[0] - 16 :, :].astype(jnp.int32).astype(f32)[0:1, :] for ref in refs]
    return jnp.concatenate(tiles + [jnp.zeros((128 - len(tiles), D), f32)], axis=0).T


def message_powers(refs):
    tiles = [ref[ref.shape[0] - 16 :, :].astype(jnp.int32).astype(f32) for ref in refs]
    return columns(tile[0:1, :] for tile in tiles)


def bundle_powers(refs):
    return columns(ref[192:208, :].astype(jnp.int32).astype(f32)[15:16, :] for ref in refs)


def weights_kernel(pos, qkv_t, proj_t, expand, shrink, out, q_s, p_s, e_s, s_s, sem_q, sem_p, sem_e, sem_s):
    core, band, chip = pos[0], pos[1], pos[2]
    start = jnp.where(core == 0, jnp.where(band < 3, 2 * band, 0), jnp.where(band == 0, 4, jnp.where(band == 3, 2, 0)))
    count = jnp.where((core == 0) == (band < 2), 4, 2)
    at_q = pl.multiple_of((start + jnp.minimum(chip, count - 1)) * 48, 8)
    at_p = pl.multiple_of(jnp.minimum(chip, 2) * 32, 8)
    at = pl.multiple_of(core * 192 + chip * 48, 8)
    copies = (
        pltpu.make_async_copy(expand, e_s, sem_e),
        pltpu.make_async_copy(qkv_t.at[pl.ds(at_q, 48), :], q_s, sem_q),
        pltpu.make_async_copy(proj_t.at[pl.ds(at_p, 32), :], p_s, sem_p),
        pltpu.make_async_copy(shrink.at[pl.ds(at, 48), :], s_s, sem_s),
    )
    for copy in copies:
        copy.start()
    for copy in copies[1:]:
        copy.wait()
    out[0:48, :] = q_s[...].astype(bf16)
    out[48:80, :] = p_s[...].astype(bf16)
    out[128:176, :] = s_s[...].astype(bf16)
    copies[0].wait()
    e_s[...] = e_s[...].T
    out[80:128, :] = e_s[pl.ds(at, 48), :].astype(bf16)


def own_weights(pos, qkv_t, proj_t, expand, shrink):
    v = pltpu.VMEM
    dma = pltpu.SemaphoreType.DMA
    scratch = [v((48, D), f32), v((32, D), f32), v((D, D), f32), v((48, D), f32), dma, dma, dma, dma]
    hbm = pl.BlockSpec(memory_space=pltpu.HBM)
    return pl.pallas_call(
        weights_kernel,
        out_shape=sds((176, D), bf16),
        in_specs=[pl.BlockSpec(memory_space=pltpu.SMEM)] + [hbm] * 4,
        out_specs=pl.BlockSpec(memory_space=pltpu.VMEM),
        scratch_shapes=scratch,
        compiler_params=pltpu.CompilerParams(vmem_limit_bytes=56 * 2**20),
    )(pos, qkv_t, proj_t, expand, shrink)


def slabs_kernel(pos, heights, widths, patches, cot, p_a, p_b, c_a, c_b):
    band = pos[1]
    slab = patches.shape[1]
    row = lax.broadcasted_iota(jnp.int32, (16, D), 0)
    for which, (p, c) in enumerate(((p_a, c_a), (p_b, c_b))):
        image = lax.rem(band + which, 2)
        p[0:slab, :] = patches[image]
        size = jnp.where(row == 0, heights[image], widths[image])
        p[slab : slab + 16, :] = size.astype(f32).astype(bf16)
        c[...] = cot[image]


def slabs(pos, heights, widths, patches, cot):
    slab = patches.shape[1]
    outs = (sds((slab + 16, D), bf16),) * 2 + (sds((slab, D), bf16),) * 2
    return kernel_call(slabs_kernel, outs, (), 3, 2)(pos, heights, widths, patches, cot)


def setup_kernel(
    pos, freq, biases, expand_mom, shrink_mom, gains_mom, biases_mom, freq_mom,
    cos, sin, rows, cols, bias_own, mom_big, vec,
    column, turned, freq_one, freq_two, band_rows, grid_w,
):
    core, band, chip, group = pos[0], pos[1], pos[2], pos[3]
    tokens = rows.shape[1]
    slab = band_rows * grid_w
    token = lax.broadcasted_iota(jnp.int32, (1, tokens), 1)
    slot = token // slab
    d = jnp.where(slot < 2, 2 * core + slot, 2 - 2 * core + slot - 2)
    row = lax.bitwise_and(band + 4 - d, 3) * band_rows + lax.rem(token, slab) // grid_w
    rows[...] = row.astype(f32)
    cols[...] = lax.rem(token, grid_w).astype(f32)
    own = pl.ds(pl.multiple_of(core * 96, 8), 96)
    freq_one[...] = jnp.broadcast_to(freq[0:1, :], (128, H * HALF)).T
    freq_two[...] = jnp.broadcast_to(freq[1:2, :], (128, H * HALF)).T
    angle = freq_one[own, 0:1] * rows[...] + freq_two[own, 0:1] * cols[...]
    cos[...] = jnp.cos(angle)
    sin[...] = jnp.sin(angle)
    for t in range(3):
        column[...] = jnp.broadcast_to(biases[2 + t : 3 + t, :], (128, D)).T
        at = pl.multiple_of(core * OWN, 8)
        bias_own[t * OWN : (t + 1) * OWN, :] = column[pl.ds(at, OWN), 0:1]
    at = pl.multiple_of(core * 192 + chip * 48, 8)
    mom_big[0:48, :] = shrink_mom[pl.ds(at, 48), :]
    turned[...] = expand_mom[...].T
    mom_big[48:96, :] = turned[pl.ds(at, 48), :]
    share = jnp.where(jnp.logical_and(core == 0, group == 0), 0.5, 0.0)
    vec[...] = jnp.zeros_like(vec)
    none = jnp.zeros((8, 144), f32)

    def wide(x, lanes):
        return jnp.concatenate([x, jnp.zeros((x.shape[0], lanes), f32)], axis=1)

    gains = jnp.concatenate([wide(gains_mom[...], 288), jnp.zeros((6, D), f32)], axis=0)
    vec[0:2, :] = share * pltpu.roll(gains, 96 * band, 1)[0:2, :]
    freqs = jnp.concatenate([freq_mom[0:1, :], none[0:1], freq_mom[1:2, :], none[0:1]], axis=1)
    vec[13:14, :] = share * pltpu.roll(jnp.broadcast_to(freqs, (8, D)), 48 * band, 1)[0:1, :]
    for i in range(11):
        block = 11 * band + i
        line = jnp.broadcast_to(wide(biases_mom[i : i + 1, :], 288), (8, D))
        vec[pl.ds(2 + block // 4, 1), :] += share * pltpu.roll(line, 96 * lax.rem(block, 4), 1)[0:1, :]


def setup(pos, freq, biases, expand_mom, shrink_mom, gains_mom, biases_mom, freq_mom, tokens, band_rows, grid_w):
    v = pltpu.VMEM
    outs = (
        sds((96, tokens), f32),
        sds((96, tokens), f32),
        sds((1, tokens), f32),
        sds((1, tokens), f32),
        sds((3 * OWN, 1), f32),
        sds((96, D), f32),
        sds((16, D), f32),
    )
    scratch = [v((D, 128), f32), v((D, D), f32), v((H * HALF, 128), f32), v((H * HALF, 128), f32)]
    body = functools.partial(setup_kernel, band_rows=band_rows, grid_w=grid_w)
    return kernel_call(body, outs, scratch, 1, 7)(
        pos, freq, biases, expand_mom, shrink_mom, gains_mom, biases_mom, freq_mom
    )


def pack_kernel(own, r1, r2, r3, qkv, first, second):
    for d, ref in enumerate((own, r1, r2, r3)):
        qkv[d] = ref[0:48, :]
        first[d] = ref[48:128, :]
        second[d] = ref[128:176, :]


def pack(own, received):
    outs = (sds((4, 48, D), bf16), sds((4, 80, D), bf16), sds((4, 48, D), bf16))
    return kernel_call(pack_kernel, outs, (), 0, 4)(own, *received)


def front_kernel(
    pos, own_a, own_b, oth_a, oth_b, w0, w1, w2, w3, bias, gains, biases, cos, sin, rows, cols,
    normed, w_own, qrot, krot, q_aug, k_aug, k_nat, v_nat, logs, o_own, o_oth,
    w_all, v_t, o_all,
):
    core, band, chip = pos[0], pos[1], pos[2]
    tokens = normed.shape[0]
    block = tokens // 4
    for e, ref in enumerate((w0, w1, w2, w3)):
        quarter = lax.bitwise_xor(chip, e)
        for shard in range(4):
            base = jnp.where(core == 0, (0, 4, 8, 10)[shard], (0, 2, 4, 8)[shard])
            count = jnp.where(core == 0, (4, 4, 2, 2)[shard], (2, 2, 4, 4)[shard])
            at = jnp.where(quarter < count, base + quarter, 12)
            w_all[pl.ds(pl.multiple_of(at * 48, 16), 48), :] = ref[lax.bitwise_xor(band, shard)]
    w_own[...] = w_all[0 : 3 * OWN, :]
    for b, src in enumerate((own_a, own_b, oth_a, oth_b)):
        xhat, _ = norm_rows(src[0:block, :].astype(f32))
        normed[b * block : (b + 1) * block, :] = (xhat * gains[0:1, :] + biases[0:1, :]).astype(bf16)
    high = own_a[block : block + 1, 0:1].astype(f32)
    wide = own_a[block + 1 : block + 2, 0:1].astype(f32)
    inside = jnp.logical_and(rows[...] < high, cols[...] < wide)
    key_bias = jnp.where(inside, 0.0, -1e9).astype(f32)
    ones_row = (lax.broadcasted_iota(jnp.int32, (AUG - HD, block), 0) == 0).astype(f32)
    for b in range(4):
        here = slice(b * block, (b + 1) * block)
        mixed = dot_nt(w_own[...], normed[here, :]) + bias[...]
        for h in range(OWN_HEADS):
            c = cos[h * HALF : (h + 1) * HALF, here]
            s = sin[h * HALF : (h + 1) * HALF, here]
            qu = mixed[h * HD : h * HD + HALF, :]
            qw = mixed[h * HD + HALF : (h + 1) * HD, :]
            ku = mixed[OWN + h * HD : OWN + h * HD + HALF, :]
            kw = mixed[OWN + h * HD + HALF : OWN + (h + 1) * HD, :]
            qr = jnp.concatenate([qu * c - qw * s, qw * c + qu * s], axis=0)
            kr = jnp.concatenate([ku * c - kw * s, kw * c + ku * s], axis=0)
            qrot[h * HD : (h + 1) * HD, here] = qr
            krot[h * HD : (h + 1) * HD, here] = kr
            q_low = qr.astype(bf16).astype(f32) * 0.125
            q_aug[h, :, here] = jnp.concatenate([q_low, ones_row], axis=0).astype(bf16)
            k_full = jnp.concatenate([kr, ones_row * key_bias[:, here]], axis=0)
            k_aug[h, :, here] = k_full.astype(bf16)
            k_nat[h, here, :] = k_full.T.astype(bf16)
            vv = mixed[2 * OWN + h * HD : 2 * OWN + (h + 1) * HD, :]
            v_t[h, :, here] = vv.astype(bf16)
            v_nat[h, here, :] = vv.T.astype(bf16)

    half = tokens // 2

    def attend(item, carry):
        here = pl.ds(pl.multiple_of(item * half, half), half)
        scores = [dot_nn(k_nat[h], q_aug[h, :, here]) for h in range(OWN_HEADS)]
        for h in range(OWN_HEADS):
            peak = jnp.max(scores[h], axis=0, keepdims=True)
            e = jnp.exp(scores[h] - peak)
            total = jnp.sum(e, axis=0, keepdims=True)
            out = dot_nn(v_t[h], (e * (1.0 / total)).astype(bf16))
            logs[h, :, here] = peak + jnp.log(total)
            o_all[h * HD : (h + 1) * HD, here] = out.astype(bf16)
        return carry

    lax.fori_loop(0, 2, attend, 0)
    o_own[...] = o_all[:, 0:half]
    o_oth[...] = o_all[:, half:tokens]


def front(pos, slab_refs, weights, bias, gains, biases, cos, sin, rows, cols):
    tokens = rows.shape[1]
    nh = OWN_HEADS
    outs = (
        sds((tokens, D), bf16),
        sds((3 * OWN, D), bf16),
        sds((OWN, tokens), f32),
        sds((OWN, tokens), f32),
        sds((nh, AUG, tokens), bf16),
        sds((nh, AUG, tokens), bf16),
        sds((nh, tokens, AUG), bf16),
        sds((nh, tokens, HD), bf16),
        sds((nh, 1, tokens), f32),
        sds((OWN, tokens // 2), bf16),
        sds((OWN, tokens // 2), bf16),
    )
    scratch = [
        pltpu.VMEM((3 * OWN + 48, D), bf16),
        pltpu.VMEM((nh, HD, tokens), bf16),
        pltpu.VMEM((OWN, tokens), bf16),
    ]
    return kernel_call(front_kernel, outs, scratch, 1, 15, extra=24)(
        pos, *slab_refs, *weights, bias, gains, biases, cos, sin, rows, cols
    )


def valid_column(pos, sized, first_slot, band_rows, grid_w):
    core, band = pos[0], pos[1]
    slab = band_rows * grid_w
    d = 2 * core + first_slot if first_slot < 2 else 2 - 2 * core + first_slot - 2
    token = lax.broadcasted_iota(jnp.int32, (slab, 1), 0)
    row = lax.bitwise_and(band + 4 - d, 3) * band_rows + token // grid_w
    col = lax.rem(token, grid_w)
    high = sized[slab : slab + 1, 0:1].astype(f32)
    wide = sized[slab + 1 : slab + 2, 0:1].astype(f32)
    return jnp.logical_and(row.astype(f32) < high, col.astype(f32) < wide).astype(f32)


def expand_kernel(
    pos, own_a, own_b, oth_a, oth_b, mine_a, mine_b, far_a, far_b, w0, w1, w2, w3, gains, biases,
    resid_own, att_own, proj_out, e_all, n2, hidden, slope,
    p_all,
):
    core, band, chip = pos[0], pos[1], pos[2]
    half = resid_own.shape[0]
    slab = half // 2
    first = core == 0
    for e, ref in enumerate((w0, w1, w2, w3)):
        quarter = lax.bitwise_xor(chip, e)
        for shard in range(4):
            d = lax.bitwise_xor(band, shard)
            at = jnp.where(quarter < 3, shard * 96 + quarter * 32, D)
            p_all[pl.ds(pl.multiple_of(at, 16), 32), :] = ref[d, 0:32, :]
            at = pl.multiple_of(shard * 192 + quarter * 48, 16)
            e_all[pl.ds(at, 48), :] = ref[d, 32:80, :]
    proj = p_all[0:D, :]
    proj_out[...] = proj
    bias = jnp.concatenate(
        [jnp.where(first, biases[6 + s : 7 + s, 0:192], biases[6 + s : 7 + s, 192:384]) for s in range(4)], axis=1
    )
    for b, src in enumerate((own_a, own_b, oth_a, oth_b)):
        here = slice(b * slab, (b + 1) * slab)
        there = slice((b % 2) * slab, (b % 2 + 1) * slab)
        m, o = (mine_a, far_b) if b < 2 else (mine_b, far_a)
        m, o = m[:, there].astype(f32), o[:, there].astype(f32)
        att = jnp.concatenate([jnp.where(first, m, o), jnp.where(first, o, m)], axis=0).T.astype(bf16)
        res = src[0:slab, :].astype(f32) + dot_nt(att, proj) + biases[5:6, :]
        if b < 2:
            resid_own[here, :] = res
            att_own[here, :] = att
        xhat, _ = norm_rows(res)
        n2[here, :] = (xhat * gains[1:2, :] + biases[1:2, :]).astype(bf16)

    def part(b, carry):
        here = pl.ds(pl.multiple_of(b * slab, slab), slab)
        pre = dot_nt(n2[here, :], e_all[...]) + bias
        cdf = 0.5 * (1.0 + lax.erf(pre * math.sqrt(0.5)))
        hidden[here, :] = (pre * cdf).astype(bf16)
        slope[here, :] = cdf + pre * (jnp.exp(-0.5 * pre * pre) * (1.0 / math.sqrt(2.0 * math.pi)))
        return carry

    lax.fori_loop(0, 4, part, 0)


def expand_layer(pos, slab_refs, att, weights, gains, biases, half):
    v = pltpu.VMEM
    outs = (
        sds((half, D), f32),
        sds((half, D), bf16),
        sds((D, D), bf16),
        sds((FF // 2, D), bf16),
        sds((2 * half, D), bf16),
        sds((2 * half, FF // 2), bf16),
        sds((2 * half, FF // 2), f32),
    )
    return kernel_call(expand_kernel, outs, [v((D + 32, D), bf16)], 1, 14, extra=12)(
        pos, *slab_refs, *att, *weights, gains, biases
    )


def slope_kernel(
    pos, own_a, cot_a, cot_b, cot_c, cot_d, w0, w1, w2, w3, e_all, slope, g16, s_all, dpre, dn_own, dn_send,
    band_rows, grid_w,
):
    core, band, chip = pos[0], pos[1], pos[2]
    slab = band_rows * grid_w
    for e, ref in enumerate((w0, w1, w2, w3)):
        quarter = lax.bitwise_xor(chip, e)
        for shard in range(4):
            at = pl.multiple_of(shard * 192 + quarter * 48, 16)
            s_all[pl.ds(at, 48), :] = ref[lax.bitwise_xor(band, shard)]
    for b, cot in enumerate((cot_a, cot_b, cot_c, cot_d)):
        here = slice(b * slab, (b + 1) * slab)
        g16[here, :] = (cot[...].astype(f32) * valid_column(pos, own_a, b, band_rows, grid_w)).astype(bf16)
    for b in range(4):
        here = slice(b * slab, (b + 1) * slab)
        dpre[here, :] = (dot_nt(g16[here, :], s_all[...]) * slope[here, :]).astype(bf16)
    half = 2 * slab
    dn_send[...] = dot_nn(dpre[half : 2 * half, :], e_all[...]).astype(bf16)
    dn_own[...] = dot_nn(dpre[0:half, :], e_all[...])


def slope_layer(pos, own_a, cots, weights, e_all, slope, band_rows, grid_w):
    half = 2 * band_rows * grid_w
    outs = (
        sds((2 * half, D), bf16),
        sds((FF // 2, D), bf16),
        sds((2 * half, FF // 2), bf16),
        sds((half, D), f32),
        sds((half, D), bf16),
    )
    body = functools.partial(slope_kernel, band_rows=band_rows, grid_w=grid_w)
    return kernel_call(body, outs, (), 1, 11, extra=10)(pos, own_a, *cots, *weights, e_all, slope)


def shrink_kernel(pos, hidden, dpre, g16, n2, s_all, resid, biases, base, acc_send, mine, s1, s2, s3, vec, grads, part):
    core, chip = pos[0], pos[2]
    half = base.shape[0]
    first = core == 0
    grads[0] = dot_tn(hidden[...], g16[...])
    grads[1] = dot_tn(dpre[...], n2[...])
    for e, ref in ((0, mine), (1, s1), (2, s2), (3, s3)):
        for z in range(4):
            at = pl.ds(pl.multiple_of(z * 192 + lax.bitwise_xor(chip, e) * 48, 16), 48)
            part[z * 96 : z * 96 + 48, :] = grads[0, at, :]
            part[z * 96 + 48 : z * 96 + 96, :] = grads[1, at, :]
        if e == 0:
            for z in range(4):
                ref[z] = part[z * 96 : (z + 1) * 96, :]
        else:
            write_rows(ref, part[...])
    base[...] = resid[...] + dot_nn(hidden[0:half, :], s_all[...]) + biases[10:11, :]
    acc_send[...] = dot_nn(hidden[half : 2 * half, :], s_all[...]).astype(bf16)
    vec[...] = jnp.zeros_like(vec)
    sums = dot_nn(jnp.ones((8, 2 * half), bf16), dpre[...])
    none = jnp.zeros((1, 192), f32)
    for s in range(4):
        x = sums[0:1, s * 192 : (s + 1) * 192]
        vec[8 + s : 9 + s, :] = jnp.where(
            first, jnp.concatenate([x, none], axis=1), jnp.concatenate([none, x], axis=1)
        )
    vec[12:13, :] = jnp.sum(g16[0:half, :].astype(f32), axis=0, keepdims=True)


def shrink_layer(pos, hidden, dpre, g16, n2, s_all, resid, biases):
    half = g16.shape[0] // 2
    outs = (
        sds((half, D), f32),
        sds((half, D), bf16),
        sds((4, 96, D), f32),
        sds((400, D), i16),
        sds((400, D), i16),
        sds((400, D), i16),
        sds((16, D), f32),
    )
    return kernel_call(shrink_kernel, outs, [pltpu.VMEM((2, FF // 2, D), f32), pltpu.VMEM((D, D), f32)], 1, 7, extra=10)(
        pos, hidden, dpre, g16, n2, s_all, resid, biases
    )


def branch_kernel(
    pos, own_a, cot_a, cot_b, resid, att, proj, dn_one, dn_two, gains, vec_in,
    d_residual, d_mine, d_send, p_keep, p_send, vec,
    g_s, dat, grad_p, band_rows, grid_w,
):
    core = pos[0]
    slab = band_rows * grid_w
    for b, cot in enumerate((cot_a, cot_b)):
        here = slice(b * slab, (b + 1) * slab)
        g_s[here, :] = cot[...].astype(f32) * valid_column(pos, own_a, b, band_rows, grid_w)
    vec[...] = vec_in[...]
    xhat, rstd = norm_rows(resid[...])
    dn = dn_one[...] + dn_two[...].astype(f32)
    vec[3:4, :] = jnp.sum(dn, axis=0, keepdims=True)
    vec[1:2, :] = jnp.sum(dn * xhat, axis=0, keepdims=True)
    dx = dn * gains[1:2, :]
    back_x = rstd * (
        dx - jnp.mean(dx, axis=-1, keepdims=True) - xhat * jnp.mean(dx * xhat, axis=-1, keepdims=True)
    )
    d_res = g_s[...] + back_x
    d_residual[...] = d_res
    low = d_res.astype(bf16)
    dat[...] = dot_nn(low, proj[...]).T.astype(bf16)
    d_mine[...] = dat[pl.ds(pl.multiple_of(core * OWN, 16), OWN), :]
    d_send[...] = dat[pl.ds(pl.multiple_of((1 - core) * OWN, 16), OWN), :]
    vec[7:8, :] = jnp.sum(low.astype(f32), axis=0, keepdims=True)
    grad_p[...] = dot_tn(low, att[...])
    p_keep[...] = grad_p[pl.ds(pl.multiple_of(core * OWN, 8), OWN), :]
    p_send[...] = grad_p[pl.ds(pl.multiple_of((1 - core) * OWN, 8), OWN), :]


def branch(pos, own_a, cots, resid, att, proj, dn_one, dn_two, gains, vec, band_rows, grid_w):
    half = resid.shape[0]
    v = pltpu.VMEM
    outs = (
        sds((half, D), f32),
        sds((OWN, half), bf16),
        sds((OWN, half), bf16),
        sds((OWN, D), f32),
        sds((OWN, D), f32),
        sds((16, D), f32),
    )
    body = functools.partial(branch_kernel, band_rows=band_rows, grid_w=grid_w)
    return kernel_call(body, outs, [v((half, D), f32), v((D, half), bf16), v((D, D), f32)], 1, 10)(
        pos, own_a, *cots, resid, att, proj, dn_one, dn_two, gains, vec
    )


def scores_kernel(which, q_aug, k_aug, k_nat, v_nat, logs, d_out, *refs):
    before, (dq, dk, dv) = refs[:-3], refs[-3:]
    half = d_out.shape[1]
    here = slice(which * half, (which + 1) * half)
    for h in range(OWN_HEADS):
        q_t = q_aug[h, :, here]
        g = d_out[h * HD : (h + 1) * HD, :]
        p = jnp.exp(dot_nn(k_nat[h], q_t) - logs[h, :, here])
        dp = dot_nn(v_nat[h], g)
        inner = jnp.sum(p * dp, axis=0, keepdims=True)
        ds = (p * (dp - inner)).astype(bf16)
        dv_one = dot_nt(g, p.astype(bf16))
        dk_one = dot_nt(q_t[0:HD, :], ds)
        dq[h] = dot_nn(k_aug[h, 0:HD, :], ds) * 0.125
        dk[h] = dk_one + before[0][h] if before else dk_one
        dv[h] = dv_one + before[1][h] if before else dv_one


def scores_back(which, q_aug, k_aug, k_nat, v_nat, logs, d_out, before=()):
    tokens = q_aug.shape[2]
    outs = (sds((OWN_HEADS, HD, tokens // 2), f32),) + (sds((OWN_HEADS, HD, tokens), f32),) * 2
    return kernel_call(functools.partial(scores_kernel, which), outs, (), 0, 6 + len(before), extra=28)(
        q_aug, k_aug, k_nat, v_nat, logs, d_out, *before
    )


def back_kernel(
    pos, normed, w_own, qrot, krot, dq_a, dq_b, dk, dv, cos, sin, rows, cols, own_a, own_b, oth_a, oth_b,
    qkv_mom, proj_mom, p_keep, p_recv, vec_in, vec_mom,
    out, s1, s2, s3, dn_own, dn_oth,
    dm, dm_full, freq, d_w, d_p, vec, bundle,
):
    core, band, chip, group = pos[0], pos[1], pos[2], pos[3]
    tokens = normed.shape[0]
    half = tokens // 2
    slab = half // 2
    dm_full[...] = jnp.zeros_like(dm_full)
    freq[...] = jnp.zeros_like(freq)
    for h in range(OWN_HEADS):
        c = cos[h * HALF : (h + 1) * HALF, :]
        s = sin[h * HALF : (h + 1) * HALF, :]
        angle = None
        d_query = jnp.concatenate([dq_a[h], dq_b[h]], axis=1)
        for which, source, rotated in ((0, d_query, qrot), (1, dk[h], krot)):
            du = source[0:HALF, :]
            dw = source[HALF:HD, :]
            u = rotated[h * HD : h * HD + HALF, :]
            w = rotated[h * HD + HALF : (h + 1) * HD, :]
            turn = dw * u - du * w
            angle = turn if angle is None else angle + turn
            at = which * OWN + h * HD
            dm[at : at + HD, :] = jnp.concatenate([du * c + dw * s, dw * c - du * s], axis=0).astype(bf16)
        at = pl.multiple_of(core * 96 + h * HALF, 32)
        freq[pl.ds(at, HALF), :] = jnp.sum(angle * rows[...], axis=1, keepdims=True)
        at = pl.multiple_of(192 + core * 96 + h * HALF, 32)
        freq[pl.ds(at, HALF), :] = jnp.sum(angle * cols[...], axis=1, keepdims=True)
        at = 2 * OWN + h * HD
        dm[at : at + HD, :] = dv[h].astype(bf16)
    for t in range(3):
        at = pl.multiple_of(t * D + core * OWN, 16)
        dm_full[pl.ds(at, OWN), :] = dm[t * OWN : (t + 1) * OWN, :]
    d_w[...] = dot_nn(dm[...], normed[...])
    for j in range(3):
        whole = band * 3 + j
        here = jnp.logical_and(lax.rem(whole, 4) // 2 == core, group == 0)
        at = pl.multiple_of(((whole // 4) * 2 + lax.rem(whole, 2)) * 96, 32)

        @pl.when(here)
        def _():
            d_w[pl.ds(at, 96), :] += 0.5 * qkv_mom[j * 96 : (j + 1) * 96, :]

    d_p[...] = p_keep[...] + p_recv[...]

    @pl.when(jnp.logical_and(band // 2 == core, group == 0))
    def _():
        d_p[pl.ds(pl.multiple_of(lax.rem(band, 2) * 96, 32), 96), :] += 0.5 * proj_mom[...]

    vec[...] = vec_in[...] + vec_mom[...]
    sums = dot_nt(jnp.ones((8, tokens), bf16), dm_full[...])
    for t in range(3):
        vec[4 + t : 5 + t, :] += sums[0:1, t * D : (t + 1) * D]
    vec[13:14, :] += jnp.broadcast_to(freq[...], (D, 128)).T[0:1, :]
    for b, src in enumerate((own_a, own_b, oth_a, oth_b)):
        part = dot_tn(dm[:, b * slab : (b + 1) * slab], w_own[...])
        xhat, _ = norm_rows(src[0:slab, :].astype(f32))
        vec[0:1, :] += jnp.sum(part * xhat, axis=0, keepdims=True)
        vec[2:3, :] += jnp.sum(part, axis=0, keepdims=True)
        to, at = (dn_own, b) if b < 2 else (dn_oth, b - 2)
        to[at * slab : (at + 1) * slab, :] = part.astype(to.dtype)
    row = lax.broadcasted_iota(jnp.int32, (16, D), 0)
    bundle[192:208, :] = jnp.where(row < 14, vec[...], 0.0)
    for e, ref in enumerate((out, s1, s2, s3)):
        quarter = lax.bitwise_xor(chip, e)
        bundle[0:144, :] = d_w[pl.ds(pl.multiple_of(quarter * 144, 16), 144), :]
        bundle[144:192, :] = d_p[pl.ds(pl.multiple_of(quarter * 48, 16), 48), :]
        write_bundle(ref, bundle[...])


def back(pos, normed, w_own, qrot, krot, grads, cos, sin, rows, cols, slab_refs, moms, projs, vecs):
    tokens = normed.shape[0]
    half = tokens // 2
    outs = (sds((208, D), i16),) * 4 + (sds((half, D), f32), sds((half, D), bf16))
    v = pltpu.VMEM
    scratch = [
        v((3 * OWN, tokens), bf16),
        v((3 * D, tokens), bf16),
        v((D, 1), f32),
        v((3 * OWN, D), f32),
        v((OWN, D), f32),
        v((16, D), f32),
        v((208, D), f32),
    ]
    return kernel_call(back_kernel, outs, scratch, 1, 22, extra=10)(
        pos, normed, w_own, qrot, krot, *grads, cos, sin, rows, cols, *slab_refs, *moms, *projs, *vecs
    )


def tail_kernel(
    pos, own_a, own_b, d_residual, dn_one, dn_two, base, acc_two, gains, out_a, out_b, band_rows, grid_w
):
    slab = band_rows * grid_w
    for b, (src, out) in enumerate(((own_a, out_a), (own_b, out_b))):
        here = slice(b * slab, (b + 1) * slab)
        total = base[here, :] + acc_two[here, :].astype(f32)
        out[0:slab, :] = (total * valid_column(pos, own_a, b, band_rows, grid_w)).astype(bf16)
        xhat, rstd = norm_rows(src[0:slab, :].astype(f32))
        dx = (dn_one[here, :] + dn_two[here, :].astype(f32)) * gains[0:1, :]
        back_x = rstd * (
            dx - jnp.mean(dx, axis=-1, keepdims=True) - xhat * jnp.mean(dx * xhat, axis=-1, keepdims=True)
        )
        out[slab : 2 * slab, :] = (d_residual[here, :] + back_x).astype(bf16)


def tail(pos, own, d_residual, dn_one, dn_two, base, acc_two, gains, band_rows, grid_w):
    outs = (sds((2 * band_rows * grid_w, D), bf16),) * 2
    body = functools.partial(tail_kernel, band_rows=band_rows, grid_w=grid_w)
    return kernel_call(body, outs, (), 1, 8)(
        pos, *own, d_residual, dn_one, dn_two, base, acc_two, gains
    )


def place_kernel(pos, a, b, block_out, patch_grad):
    band = pos[1]
    slab = block_out.shape[1]
    for which, ref in ((0, a), (1, b)):
        image = lax.rem(band + which, 2)
        block_out[image] = ref[0:slab, :]
        patch_grad[image] = ref[slab : 2 * slab, :].astype(f32)


def place(pos, got):
    slab = got[0].shape[0] // 2
    outs = (sds((2, slab, D), bf16), sds((2, slab, D), f32))
    return kernel_call(place_kernel, outs, (), 1, 2)(pos, *got)


def bands_kernel(pos, mine, r1, r2, r3, own, s1, s2, s3, power):
    band = pos[1]
    power[...] = turned_powers((r1, r2, r3))
    for d, ref in ((0, own), (1, s1), (2, s2), (3, s3)):
        z = lax.bitwise_xor(band, d)
        rows = pl.ds(pl.multiple_of(z * 96, 32), 96)
        parts = [decoded(x[rows, :], power[rows, i : i + 1]) for i, x in enumerate((r1, r2, r3))]
        total = (mine[z] + parts[0]) + (parts[1] + parts[2])
        if d == 0:
            ref[...] = total
        else:
            write_rows(ref, total)


def bands(pos, mine, received):
    outs = (sds((96, D), f32),) + (sds((112, D), i16),) * 3
    return kernel_call(bands_kernel, outs, [pltpu.VMEM((D, 128), f32)], 1, 4)(pos, mine, *received)


def piece_kernel(own, r1, r2, r3, mom, out, *total):
    parts = [decoded(x[0:96, :], p[0:96]) for x, p in zip((r1, r2, r3), message_powers((r1, r2, r3)))]
    whole = (own[...] + parts[0]) + (parts[1] + parts[2])
    for ref in total:
        ref[...] = whole
    write_rows(out, whole + 0.5 * mom[...])


def piece_sum(own, received, mom, more):
    outs = (sds((112, D), i16),) + ((sds((96, D), f32),) if more else ())
    return kernel_call(piece_kernel, outs, (), 0, 5)(own, *received, mom)


def join_kernel(a, b, out):
    n = a.shape[0] - 16
    out[0:n, :] = a[0:n, :]
    out[n : 2 * n, :] = b[0:n, :]
    first = a[n : n + 16, :].astype(jnp.int32).astype(f32)
    second = b[n : n + 16, :].astype(jnp.int32).astype(f32)
    lanes = [first[:, 0:n], second[:, 0:n]]
    if 2 * n < D:
        lanes.append(jnp.zeros((16, D - 2 * n), f32))
    out[2 * n : 2 * n + 16, :] = whole16(jnp.concatenate(lanes, axis=1))


def join(a, b):
    return kernel_call(join_kernel, sds((2 * a.shape[0] - 16, D), i16), (), 0, 2)(a, b)


def recode_kernel(total, mom, out):
    write_rows(out, total[...] + 0.5 * mom[...])


def recode(total, mom):
    return kernel_call(recode_kernel, sds((112, D), i16), (), 0, 2)(total, mom)


def sum_low_kernel(own, r1, r2, r3, out, *total):
    refs = (own, r1, r2, r3)
    x = [decoded(ref[...], p[0:208]) for ref, p in zip(refs, bundle_powers(refs))]
    whole = (x[0] + x[1]) + (x[2] + x[3])
    for ref in total:
        ref[...] = whole
    write_bundle(out, whole)


def sum_low(own, received, more):
    outs = (sds(own.shape, i16),) + ((sds(own.shape, f32),) if more else ())
    return kernel_call(sum_low_kernel, outs, (), 0, 4)(own, *received)


def recode_bundle_kernel(total, out):
    write_bundle(out, total[...])


def recode_bundle(total):
    return kernel_call(recode_bundle_kernel, sds(total.shape, i16), (), 0, 1)(total)


def split_low(x):
    high = x.astype(bf16)
    return high, (x - high.astype(f32)).astype(bf16)


def dot_three_even(a, b):
    left = jnp.concatenate([a[0], a[0], a[1]], axis=1)
    right = jnp.concatenate([b[0], b[1], b[0]], axis=0)
    side = dot_nn(left, right[:, 0:256])
    low = dot_nn(left[256:], right[:, 256:])
    return jnp.concatenate([side, jnp.concatenate([side[256:].T, low], axis=0)], axis=1)


def split_three(x):
    high, rest = split_low(x)
    return high, rest, ((x - high.astype(f32)) - rest.astype(f32)).astype(bf16)


def dot_six_even(a, b):
    left = jnp.concatenate([a[0], a[0], a[1], a[1], a[0], a[2]], axis=1)
    right = jnp.concatenate([b[0], b[1], b[0], b[1], b[2], b[0]], axis=0)
    side = dot_nn(left, right[:, 0:256])
    low = dot_nn(left[256:], right[:, 256:])
    return jnp.concatenate([side, jnp.concatenate([side[256:].T, low], axis=0)], axis=1)


def sweeps(grams):
    row = lax.broadcasted_iota(jnp.int32, (D, D), 0)
    col = lax.broadcasted_iota(jnp.int32, (D, D), 1)
    eye = (row == col).astype(f32)
    scales, current, totals = [], [], [None] * len(grams)
    for gram in grams:
        trace = jnp.sum(jnp.sum(gram * eye, axis=1, keepdims=True), axis=0, keepdims=True)
        scales.append(1.0 / (jnp.sqrt(trace) + 1e-07))
        current.append(gram * (scales[-1] * scales[-1]))
    for sweep in range(5):
        split, dot = (split_three, dot_six_even) if sweep < 1 else (split_low, dot_three_even)
        parts = [split(a) for a in current]
        polys = [coeff_one * eye + coeff_two * a + coeff_three * dot(a2, a2) for a, a2 in zip(current, parts)]
        halves = [split(poly) for poly in polys]
        if sweep < 4:
            turned = [dot(a2, p2) for a2, p2 in zip(parts, halves)]
        totals = [
            poly if total is None else dot_three_even(split_low(total), p2)
            for total, poly, p2 in zip(totals, polys, halves)
        ]
        if sweep < 4:
            current = [dot(split(t), p2) for t, p2 in zip(turned, halves)]
    return [total * scale for total, scale in zip(totals, scales)]


def gram_of(high, low):
    both = dot_tn(high, jnp.concatenate([high, low], axis=1))
    cross = both[:, D:]
    return both[:, 0:D] + (cross + cross.T)


def gram_kernel(pos, a0, a1, a2, a3, keep, send, band_rows, s_high, s_low, e_high, e_low):
    core, chip = pos[0], pos[2]
    refs = (a0, a1, a2, a3)
    for e, (ref, power) in enumerate(zip(refs, message_powers(refs))):
        x = decoded(ref[0:D, :], power)
        high, low = split_low(x)
        for d in range(4):
            at, of = (e * 4 + d) * 48, d * 96
            s_high[at : at + 48, :], e_high[at : at + 48, :] = high[of : of + 48], high[of + 48 : of + 96]
            s_low[at : at + 48, :], e_low[at : at + 48, :] = low[of : of + 48], low[of + 48 : of + 96]
        to = pl.multiple_of(lax.bitwise_xor(chip, e) * 48, 16)
        band_rows[pl.ds(to, 48), :] = x[0:48]
        band_rows[pl.ds(pl.multiple_of(192 + to, 16), 48), :] = x[48:96]
    gram_s, gram_e = gram_of(s_high[...], s_low[...]), gram_of(e_high[...], e_low[...])
    keep[...] = jnp.where(core == 0, gram_s, gram_e)
    send[...] = jnp.where(core == 0, gram_e, gram_s)


def half_grams(pos, parts):
    outs = (sds((D, D), f32),) * 3
    scratch = [pltpu.VMEM((FF // 2, D), bf16)] * 4
    return kernel_call(gram_kernel, outs, scratch, 1, 4, extra=10)(pos, *parts)


def muon_kernel(pos, keep, recv, q0, q1, q2, q3, o0, o1, o2, o3, w0, w1, w2, w3, one_out, two_out, gram, rows, lows):
    core = pos[0]
    pieces = (q0, q1, q2, q3, o0, o1, o2, o3)
    power = bundle_powers(pieces)

    @pl.when(core == 0)
    def _():
        for e, ref in enumerate(pieces):
            x = split_low(decoded(ref[0:144, :], power[e][0:144]))
            rows[e * 144 : (e + 1) * 144, :], lows[e * 144 : (e + 1) * 144, :] = x
        gram[...] = gram_of(rows[...], lows[...])

    @pl.when(core != 0)
    def _():
        for e, ref in enumerate(pieces):
            x = split_low(decoded(ref[144:192, :], power[e][144:192]))
            rows[e * 48 : (e + 1) * 48, :], lows[e * 48 : (e + 1) * 48, :] = x
        gram[...] = gram_of(rows[0:D, :], lows[0:D, :])

    one, two = sweeps([keep[...] + recv[...], gram[...]])
    one_out[...] = one
    two_out[...] = two


def muon(pos, keep, recv, own_q, oth_q, weights):
    scratch = [pltpu.VMEM((D, D), f32), pltpu.VMEM((3 * D, D), bf16), pltpu.VMEM((3 * D, D), bf16)]
    outs = (sds((D, D), f32),) * 2
    return kernel_call(muon_kernel, outs, scratch, 1, 14, extra=12)(pos, keep, recv, *own_q, *oth_q, *weights)


def final_kernel(
    pos, one, two, one_oth, two_oth, band_mine, band_oth, q0, q1, q2, q3, o0, o1, o2, o3,
    qkv_w, proj_w, expand_w, shrink_w,
    qkv_m, qkv_new, proj_m, proj_new, expand_m, expand_new, shrink_m, shrink_new,
    q_mine, q_oth, q_rows,
):
    core, band, chip = pos[0], pos[1], pos[2]
    first = core == 0

    def choose(when_first, a, b):
        return split_low(jnp.where(first == when_first, a[...], b[...]))

    pieces = (q0, q1, q2, q3, o0, o1, o2, o3)
    power = bundle_powers(pieces)
    for e in range(4):
        quarter = lax.bitwise_xor(chip, e)
        for i, to in ((e, q_mine), (4 + e, q_oth)):
            x = decoded(pieces[i][0:192, :], power[i][0:192])
            to[pl.ds(pl.multiple_of(quarter * 144, 16), 144), :] = x[0:144]
            to[pl.ds(pl.multiple_of(3 * OWN + quarter * 48, 16), 48), :] = x[144:192]
    for j in range(4):
        whole = band * 3 + j
        at = pl.multiple_of(((whole // 4) * 2 + lax.rem(whole, 2)) * 96, 32)
        mine = lax.rem(whole, 4) // 2 == core
        if j == 3:
            at = pl.multiple_of(3 * OWN + lax.rem(band, 2) * 96, 32)
            mine = band // 2 == core

        @pl.when(mine)
        def _():
            q_rows[j * 96 : (j + 1) * 96, :] = q_mine[pl.ds(at, 96), :]

        @pl.when(jnp.logical_not(mine))
        def _():
            q_rows[j * 96 : (j + 1) * 96, :] = q_oth[pl.ds(at, 96), :]

    b_mine, b_oth = band_mine[...], band_oth[...]
    low_core, high_core = jnp.where(first, b_mine, b_oth), jnp.where(first, b_oth, b_mine)
    m_shrink = jnp.concatenate([low_core[0:192], high_core[0:192]], axis=0)
    m_expand = jnp.concatenate([low_core[192:], high_core[192:]], axis=0)
    t_shrink, t_expand = choose(True, one, one_oth), choose(False, one, one_oth)
    t_qkv, t_proj = choose(True, two, two_oth), choose(False, two, two_oth)
    for w, t, m, mom, new, size in (
        (qkv_w, t_qkv, q_rows[0:288, :], qkv_m, qkv_new, 3 * D),
        (proj_w, t_proj, q_rows[288:D, :], proj_m, proj_new, D),
        (shrink_w, t_shrink, m_shrink, shrink_m, shrink_new, FF),
    ):
        high, low = split_low(m)
        mom[...] = m
        new[...] = w[...] - 0.05 * math.sqrt(size) * (dot_nn(high, t[0]) + (dot_nn(high, t[1]) + dot_nn(low, t[0])))
    high, low = split_low(m_expand)
    expand_m[...] = m_expand.T
    ortho = dot_nt(t_expand[0], high) + (dot_nt(t_expand[1], high) + dot_nt(t_expand[0], low))
    expand_new[...] = expand_w[...] - 0.05 * math.sqrt(FF) * ortho


def final(pos, turns, far_turns, band_mine, band_oth, own_q, oth_q, *weights):
    outs = []
    for w in weights:
        outs += [sds(w.shape, f32)] * 2
    v = pltpu.VMEM
    scratch = [v((4 * OWN, D), f32), v((4 * OWN, D), f32), v((D, D), f32)]
    return kernel_call(final_kernel, tuple(outs), scratch, 1, 18, extra=10)(
        pos, *turns, *far_turns, band_mine, band_oth, *own_q, *oth_q, *weights
    )


def vector_kernel(pos, mine, other, gains, biases, freq, g_mom, g_new, b_mom, b_new, f_mom, f_new, mom, new):
    band = pos[1]
    n = mine.shape[0] - 16
    power = bundle_powers((mine, other))
    total = decoded(mine[n : n + 16, :], power[0][n : n + 16]) + decoded(other[n : n + 16, :], power[1][n : n + 16])
    mom[...] = total
    new[...] = jnp.zeros_like(new)
    freqs = jnp.concatenate([freq[0:1, :], freq[1:2, :]], axis=1)
    for at, values in ((0, gains[...]), (2, biases[...]), (13, freqs)):
        here = slice(at, at + values.shape[0])
        part = total[here, :]
        square = jnp.sum(jnp.sum(part * part, axis=1, keepdims=True), axis=0, keepdims=True)
        new[here, :] = values - 0.2 * part * lax.rsqrt(square * (1.0 / (values.shape[0] * D)) + 1e-06)
    for whole, g_out, b_out, f_out in ((mom, g_mom, b_mom, f_mom), (new, g_new, b_new, f_new)):
        g_out[...] = pltpu.roll(whole[0:8, :], lax.rem(D - 96 * band, D), 1)[0:2, 0:96]
        rows = pltpu.roll(jnp.broadcast_to(whole[13:14, :], (8, D)), lax.rem(D - 48 * band, D), 1)
        f_out[...] = jnp.concatenate([rows[0:1, 0:48], rows[0:1, 192:240]], axis=0)
        blocks = []
        for i in range(11):
            block = 11 * band + i
            row = jnp.broadcast_to(whole[pl.ds(2 + block // 4, 1), :], (8, D))
            blocks.append(pltpu.roll(row, lax.rem(D - 96 * lax.rem(block, 4), D), 1)[0:1, 0:96])
        b_out[...] = jnp.concatenate(blocks, axis=1).reshape(b_out.shape)


def vector_step(pos, mine, other, gains, biases, freq):
    outs = (sds((2, 96), f32),) * 2 + (sds((11 * 96,), f32),) * 2 + (sds((2, 48), f32),) * 2
    scratch = [pltpu.VMEM((16, D), f32)] * 2
    return kernel_call(vector_kernel, outs, scratch, 1, 5, cost=10**10)(pos, mine, other, gains, biases, freq)


def flip(x, bit):
    n = lax.axis_size("batch")
    return lax.ppermute(x, "batch", [(i, i ^ bit) for i in range(n)])


def swap_bands(x, d):
    return lax.ppermute(x, "rows", [(i, i ^ d) for i in range(4)])


def moves(which):
    pairs = []
    for k in range(lax.axis_size("batch") // 2):
        for c in range(2):
            for i in range(4):
                band = (i - 2 * c - which) % 4
                pairs.append(((2 * k + i // 2) * 4 + band, (2 * k + c) * 4 + i))
    return pairs


def to_image(parts):
    return [lax.ppermute(parts[which], AXES, moves(which)) for which in range(2)]


def from_image(part, which):
    return lax.ppermute(part, AXES, [(b, a) for a, b in moves(which)])


def other_chips(x):
    bit = 8
    while bit < lax.axis_size("batch"):
        x = x + flip(x.astype(f32), bit).astype(x.dtype)
        bit *= 2
    return x


def over_chips(x):
    return [flip(x, 2 * e) for e in range(1, 4)]


def over_bands(x):
    return [swap_bands(x, d) for d in range(1, 4)]


def local(
    patches,
    cotangent,
    heights,
    widths,
    qkv_weight,
    qkv_moment,
    proj_weight,
    proj_moment,
    expand_weight,
    expand_moment,
    shrink_weight,
    shrink_moment,
    norm_gains,
    gains_moment,
    all_biases,
    biases_moment,
    frequencies,
    freq_moment,
):
    images, band_rows, grid_w, _ = patches.shape
    slab = band_rows * grid_w
    batch = lax.axis_index("batch")
    band = lax.axis_index("rows")
    core = batch % 2
    chip = (batch // 2) % 4
    pos = jnp.stack([core, band, chip, batch // 2]).astype(jnp.int32)
    grid = (band_rows, grid_w)
    more_chips = lax.axis_size("batch") > 8

    share = own_weights(pos, qkv_weight.T, proj_weight.T, expand_weight, shrink_weight)
    shares = over_bands(share)
    p_a, p_b, c_a, c_b = slabs(
        pos, heights, widths, patches.reshape(images, slab, D), cotangent.reshape(images, slab, D)
    )
    own = to_image((p_a, p_b))
    oth = [flip(x, 1) for x in own]
    biases = all_biases.reshape(-1, D)
    cos, sin, rows_tok, cols_tok, bias_own, mom_big, vec_mom = setup(
        pos, frequencies, biases, expand_moment, shrink_moment,
        gains_moment, biases_moment.reshape(11, 96), freq_moment, 4 * slab, *grid,
    )
    shares, cos, vec_mom = lax.optimization_barrier((shares, cos, vec_mom))
    w_qkv, w_first, w_second = pack(share, shares)
    w_qkv = [w_qkv] + over_chips(w_qkv)
    w_first, oth = lax.optimization_barrier((w_first, oth))
    w_first = [w_first] + over_chips(w_first)
    c_a, c_b, w_second, w_qkv = lax.optimization_barrier((c_a, c_b, w_second, w_qkv))
    cot = to_image((c_a, c_b))
    w_second = [w_second] + over_chips(w_second)

    normed, w_own, qrot, krot, q_aug, k_aug, k_nat, v_nat, logs, *o_mine = front(
        pos, own + oth, w_qkv, bias_own, norm_gains, biases, cos, sin, rows_tok, cols_tok
    )
    o_oth = [flip(x, 1) for x in o_mine]
    cot, _ = lax.optimization_barrier((cot, o_mine))
    cot = cot + [flip(x, 1) for x in cot]
    resid, att, proj16, e_all, n2, hidden, slope = expand_layer(
        pos, own + oth, (*o_mine, *o_oth), w_first, norm_gains, biases, 2 * slab
    )
    g16, s_all, dpre, dn_two, dn_two_send = slope_layer(pos, own[0], cot, w_second, e_all, slope, *grid)
    base, acc_send, big, b1, b2, b3, vec = shrink_layer(pos, hidden, dpre, g16, n2, s_all, resid, biases)
    dn_two_recv, acc_recv = flip(dn_two_send, 1), flip(acc_send, 1)
    dn_two_recv, _ = lax.optimization_barrier((dn_two_recv, acc_recv))
    big_chips = [flip(x, 2 * e) for e, x in zip((1, 2, 3), (b1, b2, b3))]
    d_residual, d_mine, d_send, p_keep, p_send, vec = branch(
        pos, own[0], cot[:2], resid, att, proj16, dn_two, dn_two_recv, norm_gains, vec, *grid
    )
    d_recv = flip(d_send, 1)
    p_recv = flip(p_send, 1)
    dq_a, dk, dv = scores_back(0, q_aug, k_aug, k_nat, v_nat, logs, d_mine)
    dq_b, dk, dv = scores_back(1, q_aug, k_aug, k_nat, v_nat, logs, d_recv, (dk, dv))

    big, dq_b = lax.optimization_barrier((big, dq_b))
    own_big, *to_bands = bands(pos, big, big_chips)
    to_bands, dq_b, acc_recv = lax.optimization_barrier((to_bands, dq_b, acc_recv))
    from_bands = [swap_bands(x, d) for d, x in zip((1, 2, 3), to_bands)]
    q_mine, *q_sends, dn_own, dn_oth = back(
        pos, normed, w_own, qrot, krot, (dq_a, dq_b, dk, dv), cos, sin, rows_tok, cols_tok, own + oth,
        (qkv_moment.T, proj_moment.T), (p_keep, p_recv), (vec, vec_mom),
    )
    dn_recv = flip(dn_oth, 1)
    from_bands, _ = lax.optimization_barrier((from_bands, q_mine))
    big_piece, *piece_total = piece_sum(own_big, from_bands, mom_big, more_chips)
    if more_chips:
        big_piece = recode(other_chips(piece_total[0]), mom_big)
    q_sends, big_piece = lax.optimization_barrier((q_sends, big_piece))

    q_low, *q_total = sum_low(q_mine, [flip(x, 2 * e) for e, x in zip((1, 2, 3), q_sends)], more_chips)
    if more_chips:
        q_low = recode_bundle(other_chips(q_total[0]))
    big_pair = join(big_piece, swap_bands(big_piece, 1))
    big_bands = join(big_pair, swap_bands(big_pair, 2))
    big_bands, q_low = lax.optimization_barrier((big_bands, q_low))
    big_all = [big_bands] + over_chips(big_bands)
    q_recv = over_bands(q_low)
    results = tail(pos, own, d_residual, dn_own, dn_recv, base, acc_recv, norm_gains, *grid)
    q_recv, results = lax.optimization_barrier((q_recv, results))
    (q_piece,) = sum_low(q_low, q_recv, False)
    big_all, q_piece = lax.optimization_barrier((big_all, q_piece))
    own_q = [q_piece] + over_chips(q_piece)
    oth_q = [flip(x, 1) for x in own_q]

    gram_keep, gram_send, band_mine = half_grams(pos, big_all)
    image_a, image_b = from_image(results[0], 0), from_image(results[1], 1)
    weights = (qkv_weight.T, proj_weight.T, expand_weight, shrink_weight)
    turns = muon(pos, gram_keep, flip(gram_send, 1), own_q, oth_q, weights)
    images_back = [from_image(part, which) for which, part in enumerate(results)]
    images_back, _ = lax.optimization_barrier((images_back, turns))
    block_out, patch_grad = place(pos, images_back)
    vec_q, block_out = lax.optimization_barrier((own_q[0], block_out))
    vector_steps = vector_step(pos, vec_q, oth_q[0], norm_gains, biases, frequencies)
    shape = (images, band_rows, grid_w, D)
    block_out, patch_grad = block_out.reshape(shape), patch_grad.reshape(shape)
    far_turns, band_oth = [flip(x, 1) for x in turns], flip(band_mine, 1)
    far_turns, block_out, vector_steps = lax.optimization_barrier((far_turns, block_out, vector_steps))
    new = final(pos, turns, far_turns, band_mine, band_oth, own_q, oth_q, *weights)
    new = [x.T for x in new[:4]] + list(new[4:])

    return (block_out, patch_grad) + tuple(new) + tuple(vector_steps)


def solution(mesh):
    image = P("batch", "rows", None, None)
    cols, rows = P(None, "rows"), P("rows", None)
    return jax.shard_map(
        local,
        mesh=mesh,
        in_specs=(
            image, image, P("batch"), P("batch"), cols, cols, cols, cols, cols, cols, rows, rows,
            P(), cols, P(), P("rows"), P(), cols,
        ),
        out_specs=(
            image, image, cols, cols, cols, cols, cols, cols, rows, rows, cols, cols, P("rows"), P("rows"), cols, cols,
        ),
        check_vma=False,
    )
```
